32 devices in a mesh: bl: 8 (over z, x), ta: 4 (over y, core).
Axes of the slice: x: 2, y: 2, z: 4, core: 2. Of those that a mesh axis runs over, the one named last changes fastest.
Arguments:
- log_amplitude: bfloat16 [2048, 4, 1536], P('bl', 'ta'), may hold values from -2.5 to 2.5
- phase: bfloat16 [2048, 4, 1536], P('bl', 'ta'), may hold values from -4 to 4
- redundant_group_index: int32 [2048], P('bl'), may hold values from 0 to 223, as said below
- antenna_couples: int32 [2048, 2], P('bl'), may hold values from 0 to 349, as said below
- tile_flag_mask: int32 [2048, 12], P(('bl', 'ta')), may hold values from 0 to 1, as said below
- inverse: float32 [2, 350, 350], replicated, may hold values from -1 to 1
- integration_kernel: float32 [4, 4], replicated, may hold values from 0.01 to 1
- channel_kernel: bfloat16 [7, 128, 128], replicated, may hold values from 0.0009994507 to 1
Outputs:
- antenna_gains: float32 [2, 350, 4, 1536], P(None, None, 'ta')
- filled: float32 [2, 2048, 4, 1536], P(None, ('bl', 'ta'))
The draws below stay inside these ranges and needn't reach their ends.
Inputs may be any that keep to these rules, and one draw needn't show every extreme that they name: `redundant_group_index`: every group from 0 to 223 holds at least one baseline. `antenna_couples`: the two antennas of a baseline differ. `tile_flag_mask`: both neighbouring tiles of a flagged tile are unflagged.
All inputs are finite; a program needn't handle non-finite values.
Results may differ from the reference program's by a relative error of at most 0.0029.
Values may be sent and summed in bfloat16 or wider, within the bound.
No kernel may reach another device: no remote copies, remote signals or barrier semaphores. Data moves between devices by JAX's collectives and lax.ppermute only.
A program may use at most 64 MiB of HBM per device.

```python
import math
import jax
import jax.numpy as jnp
from jax import lax

ANTENNA_COUNT = 350
F = 1536
TILE = 128
REACH = 3
NGRP = 224
BL_DEV = 256
BASELINE_TOTAL = 2048
TIMES = 4
NTILE = 12
N_TA = 4


def draw_redundant_group_index(key, part):
    order_key = jax.random.fold_in(key, 101)
    left_key = jax.random.fold_in(key, 102)
    right_key = jax.random.fold_in(key, 103)
    order = jax.random.permutation(order_key, BASELINE_TOTAL).astype(jnp.int32)
    left_part = jax.random.randint(left_key, (BASELINE_TOTAL,), 0, NGRP, dtype=jnp.int32)
    right_part = jax.random.randint(right_key, (BASELINE_TOTAL,), 0, NGRP, dtype=jnp.int32)
    skewed = left_part * right_part // NGRP
    return jnp.where(order < NGRP, order, skewed).astype(jnp.int32)


def draw_antenna_couples(key, part):
    first_random_key = jax.random.fold_in(key, 201)
    step_key = jax.random.fold_in(key, 202)
    first_antenna = jax.random.randint(first_random_key, (BASELINE_TOTAL,), 0, ANTENNA_COUNT, dtype=jnp.int32)
    step_spacing = jax.random.randint(step_key, (BASELINE_TOTAL,), 1, ANTENNA_COUNT, dtype=jnp.int32)
    second_antenna = (first_antenna + step_spacing) % ANTENNA_COUNT
    return jnp.stack([first_antenna, second_antenna], axis=1).astype(jnp.int32)


def draw_tile_flag_mask(key, part):
    rate_key = jax.random.fold_in(key, 301)
    raw_key = jax.random.fold_in(key, 302)
    rates = jax.random.randint(rate_key, (BASELINE_TOTAL, 1), 0, 4, dtype=jnp.int32)
    rolls = jax.random.randint(raw_key, (BASELINE_TOTAL, NTILE), 0, 8, dtype=jnp.int32)
    marked = (rolls < rates).astype(jnp.int32)
    before = jnp.pad(marked[:, :-1], ((0, 0), (1, 0)))
    return (marked * (1 - before)).astype(jnp.int32)


def draw_inverse(key, part):
    off_key = jax.random.fold_in(key, 401)
    diag_key = jax.random.fold_in(key, 402)
    identity = jnp.eye(ANTENNA_COUNT, dtype=jnp.float32)
    off_diag = jnp.clip(jax.random.normal(off_key, (2, ANTENNA_COUNT, ANTENNA_COUNT), jnp.float32), -4.0, 4.0) * (0.06 / math.sqrt(ANTENNA_COUNT))
    diagonal = jax.random.uniform(diag_key, (2, ANTENNA_COUNT), jnp.float32, 0.05, 0.15)
    return off_diag * (1.0 - identity) + diagonal[:, :, None] * identity


def level_of(stream_key, shape, cuts, least, high):
    level = 1.0
    for axis_at, parts in cuts:
        heights = jax.random.uniform(jax.random.fold_in(jax.random.fold_in(stream_key, 6), axis_at), (parts,), jnp.float32, least / len(cuts), high / len(cuts))
        level = level * jnp.repeat(jnp.exp(heights), shape[axis_at] // parts).reshape((-1,) + (1,) * (len(shape) - 1 - axis_at))
    return level


def scatter_about(rng, shape, spread, most, split=(), kind=jnp.bfloat16):
    drawn = spread * jax.random.normal(rng, shape, jnp.float32)
    if split:
        drawn = drawn * level_of(rng, shape, split, -0.22, 0.18)
    return jnp.clip(drawn, -most, most).astype(kind)


def setup_inputs(seed: int = 0) -> dict:
    keys = jax.random.split(jax.random.key(seed), 9)
    return {
        "log_amplitude": scatter_about(keys[0], (BASELINE_TOTAL, TIMES, F), 0.35, 2.5, ((0, 8), (1, 4))),
        "phase": scatter_about(keys[1], (BASELINE_TOTAL, TIMES, F), 1.0, 4.0, ((0, 8), (1, 4))),
        "redundant_group_index": draw_redundant_group_index(jax.random.fold_in(keys[8], 71), 0),
        "antenna_couples": draw_antenna_couples(jax.random.fold_in(keys[8], 71), 0),
        "tile_flag_mask": draw_tile_flag_mask(jax.random.fold_in(keys[8], 71), 0),
        "inverse": draw_inverse(jax.random.fold_in(keys[8], 71), 0),
        "integration_kernel": jnp.clip(jnp.exp(jax.random.uniform(keys[6], (TIMES, TIMES), jnp.float32, math.log(0.01), math.log(1.0))), 0.01, 1.0),
        "channel_kernel": jnp.clip(jnp.exp(jax.random.uniform(keys[7], (2 * REACH + 1, TILE, TILE), jnp.float32, math.log(0.0009994507), math.log(1.0))), 0.0009994507, 1.0).astype(jnp.bfloat16),
    }


def mix_channels(values, channel_kernel):
    span_tiles = (channel_kernel.shape[0] - 1) // 2
    tile_width = channel_kernel.shape[1]
    leading = values.shape[:-1]
    tile_count = values.shape[-1] // tile_width
    tiled = values.reshape(leading + (tile_count, tile_width)).astype(jnp.float32)
    pad_spec = [(0, 0)] * len(leading) + [(span_tiles, span_tiles), (0, 0)]
    padded = jnp.pad(tiled, pad_spec)
    summed = jnp.zeros(leading + (tile_count, tile_width), jnp.float32)
    for offset in range(2 * span_tiles + 1):
        window = lax.slice_in_dim(padded, offset, offset + tile_count, axis=len(leading))
        summed = summed + jnp.einsum("...kj,ij->...ki", window, channel_kernel[offset].astype(jnp.float32),
                                     precision=lax.Precision.HIGHEST)
    return summed.reshape(leading + (tile_count * tile_width,))


def fill_block(calibrated, tile_flag_mask, integration_kernel, channel_kernel):
    tile_width = channel_kernel.shape[1]
    weight = jnp.repeat((1 - tile_flag_mask).astype(jnp.bfloat16), tile_width, axis=1)
    masked = calibrated * weight[None, :, None, :]
    mixed = mix_channels(masked, channel_kernel)
    numerator = jnp.einsum("tu,kbuf->kbtf", integration_kernel, mixed, precision=lax.Precision.HIGHEST)
    weight_mix = mix_channels(weight, channel_kernel)
    denominator = jnp.sum(integration_kernel, axis=1)[None, :, None] * weight_mix[:, None, :]
    keep = weight.astype(jnp.float32)[None, :, None, :]
    return keep * calibrated.astype(jnp.float32) + (1.0 - keep) * numerator / denominator[None]


def reference(log_amplitude, phase, redundant_group_index, antenna_couples, tile_flag_mask, inverse, integration_kernel, channel_kernel):
    first_antenna = antenna_couples[:, 0]
    second_antenna = antenna_couples[:, 1]
    group_counts = jax.ops.segment_sum(jnp.ones((BASELINE_TOTAL,), jnp.float32), redundant_group_index, num_segments=NGRP)
    sign_reversal = jnp.array([1.0, -1.0], dtype=jnp.float32)

    def per_time(rows):
        amp_rows, phase_rows = rows
        stacked_terms = jnp.stack([amp_rows, phase_rows], axis=1).astype(jnp.float32)
        group_mean = jax.ops.segment_sum(stacked_terms, redundant_group_index, num_segments=NGRP) / group_counts[:, None, None]
        fit_residual = stacked_terms - group_mean[redundant_group_index]
        normal_right_side = jax.ops.segment_sum(fit_residual, first_antenna, num_segments=ANTENNA_COUNT)
        normal_right_side = normal_right_side + sign_reversal[None, :, None] * jax.ops.segment_sum(fit_residual, second_antenna, num_segments=ANTENNA_COUNT)
        gain_terms = jnp.einsum("sab,bsf->saf", inverse, normal_right_side, precision=lax.Precision.HIGHEST)
        amplitude_gain = gain_terms[0]
        phase_gain_term = gain_terms[1]
        calibrated_amplitude = stacked_terms[:, 0] - amplitude_gain[first_antenna] - amplitude_gain[second_antenna]
        calibrated_phase = stacked_terms[:, 1] - phase_gain_term[first_antenna] + phase_gain_term[second_antenna]
        magnitude = jnp.exp(calibrated_amplitude)
        calibrated = jnp.stack([magnitude * jnp.cos(calibrated_phase), magnitude * jnp.sin(calibrated_phase)]).astype(jnp.bfloat16)
        return gain_terms, calibrated

    gain_time, cal_time = lax.map(per_time, (jnp.swapaxes(log_amplitude, 0, 1), jnp.swapaxes(phase, 0, 1)))
    antenna_gains = jnp.transpose(gain_time, (1, 2, 0, 3))
    calibrated = jnp.transpose(cal_time, (1, 2, 0, 3))
    block_rows = BL_DEV // N_TA
    block_count = BASELINE_TOTAL // block_rows
    cal_blocks = jnp.transpose(calibrated.reshape(2, block_count, block_rows, TIMES, F), (1, 0, 2, 3, 4))
    flag_blocks = tile_flag_mask.reshape(block_count, block_rows, NTILE)

    def one_block(pair):
        return fill_block(pair[0], pair[1], integration_kernel, channel_kernel)

    filled_blocks = lax.map(one_block, (cal_blocks, flag_blocks))
    filled = jnp.transpose(filled_blocks, (1, 0, 2, 3, 4)).reshape(2, BASELINE_TOTAL, TIMES, F)
    return antenna_gains, filled
```

```python
import functools

import jax
import jax.numpy as jnp
from jax import lax
from jax.experimental import pallas as pl
from jax.experimental.pallas import tpu as pltpu
from jax.sharding import PartitionSpec as P

NGRP = 224
GROUP_ROWS = 256
LANES = 128
HIGHEST = lax.Precision.HIGHEST
VMEM_BYTES = 48 * 1024 * 1024


def round_up(value, unit):
    return -(-value // unit) * unit


class Chunks:
    def __init__(self, channels, devices):
        width = channels // devices
        self.channels = channels
        self.devices = devices
        self.full = width // LANES
        self.rest = width % LANES
        self.whole = self.full * LANES
        self.lanes = 2 * width

    def device_pieces(self, device, which):
        pieces = []
        if self.full:
            pieces.append((device * self.whole, which * self.whole, self.whole))
        if self.rest:
            first = self.devices * self.whole + device * self.rest
            pieces.append((first, 2 * self.whole + which * self.rest, self.rest))
        return pieces

    def tile_pieces(self, tile, which):
        start = tile * LANES
        split = self.devices * self.whole
        if start < split:
            device, inside = divmod(start, self.whole)
            return [(device, which * self.whole + inside, LANES)]
        pieces = []
        at = start - split
        end = at + LANES
        while at < end:
            device, inside = divmod(at, self.rest)
            width = min(self.rest - inside, end - at)
            pieces.append((device, 2 * self.whole + which * self.rest + inside, width))
            at += width
        return pieces


def join(pieces):
    return pieces[0] if len(pieces) == 1 else jnp.concatenate(pieces, axis=-1)


def call(body, out_shape, **kwargs):
    return pl.pallas_call(
        body,
        out_shape=out_shape,
        compiler_params=pltpu.CompilerParams(vmem_limit_bytes=VMEM_BYTES),
        **kwargs,
    )


def pack_kernel(chunks, amp_ref, phase_ref, out_ref):
    for device in range(chunks.devices):
        for which, ref in enumerate((amp_ref, phase_ref)):
            for channel, lane, width in chunks.device_pieces(device, which):
                out_ref[device, :, lane : lane + width] = ref[:, channel : channel + width]


def index_kernel(antennas, index_ref, inverse_ref, down_ref, up_ref, mix_ref, counts, shared):
    step = pl.program_id(0)
    rows = index_ref.shape[1]

    @pl.when(step == 0)
    def _():
        counts[...] = jnp.zeros_like(counts)
        shared[...] = jnp.zeros_like(shared)

    group = index_ref[0:1, :]
    first = index_ref[1:2, :]
    second = index_ref[2:3, :]
    group_labels = lax.broadcasted_iota(jnp.int32, (GROUP_ROWS, rows), 0)
    group_hot = (group_labels == group).astype(jnp.float32).astype(jnp.bfloat16)
    labels = lax.broadcasted_iota(jnp.int32, (antennas, rows), 0)
    first_hot = (labels == first).astype(jnp.float32)
    second_hot = (labels == second).astype(jnp.float32)
    counts[...] += lax.dot_general(
        jnp.ones((8, rows), jnp.bfloat16),
        group_hot,
        (((1,), (1,)), ((), ())),
        preferred_element_type=jnp.float32,
    )
    columns = jnp.transpose(jnp.concatenate([first, second] * 4, axis=0))
    side_labels = lax.broadcasted_iota(jnp.int32, (rows, antennas), 1)
    first_side = (side_labels == columns[:, 0:1]).astype(jnp.float32)
    second_side = (side_labels == columns[:, 1:2]).astype(jnp.float32)
    for s, sign in enumerate((1.0, -1.0)):
        couple = (first_hot + sign * second_hot).astype(jnp.bfloat16)
        down_ref[s, 0:GROUP_ROWS, :] = group_hot
        down_ref[s, GROUP_ROWS:, :] = couple
        up_ref[s] = (first_side + sign * second_side).astype(jnp.bfloat16)
        shared[s] += lax.dot_general(
            couple, group_hot, (((1,), (1,)), ((), ())), preferred_element_type=jnp.float32
        )

    @pl.when(step == pl.num_programs(0) - 1)
    def _():
        share = 1.0 / jnp.maximum(counts[0:1, :], 1.0)
        for s in range(2):
            inverse = inverse_ref[s]
            mix_ref[s, :, 0:GROUP_ROWS] = -jnp.dot(
                inverse, shared[s] * share, precision=HIGHEST, preferred_element_type=jnp.float32
            )
            mix_ref[s, :, GROUP_ROWS:] = inverse


def solve_kernel(chunks, x_ref, down_ref, mix_ref, split_ref, sent_ref, sums):
    step = pl.program_id(0)
    whole = chunks.whole
    x = x_ref[...]
    rest = x[:, 2 * whole :]

    @pl.when(step == 0)
    def _():
        sums[...] = jnp.zeros_like(sums)

    for s in range(2):
        terms = rest
        if whole:
            terms = jnp.concatenate([x[:, s * whole : (s + 1) * whole], rest], axis=1)
        part = jnp.dot(down_ref[s], terms, preferred_element_type=jnp.float32)

        sums[s] += part

    @pl.when(step == pl.num_programs(0) - 1)
    def _():
        tails = []
        for s in range(2):
            gain = jnp.dot(
                mix_ref[s], sums[s], precision=HIGHEST, preferred_element_type=jnp.float32
            )
            left = gain
            for k in range(3):
                part = left.astype(jnp.bfloat16)
                split_ref[s, k] = part
                left = left - part.astype(jnp.float32)
            if whole:
                sent_ref[:, s * whole : (s + 1) * whole] = gain[:, :whole].astype(jnp.bfloat16)
            tails.append(gain[:, whole:])
        lane = lax.broadcasted_iota(jnp.int32, tails[0].shape, 1)
        sent_ref[:, 2 * whole :] = jnp.where(lane < chunks.rest, tails[0], tails[1]).astype(
            jnp.bfloat16
        )


def reduced(angle):
    turns = jnp.floor(angle * 0.6366197723675814 + 0.5)
    left = angle - turns * 1.5703125
    left = left - turns * 4.83751296997070312e-4
    left = left - turns * 7.54978995489188216e-8
    square = left * left
    sine = ((-1.9515295891e-4 * square + 8.3321608736e-3) * square - 1.6666654611e-1) * square
    sine = sine * left + left
    cosine = (2.443315711809948e-5 * square - 1.388731625493765e-3) * square
    cosine = (cosine + 4.166664568298827e-2) * square * square - 0.5 * square + 1.0
    return turns.astype(jnp.int32), sine, cosine


def quarter(turns, sine, cosine):
    value = jnp.where((turns & 1) == 1, cosine, sine)
    return jnp.where((turns & 2) == 2, -value, value)


def swap(values, half):
    if 2 * half == LANES:
        return pltpu.roll(values, half, 1)
    return jnp.concatenate([values[:, half:], values[:, :half]], axis=1)


def calibrate_kernel(chunks, x_ref, up_ref, split_ref, out_ref):
    whole = chunks.whole
    x = x_ref[...].astype(jnp.float32)
    moves = []
    for s in range(2):
        move = None
        for k in range(3):
            part = jnp.dot(up_ref[s], split_ref[s, k], preferred_element_type=jnp.float32)
            move = part if move is None else move + part
        moves.append(move)
    if whole:
        magnitude = jnp.exp(x[:, :whole] - moves[0][:, :whole])
        turns, sine, cosine = reduced(x[:, whole : 2 * whole] - moves[1][:, :whole])
        out_ref[:, :whole] = (magnitude * quarter(turns + 1, sine, cosine)).astype(jnp.bfloat16)
        out_ref[:, whole : 2 * whole] = (magnitude * quarter(turns, sine, cosine)).astype(
            jnp.bfloat16
        )
    if chunks.rest:
        tail = x[:, 2 * whole :]
        lane = lax.broadcasted_iota(jnp.int32, tail.shape, 1)
        low = lane < chunks.rest
        tail = tail - jnp.where(low, moves[0][:, whole:], moves[1][:, whole:])
        turned = swap(tail, chunks.rest)
        magnitude = jnp.exp(jnp.where(low, tail, turned))
        turns, sine, cosine = reduced(jnp.where(low, turned, tail))
        turns = jnp.where(low, turns + 1, turns)
        out_ref[:, 2 * whole :] = (magnitude * quarter(turns, sine, cosine)).astype(jnp.bfloat16)


def spread_kernel(chunks, antennas, gain_ref, out_ref):
    which = pl.program_id(0)
    for s in range(2):

        @pl.when(which == s)
        def _():
            for tile in range(chunks.channels // LANES):
                values = join(
                    [
                        gain_ref[device, :, lane : lane + width].astype(jnp.float32)
                        for device, lane, width in chunks.tile_pieces(tile, s)
                    ]
                )
                out_ref[0, :, tile * LANES : (tile + 1) * LANES] = values[:antennas]


def fill_kernel(chunks, times, reach, cal_ref, mask_ref, times_ref, kernel_ref, out_ref, rows, band):
    step = pl.program_id(0)
    tiles = chunks.channels // LANES
    block = mask_ref.shape[0]
    count = 2 * times * block

    @pl.when(step == 0)
    def _():
        keep = (1 - mask_ref[...]).astype(jnp.float32)
        for side in range(reach):
            rows[side] = jnp.zeros(rows.shape[1:], rows.dtype)
            rows[reach + tiles + side] = jnp.zeros(rows.shape[1:], rows.dtype)
        rows[reach + tiles + reach] = jnp.zeros(rows.shape[1:], rows.dtype)
        for tile in range(tiles):
            weight = jnp.broadcast_to(keep[:, tile : tile + 1], (block, LANES))
            rows[reach + tile, count:, :] = weight.astype(rows.dtype)
            for c in range(2):
                for t in range(times):
                    values = join(
                        [
                            cal_ref[device, t, :, lane : lane + width].astype(jnp.float32)
                            for device, lane, width in chunks.tile_pieces(tile, c)
                        ]
                    )
                    at = (c * times + t) * block
                    rows[reach + tile, at : at + block, :] = (values * weight).astype(rows.dtype)
        zeros = jnp.zeros((LANES, LANES), band.dtype)
        for source in range(2 * reach + 2):
            for target in range(2):
                offset = source - target
                inside = 0 <= offset <= 2 * reach
                band[
                    target * LANES : (target + 1) * LANES, source * LANES : (source + 1) * LANES
                ] = kernel_ref[offset] if inside else zeros

    mixed = None
    for source in range(2 * reach + 2):
        part = lax.dot_general(
            rows[2 * step + source],
            band[:, source * LANES : (source + 1) * LANES],
            (((1,), (1,)), ((), ())),
            preferred_element_type=jnp.float32,
        )
        mixed = part if mixed is None else mixed + part
    total = mixed[count:]
    kept = [rows[2 * step + half + reach].astype(jnp.float32) for half in range(2)]
    kept = jnp.concatenate(kept, axis=1)
    keep = kept[count:]
    order = times * block
    place = lax.broadcasted_iota(jnp.int32, (order, order), 0)
    origin = lax.broadcasted_iota(jnp.int32, (order, order), 1)
    interleave = (place % times) * block + place // times == origin
    interleave = interleave.astype(jnp.float32).astype(jnp.bfloat16)
    scales = []
    for t in range(times):
        scale = times_ref[t, 0]
        for u in range(1, times):
            scale = scale + times_ref[t, u]
        scales.append(1.0 / (scale * total))
    for c in range(2):
        values = []
        for t in range(times):
            value = None
            for u in range(times):
                at = (c * times + u) * block
                part = times_ref[t, u] * mixed[at : at + block]
                value = part if value is None else value + part
            at = (c * times + t) * block
            values.append(jnp.where(keep > 0.5, kept[at : at + block], value * scales[t]))
        values = jnp.concatenate(values, axis=0)
        large = values.astype(jnp.bfloat16)
        small = (values - large.astype(jnp.float32)).astype(jnp.bfloat16)
        values = jnp.dot(interleave, large, preferred_element_type=jnp.float32) + jnp.dot(
            interleave, small, preferred_element_type=jnp.float32
        )
        out_ref[c] = values.reshape(block, times, 2 * LANES)


def on_device(
    devices,
    log_amplitude,
    phase,
    redundant_group_index,
    antenna_couples,
    tile_flag_mask,
    inverse,
    integration_kernel,
    channel_kernel,
):
    own, _, channels = log_amplitude.shape
    total = own * devices
    real_antennas = inverse.shape[1]
    antennas = round_up(real_antennas, LANES)
    times = integration_kernel.shape[0]
    block = tile_flag_mask.shape[0]
    reach = (channel_kernel.shape[0] - 1) // 2
    tiles = channels // LANES
    chunks = Chunks(channels, devices)
    lanes = chunks.lanes
    gain_lanes = chunks.whole + 2 * chunks.rest
    step_rows = 512
    steps = total // step_rows

    packed = call(
        functools.partial(pack_kernel, chunks),
        jax.ShapeDtypeStruct((devices, own, lanes), jnp.bfloat16),
        name="pack",
    )(log_amplitude.reshape(own, channels), phase.reshape(own, channels))
    terms = lax.all_to_all(
        packed.reshape(total, lanes), "bl", split_axis=0, concat_axis=0, tiled=True
    )

    indices = jnp.concatenate(
        [redundant_group_index, antenna_couples[:, 0], antenna_couples[:, 1]]
    )
    indices = lax.all_gather(indices, "bl", axis=0, tiled=True)
    indices = jnp.transpose(indices.reshape(devices, 3, own), (1, 0, 2)).reshape(3, total)
    gap = antennas - real_antennas
    inverse = jnp.pad(inverse, ((0, 0), (0, gap), (0, gap)))
    down, up, mix = call(
        functools.partial(index_kernel, antennas),
        (
            jax.ShapeDtypeStruct((2, GROUP_ROWS + antennas, total), jnp.bfloat16),
            jax.ShapeDtypeStruct((2, total, antennas), jnp.bfloat16),
            jax.ShapeDtypeStruct((2, antennas, GROUP_ROWS + antennas), jnp.float32),
        ),
        grid=(steps,),
        in_specs=[
            pl.BlockSpec((3, step_rows), lambda i: (0, i)),
            pl.BlockSpec((2, antennas, antennas), lambda i: (0, 0, 0)),
        ],
        out_specs=(
            pl.BlockSpec((2, GROUP_ROWS + antennas, step_rows), lambda i: (0, 0, i)),
            pl.BlockSpec((2, step_rows, antennas), lambda i: (0, i, 0)),
            pl.BlockSpec((2, antennas, GROUP_ROWS + antennas), lambda i: (0, 0, 0)),
        ),
        scratch_shapes=[
            pltpu.VMEM((8, GROUP_ROWS), jnp.float32),
            pltpu.VMEM((2, antennas, GROUP_ROWS), jnp.float32),
        ],
        name="indices",
    )(indices, inverse)

    split, sent = call(
        functools.partial(solve_kernel, chunks),
        (
            jax.ShapeDtypeStruct((2, 3, antennas, gain_lanes), jnp.bfloat16),
            jax.ShapeDtypeStruct((antennas, lanes), jnp.bfloat16),
        ),
        grid=(steps,),
        in_specs=[
            pl.BlockSpec((step_rows, lanes), lambda i: (i, 0)),
            pl.BlockSpec((2, GROUP_ROWS + antennas, step_rows), lambda i: (0, 0, i)),
            pl.BlockSpec((2, antennas, GROUP_ROWS + antennas), lambda i: (0, 0, 0)),
        ],
        out_specs=(
            pl.BlockSpec((2, 3, antennas, gain_lanes), lambda i: (0, 0, 0, 0)),
            pl.BlockSpec((antennas, lanes), lambda i: (0, 0)),
        ),
        scratch_shapes=[pltpu.VMEM((2, GROUP_ROWS + antennas, gain_lanes), jnp.float32)],
        name="solve",
    )(terms, down, mix)

    calibrated = call(
        functools.partial(calibrate_kernel, chunks),
        jax.ShapeDtypeStruct((total, lanes), jnp.bfloat16),
        grid=(steps,),
        in_specs=[
            pl.BlockSpec((step_rows, lanes), lambda i: (i, 0)),
            pl.BlockSpec((2, step_rows, antennas), lambda i: (0, i, 0)),
            pl.BlockSpec((2, 3, antennas, gain_lanes), lambda i: (0, 0, 0, 0)),
        ],
        out_specs=pl.BlockSpec((step_rows, lanes), lambda i: (i, 0)),
        name="calibrate",
    )(terms, up, split)
    spread = lax.all_to_all(calibrated, ("bl", "ta"), split_axis=0, concat_axis=0, tiled=True)
    gathered = lax.all_gather(sent, "bl", axis=0, tiled=False)

    gains = call(
        functools.partial(spread_kernel, chunks, real_antennas),
        jax.ShapeDtypeStruct((2, real_antennas, channels), jnp.float32),
        grid=(2,),
        in_specs=[pl.BlockSpec((devices, antennas, lanes), lambda i: (0, 0, 0))],
        out_specs=pl.BlockSpec((1, real_antennas, channels), lambda i: (i, 0, 0)),
        name="gains",
    )(gathered)

    filled = call(
        functools.partial(fill_kernel, chunks, times, reach),
        jax.ShapeDtypeStruct((2, block, times, channels), jnp.float32),
        grid=(tiles // 2,),
        in_specs=[
            pl.BlockSpec((devices, times, block, lanes), lambda i: (0, 0, 0, 0)),
            pl.BlockSpec((block, tiles), lambda i: (0, 0)),
            pl.BlockSpec(memory_space=pltpu.SMEM),
            pl.BlockSpec(channel_kernel.shape, lambda i: (0, 0, 0)),
        ],
        out_specs=pl.BlockSpec((2, block, times, 2 * LANES), lambda i: (0, 0, 0, i)),
        scratch_shapes=[
            pltpu.VMEM((tiles + 2 * reach + 1, (2 * times + 1) * block, LANES), jnp.bfloat16),
            pltpu.VMEM((2 * LANES, (2 * reach + 2) * LANES), jnp.bfloat16),
        ],
        name="fill",
    )(
        spread.reshape(devices, times, block, lanes),
        tile_flag_mask,
        integration_kernel,
        channel_kernel,
    )
    return gains.reshape(2, real_antennas, 1, channels), filled


def solution(mesh):
    in_specs = (
        P("bl", "ta", None),
        P("bl", "ta", None),
        P("bl"),
        P("bl", None),
        P(("bl", "ta"), None),
        P(),
        P(),
        P(),
    )
    out_specs = (P(None, None, "ta", None), P(None, ("bl", "ta"), None, None))
    return jax.shard_map(
        functools.partial(on_device, mesh.shape["bl"]),
        mesh=mesh,
        in_specs=in_specs,
        out_specs=out_specs,
        check_vma=False,
    )
```

```python
import functools

import jax
import jax.numpy as jnp
from jax import lax
from jax.experimental import pallas as pl
from jax.experimental.pallas import tpu as pltpu
from jax.sharding import PartitionSpec as P

NGRP = 224
GROUP_ROWS = 256
LANES = 128
HIGHEST = lax.Precision.HIGHEST


def round_up(value, unit):
    return -(-value // unit) * unit


class Part:
    def __init__(self, first, half):
        self.first = first
        self.half = half
        self.lanes = 2 * half


def parts_of(channels, devices):
    width = channels // devices
    whole = width // LANES * LANES
    parts = []
    if whole:
        parts.append(Part(0, whole))
    if width - whole:
        parts.append(Part(devices * whole, width - whole))
    return parts


def tile_pieces(parts, tile, which):
    at = tile * LANES
    index = max(k for k, part in enumerate(parts) if part.first <= at)
    part = parts[index]
    at -= part.first
    end = at + LANES
    pieces = []
    while at < end:
        device, inside = divmod(at, part.half)
        width = min(part.half - inside, end - at)
        pieces.append((index, device, which * part.half + inside, width))
        at += width
    return pieces


def join(pieces):
    return pieces[0] if len(pieces) == 1 else jnp.concatenate(pieces, axis=-1)


def call(body, out_shape, vmem, **kwargs):
    return pl.pallas_call(
        body,
        out_shape=out_shape,
        compiler_params=pltpu.CompilerParams(vmem_limit_bytes=vmem * 1024 * 1024),
        **kwargs,
    )


def pack_kernel(parts, devices, amp_ref, phase_ref, *out_refs):
    for part, out_ref in zip(parts, out_refs):
        half = part.half
        for device in range(devices):
            at = part.first + device * half
            for which, ref in enumerate((amp_ref, phase_ref)):
                out_ref[device, :, which * half : (which + 1) * half] = ref[:, at : at + half]


def index_kernel(antennas, index_ref, inverse_ref, down_ref, up_ref, mix_ref, counts, shared):
    step = pl.program_id(0)
    rows = index_ref.shape[1]

    @pl.when(step == 0)
    def _():
        counts[...] = jnp.zeros_like(counts)
        shared[...] = jnp.zeros_like(shared)

    group = index_ref[0:1, :]
    first = index_ref[1:2, :]
    second = index_ref[2:3, :]
    group_labels = lax.broadcasted_iota(jnp.int32, (GROUP_ROWS, rows), 0)
    group_hot = (group_labels == group).astype(jnp.float32).astype(jnp.bfloat16)
    labels = lax.broadcasted_iota(jnp.int32, (antennas, rows), 0)
    counts[...] += lax.dot_general(
        jnp.ones((8, rows), jnp.bfloat16),
        group_hot,
        (((1,), (1,)), ((), ())),
        preferred_element_type=jnp.float32,
    )
    down_ref[0:GROUP_ROWS, :] = group_hot
    columns = jnp.transpose(jnp.concatenate([first, second] * 4, axis=0))
    side_labels = lax.broadcasted_iota(jnp.int32, (rows, antennas), 1)
    for k, which in enumerate((first, second)):
        hot = (labels == which).astype(jnp.float32).astype(jnp.bfloat16)
        at = GROUP_ROWS + k * antennas
        down_ref[at : at + antennas, :] = hot
        up_ref[:, k * antennas : (k + 1) * antennas] = (
            (side_labels == columns[:, k : k + 1]).astype(jnp.float32).astype(jnp.bfloat16)
        )
        shared[k] += lax.dot_general(
            hot, group_hot, (((1,), (1,)), ((), ())), preferred_element_type=jnp.float32
        )

    @pl.when(step == pl.num_programs(0) - 1)
    def _():
        share = 1.0 / jnp.maximum(counts[0:1, :], 1.0)
        for s, sign in enumerate((1.0, -1.0)):
            inverse = inverse_ref[s]
            mix_ref[s, :, 0:GROUP_ROWS] = -jnp.dot(
                inverse,
                (shared[0] + sign * shared[1]) * share,
                precision=HIGHEST,
                preferred_element_type=jnp.float32,
            )
            mix_ref[s, :, GROUP_ROWS:] = inverse


def reduced(angle):
    turns = jnp.floor(angle * 0.6366197723675814 + 0.5)
    left = angle - turns * 1.5703125
    left = left - turns * 4.83751296997070312e-4
    left = left - turns * 7.54978995489188216e-8
    square = left * left
    sine = ((-1.9515295891e-4 * square + 8.3321608736e-3) * square - 1.6666654611e-1) * square
    sine = sine * left + left
    cosine = (2.443315711809948e-5 * square - 1.388731625493765e-3) * square
    cosine = (cosine + 4.166664568298827e-2) * square * square - 0.5 * square + 1.0
    return turns.astype(jnp.int32), sine, cosine


def quarter(turns, sine, cosine):
    value = jnp.where((turns & 1) == 1, cosine, sine)
    return jnp.where((turns & 2) == 2, -value, value)


def swap(values, half):
    if 2 * half == LANES:
        return pltpu.roll(values, half, 1)
    return jnp.concatenate([values[:, half:], values[:, :half]], axis=1)


def solve_kernel(half, rows, x_ref, down_ref, up_ref, mix_ref, sent_ref, out_ref, sums, split):
    total, lanes = x_ref.shape
    antennas = mix_ref.shape[1]
    sums[...] = jnp.zeros_like(sums)

    def gather(step, carry):
        at = pl.multiple_of(step * rows, rows)
        sums[...] += jnp.dot(
            down_ref[:, pl.ds(at, rows)],
            x_ref[pl.ds(at, rows), :],
            preferred_element_type=jnp.float32,
        )
        return carry

    lax.fori_loop(0, total // rows, gather, 0)
    low = lax.broadcasted_iota(jnp.int32, (antennas, lanes), 1) < half
    firsts = sums[GROUP_ROWS : GROUP_ROWS + antennas, :]
    seconds = sums[GROUP_ROWS + antennas :, :]
    terms = jnp.concatenate(
        [sums[:GROUP_ROWS, :], firsts + jnp.where(low, seconds, -seconds)], axis=0
    )
    if half % LANES == 0:
        gain = jnp.concatenate(
            [
                jnp.dot(
                    mix_ref[s],
                    terms[:, s * half : (s + 1) * half],
                    precision=HIGHEST,
                    preferred_element_type=jnp.float32,
                )
                for s in range(2)
            ],
            axis=1,
        )
    else:
        both = [
            jnp.dot(mix_ref[s], terms, precision=HIGHEST, preferred_element_type=jnp.float32)
            for s in range(2)
        ]
        gain = jnp.where(low, both[0], both[1])
    sent_ref[...] = gain.astype(jnp.bfloat16)
    left = gain
    for k in range(3):
        part = left.astype(jnp.bfloat16)
        wide = part.astype(jnp.float32)
        split[k, :antennas, :] = part
        split[k, antennas:, :] = jnp.where(low, wide, -wide).astype(jnp.bfloat16)
        left = left - wide

    def calibrate(step, carry):
        at = pl.multiple_of(step * rows, rows)
        hot = up_ref[pl.ds(at, rows), :]
        move = jnp.dot(hot, split[0], preferred_element_type=jnp.float32)
        for k in range(1, 3):
            move = move + jnp.dot(hot, split[k], preferred_element_type=jnp.float32)
        left = x_ref[pl.ds(at, rows), :].astype(jnp.float32) - move
        if half % LANES == 0:
            magnitude = jnp.exp(left[:, :half])
            turns, sine, cosine = reduced(left[:, half:])
            real = magnitude * quarter(turns + 1, sine, cosine)
            imaginary = magnitude * quarter(turns, sine, cosine)
            out_ref[pl.ds(at, rows), :half] = real.astype(jnp.bfloat16)
            out_ref[pl.ds(at, rows), half:] = imaginary.astype(jnp.bfloat16)
        else:
            lower = lax.broadcasted_iota(jnp.int32, left.shape, 1) < half
            turned = swap(left, half)
            magnitude = jnp.exp(jnp.where(lower, left, turned))
            turns, sine, cosine = reduced(jnp.where(lower, turned, left))
            turns = jnp.where(lower, turns + 1, turns)
            value = magnitude * quarter(turns, sine, cosine)
            out_ref[pl.ds(at, rows), :] = value.astype(jnp.bfloat16)
        return carry

    lax.fori_loop(0, total // rows, calibrate, 0)


def gather_far_first(values, devices):
    held = values[None]
    reach = devices // 2
    while reach:
        pairs = [(i, i ^ reach) for i in range(devices)]
        held = jnp.concatenate([held, lax.ppermute(held, "bl", pairs)], axis=0)
        reach //= 2
    return held


def entries_of(devices):
    apart = jnp.arange(devices, dtype=jnp.int32) ^ lax.axis_index("bl")
    entries = jnp.zeros_like(apart)
    reach, weight = devices // 2, 1
    while reach:
        entries = entries + weight * ((apart // reach) % 2)
        reach //= 2
        weight *= 2
    return entries


def spread_kernel(parts, antennas, tiles, entry_ref, *refs):
    gain_refs, out_ref = refs[:-1], refs[-1]
    which = pl.program_id(0)
    for s in range(2):

        @pl.when(which == s)
        def _():
            for tile in range(tiles):
                values = join(
                    [
                        gain_refs[part][entry_ref[device], :, lane : lane + width].astype(
                            jnp.float32
                        )
                        for part, device, lane, width in tile_pieces(parts, tile, s)
                    ]
                )
                out_ref[pl.ds(tile, antennas, tiles), :] = values[:antennas]


def fill_kernel(parts, times, reach, mask_ref, times_ref, kernel_ref, *refs):
    cal_refs, (out_ref, rows, band) = refs[:-3], refs[-3:]
    step = pl.program_id(0)
    block, tiles = mask_ref.shape
    count = 2 * times * block
    span = (2 * reach + 2) * LANES

    @pl.when(step == 0)
    def _():
        keep = (1 - mask_ref[...]).astype(jnp.float32)
        edge = reach * LANES
        inner = (reach + tiles) * LANES
        rows[:, :edge] = jnp.zeros((rows.shape[0], edge), rows.dtype)
        rows[:, inner:] = jnp.zeros((rows.shape[0], rows.shape[1] - inner), rows.dtype)
        for tile in range(tiles):
            lanes = slice((reach + tile) * LANES, (reach + tile + 1) * LANES)
            weight = jnp.broadcast_to(keep[:, tile : tile + 1], (block, LANES))
            weight = weight.astype(rows.dtype)
            rows[count:, lanes] = weight
            for c in range(2):
                for t in range(times):
                    values = join(
                        [
                            cal_refs[part][device, t, :, lane : lane + width]
                            for part, device, lane, width in tile_pieces(parts, tile, c)
                        ]
                    )
                    at = (c * times + t) * block
                    rows[at : at + block, lanes] = values * weight
        zeros = jnp.zeros((LANES, LANES), band.dtype)
        for source in range(2 * reach + 2):
            for target in range(2):
                offset = source - target
                inside = 0 <= offset <= 2 * reach
                band[
                    target * LANES : (target + 1) * LANES, source * LANES : (source + 1) * LANES
                ] = kernel_ref[offset] if inside else zeros

    at = pl.multiple_of(step * 2 * LANES, 2 * LANES)
    mixed = lax.dot_general(
        rows[:, pl.ds(at, span)],
        band[...],
        (((1,), (1,)), ((), ())),
        preferred_element_type=jnp.float32,
    )
    total = mixed[count:]
    kept = rows[:, pl.ds(pl.multiple_of(at + reach * LANES, LANES), 2 * LANES)]
    kept = kept.astype(jnp.float32)
    keep = kept[count:] > 0.5
    order = times * block
    place = lax.broadcasted_iota(jnp.int32, (order, order), 0)
    origin = lax.broadcasted_iota(jnp.int32, (order, order), 1)
    interleave = (place % times) * block + place // times == origin
    interleave = interleave.astype(jnp.float32).astype(jnp.bfloat16)
    scales = []
    for t in range(times):
        scale = times_ref[t, 0]
        for u in range(1, times):
            scale = scale + times_ref[t, u]
        scales.append(1.0 / (scale * total))
    for c in range(2):
        values = []
        for t in range(times):
            value = None
            for u in range(times):
                at = (c * times + u) * block
                part = times_ref[t, u] * mixed[at : at + block]
                value = part if value is None else value + part
            at = (c * times + t) * block
            values.append(jnp.where(keep, kept[at : at + block], value * scales[t]))
        values = jnp.concatenate(values, axis=0)
        large = values.astype(jnp.bfloat16)
        small = (values - large.astype(jnp.float32)).astype(jnp.bfloat16)
        values = jnp.dot(interleave, large, preferred_element_type=jnp.float32) + jnp.dot(
            interleave, small, preferred_element_type=jnp.float32
        )
        out_ref[c] = values.reshape(block, times, 2 * LANES)


def on_device(
    devices,
    log_amplitude,
    phase,
    redundant_group_index,
    antenna_couples,
    tile_flag_mask,
    inverse,
    integration_kernel,
    channel_kernel,
):
    own, _, channels = log_amplitude.shape
    total = own * devices
    real_antennas = inverse.shape[1]
    antennas = round_up(real_antennas, LANES)
    sent_antennas = round_up(real_antennas, 16)
    times = integration_kernel.shape[0]
    block = tile_flag_mask.shape[0]
    reach = (channel_kernel.shape[0] - 1) // 2
    tiles = channels // LANES
    parts = parts_of(channels, devices)
    rows = 512
    steps = total // rows
    large = total // 2048

    indices = jnp.concatenate(
        [redundant_group_index, antenna_couples[:, 0], antenna_couples[:, 1]]
    )
    indices = lax.all_to_all(
        jnp.broadcast_to(indices[None], (devices, 3 * own)),
        "bl",
        split_axis=0,
        concat_axis=0,
        tiled=True,
    )
    indices = jnp.transpose(indices.reshape(devices, 3, own), (1, 0, 2)).reshape(3, total)

    packed = call(
        functools.partial(pack_kernel, parts, devices),
        [jax.ShapeDtypeStruct((devices, own, part.lanes), jnp.bfloat16) for part in parts],
        32,
        name="pack",
    )(log_amplitude.reshape(own, channels), phase.reshape(own, channels))
    terms = [
        lax.all_to_all(
            values.reshape(total, part.lanes), "bl", split_axis=0, concat_axis=0, tiled=True
        )
        for part, values in zip(parts, packed)
    ]

    gap = antennas - real_antennas
    inverse = jnp.pad(inverse, ((0, 0), (0, gap), (0, gap)))
    down_rows = GROUP_ROWS + 2 * antennas
    down, up, mix = call(
        functools.partial(index_kernel, antennas),
        (
            jax.ShapeDtypeStruct((down_rows, total), jnp.bfloat16),
            jax.ShapeDtypeStruct((total, 2 * antennas), jnp.bfloat16),
            jax.ShapeDtypeStruct((2, antennas, GROUP_ROWS + antennas), jnp.float32),
        ),
        24,
        grid=(steps,),
        in_specs=[
            pl.BlockSpec((3, rows), lambda i: (0, i)),
            pl.BlockSpec((2, antennas, antennas), lambda i: (0, 0, 0)),
        ],
        out_specs=(
            pl.BlockSpec((down_rows, rows), lambda i: (0, i)),
            pl.BlockSpec((rows, 2 * antennas), lambda i: (i, 0)),
            pl.BlockSpec((2, antennas, GROUP_ROWS + antennas), lambda i: (0, 0, 0)),
        ),
        scratch_shapes=[
            pltpu.VMEM((8, GROUP_ROWS), jnp.float32),
            pltpu.VMEM((2, antennas, GROUP_ROWS), jnp.float32),
        ],
        name="indices",
    )(indices, inverse)

    spread = []
    gathered = []
    for part, values in zip(parts, terms):
        lanes = part.lanes
        sent, calibrated = call(
            functools.partial(solve_kernel, part.half, rows),
            (
                jax.ShapeDtypeStruct((antennas, lanes), jnp.bfloat16),
                jax.ShapeDtypeStruct((total, lanes), jnp.bfloat16),
            ),
            min(56, 24 * large),
            scratch_shapes=[
                pltpu.VMEM((down_rows, lanes), jnp.float32),
                pltpu.VMEM((3, 2 * antennas, lanes), jnp.bfloat16),
            ],
            name="solve",
        )(values, down, up, mix)
        spread.append(
            lax.all_to_all(
                calibrated, ("bl", "ta"), split_axis=0, concat_axis=0, tiled=True
            ).reshape(devices, times, block, lanes)
        )
        gathered.append(gather_far_first(sent[:sent_antennas], devices))

    gains = call(
        functools.partial(spread_kernel, parts, real_antennas, tiles),
        jax.ShapeDtypeStruct((2 * real_antennas * tiles, LANES), jnp.float32),
        32,
        grid=(2,),
        in_specs=[pl.BlockSpec(memory_space=pltpu.SMEM)]
        + [pl.BlockSpec(values.shape, lambda i: (0, 0, 0)) for values in gathered],
        out_specs=pl.BlockSpec((real_antennas * tiles, LANES), lambda i: (i, 0)),
        name="gains",
    )(entries_of(devices), *gathered)

    filled = call(
        functools.partial(fill_kernel, parts, times, reach),
        jax.ShapeDtypeStruct((2, block, times, channels), jnp.float32),
        32,
        grid=(tiles // 2,),
        in_specs=[
            pl.BlockSpec((block, tiles), lambda i: (0, 0)),
            pl.BlockSpec(memory_space=pltpu.SMEM),
            pl.BlockSpec(channel_kernel.shape, lambda i: (0, 0, 0)),
        ]
        + [pl.BlockSpec(values.shape, lambda i: (0, 0, 0, 0)) for values in spread],
        out_specs=pl.BlockSpec((2, block, times, 2 * LANES), lambda i: (0, 0, 0, i)),
        scratch_shapes=[
            pltpu.VMEM(((2 * times + 1) * block, (tiles + 2 * reach) * LANES), jnp.bfloat16),
            pltpu.VMEM((2 * LANES, (2 * reach + 2) * LANES), jnp.bfloat16),
        ],
        name="fill",
    )(tile_flag_mask, integration_kernel, channel_kernel, *spread)
    return gains.reshape(2, real_antennas, 1, channels), filled


def solution(mesh):
    in_specs = (
        P("bl", "ta", None),
        P("bl", "ta", None),
        P("bl"),
        P("bl", None),
        P(("bl", "ta"), None),
        P(),
        P(),
        P(),
    )
    out_specs = (P(None, None, "ta", None), P(None, ("bl", "ta"), None, None))
    return jax.shard_map(
        functools.partial(on_device, mesh.shape["bl"]),
        mesh=mesh,
        in_specs=in_specs,
        out_specs=out_specs,
        check_vma=False,
    )
```

```python
import functools

import jax
import jax.numpy as jnp
from jax import lax
from jax.experimental import pallas as pl
from jax.experimental.pallas import tpu as pltpu
from jax.sharding import PartitionSpec as P

NGRP = 224
GROUP_ROWS = 256
LANES = 128
HIGHEST = lax.Precision.HIGHEST


def round_up(value, unit):
    return -(-value // unit) * unit


class Part:
    def __init__(self, first, half):
        self.first = first
        self.half = half
        self.lanes = 2 * half


def parts_of(channels, devices):
    width = channels // devices
    whole = width // LANES * LANES
    parts = []
    if whole:
        parts.append(Part(0, whole))
    if width - whole:
        parts.append(Part(devices * whole, width - whole))
    return parts


def tile_pieces(parts, tile, which):
    at = tile * LANES
    index = max(k for k, part in enumerate(parts) if part.first <= at)
    part = parts[index]
    at -= part.first
    end = at + LANES
    pieces = []
    while at < end:
        device, inside = divmod(at, part.half)
        width = min(part.half - inside, end - at)
        pieces.append((index, device, which * part.half + inside, width))
        at += width
    return pieces


def join(pieces):
    return pieces[0] if len(pieces) == 1 else jnp.concatenate(pieces, axis=-1)


def call(body, out_shape, vmem, **kwargs):
    return pl.pallas_call(
        body,
        out_shape=out_shape,
        compiler_params=pltpu.CompilerParams(vmem_limit_bytes=vmem * 1024 * 1024),
        **kwargs,
    )


def digit_groups(own, lanes):
    return [(at, min(lanes, own - at)) for at in range(0, own, lanes)]


def digit_rows(own, lanes):
    return round_up(6 * len(digit_groups(own, lanes)), 16)


def pack_kernel(parts, devices, group_ref, couple_ref, amp_hbm, phase_hbm, *refs):
    count = len(parts)
    out_hbms, outs = refs[:count], refs[count : 2 * count]
    amp, phase, in_sems, out_sems = refs[2 * count :]
    own = amp.shape[0]
    blocks = in_sems.shape[1]
    rows = own // blocks
    copies = []
    for k in range(blocks):
        at = pl.ds(k * rows, rows)
        pair = [
            pltpu.make_async_copy(source.at[at], target.at[at], in_sems.at[which, k])
            for which, (source, target) in enumerate(((amp_hbm, amp), (phase_hbm, phase)))
        ]
        for copy in pair:
            copy.start()
        copies.append(pair)
    sent = []
    lanes = parts[0].lanes
    numbers = [group_ref[...], couple_ref[0:1, :], couple_ref[1:2, :]]
    digits = []
    for number in numbers:
        wide = number.astype(jnp.float32)
        high = jnp.floor(wide * (1.0 / LANES))
        digits += [high, wide - high * LANES]
    lines = []
    for first, width in digit_groups(own, lanes):
        for digit in digits:
            line = digit[:, first : first + width]
            if width < lanes:
                line = jnp.concatenate([line, jnp.zeros((1, lanes - width), line.dtype)], axis=1)
            lines.append(line)
    extra = digit_rows(own, lanes)
    lines.append(jnp.zeros((extra - len(lines), lanes), jnp.float32))
    lines = jnp.concatenate(lines, axis=0).astype(jnp.bfloat16)
    for device in range(devices):
        outs[0][device, own:, :] = lines
    copy = pltpu.make_async_copy(
        outs[0].at[:, pl.ds(own, extra)], out_hbms[0].at[:, pl.ds(own, extra)], out_sems.at[0, blocks]
    )
    copy.start()
    sent.append(copy)
    for k in range(blocks):
        for copy in copies[k]:
            copy.wait()
        at = slice(k * rows, (k + 1) * rows)
        for index, part in enumerate(parts):
            half = part.half
            for device in range(devices):
                first = part.first + device * half
                for which, ref in enumerate((amp, phase)):
                    outs[index][device, at, which * half : (which + 1) * half] = ref[
                        at, first : first + half
                    ]
            block = pl.ds(k * rows, rows)
            copy = pltpu.make_async_copy(
                outs[index].at[:, block], out_hbms[index].at[:, block], out_sems.at[index, k]
            )
            copy.start()
            sent.append(copy)
    for copy in sent:
        copy.wait()


def hot_rows(labels, number):
    rows = lax.broadcasted_iota(jnp.int32, (labels, number.shape[1]), 0).astype(jnp.float32)
    return (rows == number).astype(jnp.float32).astype(jnp.bfloat16)


def solve_kernel(half, own, antennas, leads, *refs):
    if leads:
        x_ref, inverse_ref, gain_ref, sent_ref, index_ref, link_ref, sums = refs
    else:
        x_ref, inverse_ref, index_ref, link_ref, gain_ref, sent_ref, sums = refs
    devices, _, lanes = x_ref.shape
    sums[...] = jnp.zeros_like(sums)
    if leads:
        link_ref[...] = jnp.zeros_like(link_ref)

    def gather(device, carry):
        values = x_ref[device, 0:own, :]
        if leads:
            numbers = []
            for k in range(3):
                pieces = []
                for piece, (_, width) in enumerate(digit_groups(own, lanes)):
                    at = own + 6 * piece + 2 * k
                    block = x_ref[device, own:, :].astype(jnp.float32)
                    at -= own
                    pieces.append(
                        block[at : at + 1, :width] * LANES + block[at + 1 : at + 2, :width]
                    )
                numbers.append(join(pieces))
            index_ref[device] = jnp.concatenate(
                numbers + [jnp.zeros((5, own), jnp.float32)], axis=0
            )
        else:
            numbers = [index_ref[device, k : k + 1, :] for k in range(3)]
        group_hot = hot_rows(GROUP_ROWS, numbers[0])
        hots = [hot_rows(antennas, number) for number in numbers[1:]]
        hot = jnp.concatenate([group_hot] + hots, axis=0)
        sums[...] += jnp.dot(hot, values, preferred_element_type=jnp.float32)
        if leads:
            for k in range(2):
                link_ref[k] += lax.dot_general(
                    hots[k],
                    group_hot,
                    (((1,), (1,)), ((), ())),
                    preferred_element_type=jnp.float32,
                )
        return carry

    lax.fori_loop(0, devices, gather, 0)
    if leads:
        counts = jnp.sum(link_ref[0], axis=0, keepdims=True)
        share = 1.0 / jnp.maximum(counts, 1.0)
        firsts = link_ref[0] * share
        seconds = link_ref[1] * share
        link_ref[0] = firsts + seconds
        link_ref[1] = firsts - seconds
    low = lax.broadcasted_iota(jnp.int32, (antennas, lanes), 1) < half
    seconds = sums[GROUP_ROWS + antennas :, :]
    sides = sums[GROUP_ROWS : GROUP_ROWS + antennas, :] + jnp.where(low, seconds, -seconds)
    both = []
    for s in range(2):
        use = slice(s * half, (s + 1) * half) if half % LANES == 0 else slice(0, lanes)
        rhs = sides[:, use] - jnp.dot(
            link_ref[s],
            sums[:GROUP_ROWS, use],
            precision=HIGHEST,
            preferred_element_type=jnp.float32,
        )
        both.append(
            jnp.dot(
                inverse_ref[s], rhs, precision=HIGHEST, preferred_element_type=jnp.float32
            )
        )
    if half % LANES == 0:
        gain = jnp.concatenate(both, axis=1)
    else:
        gain = jnp.where(low, both[0], both[1])
    gain_ref[...] = gain
    sent_ref[0] = gain[: sent_ref.shape[1]].astype(jnp.bfloat16)


def reduced(angle):
    turns = jnp.floor(angle * 0.6366197723675814 + 0.5)
    left = angle - turns * 1.5703125
    left = left - turns * 4.83751296997070312e-4
    left = left - turns * 7.54978995489188216e-8
    square = left * left
    sine = ((-1.9515295891e-4 * square + 8.3321608736e-3) * square - 1.6666654611e-1) * square
    sine = sine * left + left
    cosine = (2.443315711809948e-5 * square - 1.388731625493765e-3) * square
    cosine = (cosine + 4.166664568298827e-2) * square * square - 0.5 * square + 1.0
    return turns.astype(jnp.int32), sine, cosine


def quarter(turns, sine, cosine):
    value = jnp.where((turns & 1) == 1, cosine, sine)
    return jnp.where((turns & 2) == 2, -value, value)


def swap(values, half):
    if 2 * half == LANES:
        return pltpu.roll(values, half, 1)
    return jnp.concatenate([values[:, half:], values[:, :half]], axis=1)


def calibrate_kernel(half, own, antennas, x_ref, index_ref, gain_ref, out_ref, split):
    lanes = gain_ref.shape[1]

    @pl.when(pl.program_id(0) == 0)
    def _():
        low = lax.broadcasted_iota(jnp.int32, (antennas, lanes), 1) < half
        left = gain_ref[...]
        for k in range(3):
            part = left.astype(jnp.bfloat16)
            wide = part.astype(jnp.float32)
            split[k, :antennas, :] = part
            split[k, antennas:, :] = jnp.where(low, wide, -wide).astype(jnp.bfloat16)
            left = left - wide

    labels = lax.broadcasted_iota(jnp.int32, (own, antennas), 1).astype(jnp.float32)
    for device in range(x_ref.shape[0]):
        columns = jnp.transpose(index_ref[device])
        hot = jnp.concatenate(
            [
                (labels == columns[:, k : k + 1]).astype(jnp.float32).astype(jnp.bfloat16)
                for k in (1, 2)
            ],
            axis=1,
        )
        move = jnp.dot(hot, split[0], preferred_element_type=jnp.float32)
        for k in range(1, 3):
            move = move + jnp.dot(hot, split[k], preferred_element_type=jnp.float32)
        left = x_ref[device, 0:own, :].astype(jnp.float32) - move
        at = slice(device * own, (device + 1) * own)
        if half % LANES == 0:
            magnitude = jnp.exp(left[:, :half])
            turns, sine, cosine = reduced(left[:, half:])
            real = magnitude * quarter(turns + 1, sine, cosine)
            imaginary = magnitude * quarter(turns, sine, cosine)
            out_ref[at, :half] = real.astype(jnp.bfloat16)
            out_ref[at, half:] = imaginary.astype(jnp.bfloat16)
        else:
            lower = lax.broadcasted_iota(jnp.int32, left.shape, 1) < half
            turned = swap(left, half)
            magnitude = jnp.exp(jnp.where(lower, left, turned))
            turns, sine, cosine = reduced(jnp.where(lower, turned, left))
            turns = jnp.where(lower, turns + 1, turns)
            value = magnitude * quarter(turns, sine, cosine)
            out_ref[at, :] = value.astype(jnp.bfloat16)


def gather_far_first(values, devices):
    held = values
    reach = devices // 2
    while reach:
        pairs = [(i, i ^ reach) for i in range(devices)]
        held = jnp.concatenate([held, lax.ppermute(held, "bl", pairs)], axis=0)
        reach //= 2
    return held


def entries_of(devices):
    apart = jnp.arange(devices, dtype=jnp.int32) ^ lax.axis_index("bl")
    entries = jnp.zeros_like(apart)
    reach, weight = devices // 2, 1
    while reach:
        entries = entries + weight * ((apart // reach) % 2)
        reach //= 2
        weight *= 2
    return entries


def spread_kernel(parts, antennas, tiles, entry_ref, *refs):
    gain_refs, out_ref = refs[:-1], refs[-1]
    which = pl.program_id(0)
    for s in range(2):

        @pl.when(which == s)
        def _():
            for tile in range(tiles):
                values = join(
                    [
                        gain_refs[part][entry_ref[device], :, lane : lane + width].astype(
                            jnp.float32
                        )
                        for part, device, lane, width in tile_pieces(parts, tile, s)
                    ]
                )
                out_ref[pl.ds(tile, antennas, tiles), :] = values[:antennas]


def fill_kernel(parts, times, reach, mask_ref, times_ref, kernel_ref, *refs):
    cal_refs, (out_ref, rows, band, interleave) = refs[:-4], refs[-4:]
    step = pl.program_id(0)
    block, tiles = mask_ref.shape
    count = 2 * times * block
    span = (2 * reach + 2) * LANES

    @pl.when(step == 0)
    def _():
        keep = (1 - mask_ref[...]).astype(jnp.float32)
        edge = reach * LANES
        inner = (reach + tiles) * LANES
        rows[:, :edge] = jnp.zeros((rows.shape[0], edge), rows.dtype)
        rows[:, inner:] = jnp.zeros((rows.shape[0], rows.shape[1] - inner), rows.dtype)
        for tile in range(tiles):
            lanes = slice((reach + tile) * LANES, (reach + tile + 1) * LANES)
            weight = jnp.broadcast_to(keep[:, tile : tile + 1], (block, LANES))
            weight = weight.astype(rows.dtype)
            rows[count:, lanes] = weight
            for c in range(2):
                for t in range(times):
                    values = join(
                        [
                            cal_refs[part][device, t, :, lane : lane + width]
                            for part, device, lane, width in tile_pieces(parts, tile, c)
                        ]
                    )
                    at = (c * times + t) * block
                    rows[at : at + block, lanes] = values * weight
        order = times * block
        place = lax.broadcasted_iota(jnp.int32, (order, order), 0)
        origin = lax.broadcasted_iota(jnp.int32, (order, order), 1)
        moved = (place % times) * block + place // times == origin
        interleave[...] = moved.astype(jnp.float32).astype(jnp.bfloat16)
        zeros = jnp.zeros((LANES, LANES), band.dtype)
        for source in range(2 * reach + 2):
            for target in range(2):
                offset = source - target
                inside = 0 <= offset <= 2 * reach
                band[
                    target * LANES : (target + 1) * LANES, source * LANES : (source + 1) * LANES
                ] = kernel_ref[offset] if inside else zeros

    at = pl.multiple_of(step * 2 * LANES, 2 * LANES)
    mixed = lax.dot_general(
        rows[:, pl.ds(at, span)],
        band[...],
        (((1,), (1,)), ((), ())),
        preferred_element_type=jnp.float32,
    )
    total = mixed[count:]
    kept = rows[:, pl.ds(pl.multiple_of(at + reach * LANES, LANES), 2 * LANES)]
    kept = kept.astype(jnp.float32)
    keep = kept[count:] > 0.5
    scales = []
    for t in range(times):
        scale = times_ref[t, 0]
        for u in range(1, times):
            scale = scale + times_ref[t, u]
        scales.append(1.0 / (scale * total))
    for c in range(2):
        values = []
        for t in range(times):
            value = None
            for u in range(times):
                at = (c * times + u) * block
                part = times_ref[t, u] * mixed[at : at + block]
                value = part if value is None else value + part
            at = (c * times + t) * block
            values.append(jnp.where(keep, kept[at : at + block], value * scales[t]))
        values = jnp.concatenate(values, axis=0)
        large = values.astype(jnp.bfloat16)
        small = (values - large.astype(jnp.float32)).astype(jnp.bfloat16)
        values = jnp.dot(interleave[...], large, preferred_element_type=jnp.float32) + jnp.dot(
            interleave[...], small, preferred_element_type=jnp.float32
        )
        out_ref[c] = values.reshape(block, times, 2 * LANES)


def on_device(
    devices,
    log_amplitude,
    phase,
    redundant_group_index,
    antenna_couples,
    tile_flag_mask,
    inverse,
    integration_kernel,
    channel_kernel,
):
    own, _, channels = log_amplitude.shape
    total = own * devices
    real_antennas = inverse.shape[1]
    antennas = round_up(real_antennas, LANES)
    sent_antennas = round_up(real_antennas, 16)
    times = integration_kernel.shape[0]
    block = tile_flag_mask.shape[0]
    reach = (channel_kernel.shape[0] - 1) // 2
    tiles = channels // LANES
    parts = parts_of(channels, devices)
    gap = antennas - real_antennas
    wide_inverse = jnp.pad(inverse, ((0, 0), (0, gap), (0, gap)))
    extra = [digit_rows(own, part.lanes) if k == 0 else 0 for k, part in enumerate(parts)]
    shapes = [(devices, own + more, part.lanes) for part, more in zip(parts, extra)]
    blocks = 4
    packed = call(
        functools.partial(pack_kernel, parts, devices),
        [jax.ShapeDtypeStruct(shape, jnp.bfloat16) for shape in shapes],
        60,
        in_specs=[
            pl.BlockSpec(memory_space=pltpu.VMEM),
            pl.BlockSpec(memory_space=pltpu.VMEM),
            pl.BlockSpec(memory_space=pl.ANY),
            pl.BlockSpec(memory_space=pl.ANY),
        ],
        out_specs=[pl.BlockSpec(memory_space=pl.ANY)] * len(parts),
        scratch_shapes=[pltpu.VMEM(shape, jnp.bfloat16) for shape in shapes]
        + [pltpu.VMEM((own, channels), jnp.bfloat16)] * 2
        + [
            pltpu.SemaphoreType.DMA((2, blocks)),
            pltpu.SemaphoreType.DMA((len(parts), blocks + 1)),
        ],
        name="pack",
    )(
        redundant_group_index.reshape(1, own),
        jnp.transpose(antenna_couples),
        log_amplitude.reshape(own, channels),
        phase.reshape(own, channels),
    )
    terms = [
        lax.all_to_all(values, "bl", split_axis=0, concat_axis=0, tiled=True) for values in packed
    ]

    spread = []
    gathered = []
    indices = links = None
    large = total // 2048
    for k, (part, values) in enumerate(zip(parts, terms)):
        lanes = part.lanes
        shared = [
            jax.ShapeDtypeStruct((devices, 8, own), jnp.float32),
            jax.ShapeDtypeStruct((2, antennas, GROUP_ROWS), jnp.float32),
        ]
        results = call(
            functools.partial(solve_kernel, part.half, own, antennas, k == 0),
            [
                jax.ShapeDtypeStruct((antennas, lanes), jnp.float32),
                jax.ShapeDtypeStruct((1, sent_antennas, lanes), jnp.bfloat16),
            ]
            + (shared if k == 0 else []),
            min(56, 16 * large),
            scratch_shapes=[pltpu.VMEM((GROUP_ROWS + 2 * antennas, lanes), jnp.float32)],
            name="solve",
        )(values, wide_inverse, *([] if k == 0 else [indices, links]))
        gain, sent = results[:2]
        if k == 0:
            indices, links = results[2:]
        calibrated = call(
            functools.partial(calibrate_kernel, part.half, own, antennas),
            jax.ShapeDtypeStruct((total, lanes), jnp.bfloat16),
            16,
            grid=(devices // 2,),
            in_specs=[
                pl.BlockSpec((2,) + values.shape[1:], lambda i: (i, 0, 0)),
                pl.BlockSpec((2, 8, own), lambda i: (i, 0, 0)),
                pl.BlockSpec((antennas, lanes), lambda i: (0, 0)),
            ],
            out_specs=pl.BlockSpec((2 * own, lanes), lambda i: (i, 0)),
            scratch_shapes=[pltpu.VMEM((3, 2 * antennas, lanes), jnp.bfloat16)],
            name="calibrate",
        )(values, indices, gain)
        gathered.append(gather_far_first(sent, devices))
        spread.append(
            lax.all_to_all(
                calibrated, ("bl", "ta"), split_axis=0, concat_axis=0, tiled=True
            ).reshape(devices, times, block, lanes)
        )

    gains = call(
        functools.partial(spread_kernel, parts, real_antennas, tiles),
        jax.ShapeDtypeStruct((2 * real_antennas * tiles, LANES), jnp.float32),
        32,
        grid=(2,),
        in_specs=[pl.BlockSpec(memory_space=pltpu.SMEM)]
        + [pl.BlockSpec(values.shape, lambda i: (0, 0, 0)) for values in gathered],
        out_specs=pl.BlockSpec((real_antennas * tiles, LANES), lambda i: (i, 0)),
        name="gains",
    )(entries_of(devices), *gathered)

    filled = call(
        functools.partial(fill_kernel, parts, times, reach),
        jax.ShapeDtypeStruct((2, block, times, channels), jnp.float32),
        32,
        grid=(tiles // 2,),
        in_specs=[
            pl.BlockSpec((block, tiles), lambda i: (0, 0)),
            pl.BlockSpec(memory_space=pltpu.SMEM),
            pl.BlockSpec(channel_kernel.shape, lambda i: (0, 0, 0)),
        ]
        + [pl.BlockSpec(values.shape, lambda i: (0, 0, 0, 0)) for values in spread],
        out_specs=pl.BlockSpec((2, block, times, 2 * LANES), lambda i: (0, 0, 0, i)),
        scratch_shapes=[
            pltpu.VMEM(((2 * times + 1) * block, (tiles + 2 * reach) * LANES), jnp.bfloat16),
            pltpu.VMEM((2 * LANES, (2 * reach + 2) * LANES), jnp.bfloat16),
            pltpu.VMEM((times * block, times * block), jnp.bfloat16),
        ],
        name="fill",
    )(tile_flag_mask, integration_kernel, channel_kernel, *spread)
    return gains.reshape(2, real_antennas, 1, channels), filled


def solution(mesh):
    in_specs = (
        P("bl", "ta", None),
        P("bl", "ta", None),
        P("bl"),
        P("bl", None),
        P(("bl", "ta"), None),
        P(),
        P(),
        P(),
    )
    out_specs = (P(None, None, "ta", None), P(None, ("bl", "ta"), None, None))
    return jax.shard_map(
        functools.partial(on_device, mesh.shape["bl"]),
        mesh=mesh,
        in_specs=in_specs,
        out_specs=out_specs,
        check_vma=False,
    )
```

```python
import functools

import jax
import jax.numpy as jnp
from jax import lax
from jax.experimental import pallas as pl
from jax.experimental.pallas import tpu as pltpu
from jax.sharding import PartitionSpec as P

NGRP = 224
GROUP_ROWS = 256
LANES = 128
HIGHEST = lax.Precision.HIGHEST


def round_up(value, unit):
    return -(-value // unit) * unit


class Part:
    def __init__(self, first, half):
        self.first = first
        self.half = half
        self.lanes = 2 * half


def parts_of(channels, devices):
    width = channels // devices
    whole = width // LANES * LANES
    parts = []
    if width - whole:
        parts.append(Part(devices * whole, width - whole))
    if whole:
        parts.append(Part(0, whole))
    return parts


def tile_pieces(parts, tile, which):
    at = tile * LANES
    _, index = max((part.first, k) for k, part in enumerate(parts) if part.first <= at)
    part = parts[index]
    at -= part.first
    end = at + LANES
    pieces = []
    while at < end:
        device, inside = divmod(at, part.half)
        width = min(part.half - inside, end - at)
        pieces.append((index, device, which * part.half + inside, width))
        at += width
    return pieces


def join(pieces):
    return pieces[0] if len(pieces) == 1 else jnp.concatenate(pieces, axis=-1)


def call(body, out_shape, vmem, work, **kwargs):
    flops, moved = work
    return pl.pallas_call(
        body,
        out_shape=out_shape,
        cost_estimate=pl.CostEstimate(flops=flops, bytes_accessed=moved, transcendentals=0),
        compiler_params=pltpu.CompilerParams(vmem_limit_bytes=vmem * 1024 * 1024),
        **kwargs,
    )


def digit_groups(own, lanes):
    return [(at, min(lanes, own - at)) for at in range(0, own, lanes)]


def digit_rows(own, lanes):
    return round_up(6 * len(digit_groups(own, lanes)), 16)


def pack_kernel(parts, devices, group_ref, couple_ref, amp_hbm, phase_hbm, *refs):
    count = len(parts)
    out_hbms, outs = refs[:count], refs[count : 2 * count]
    amp, phase, in_sems, out_sems = refs[2 * count :]
    own = amp.shape[0]
    blocks = in_sems.shape[1]
    rows = own // blocks
    copies = []
    for k in range(blocks):
        at = pl.ds(k * rows, rows)
        pair = [
            pltpu.make_async_copy(source.at[at], target.at[at], in_sems.at[which, k])
            for which, (source, target) in enumerate(((amp_hbm, amp), (phase_hbm, phase)))
        ]
        for copy in pair:
            copy.start()
        copies.append(pair)
    sent = []
    lanes = parts[0].lanes
    numbers = [group_ref[...], couple_ref[0:1, :], couple_ref[1:2, :]]
    digits = []
    for number in numbers:
        wide = number.astype(jnp.float32)
        high = jnp.floor(wide * (1.0 / LANES))
        digits += [high, wide - high * LANES]
    lines = []
    for first, width in digit_groups(own, lanes):
        for digit in digits:
            line = digit[:, first : first + width]
            if width < lanes:
                line = jnp.concatenate([line, jnp.zeros((1, lanes - width), line.dtype)], axis=1)
            lines.append(line)
    extra = digit_rows(own, lanes)
    lines.append(jnp.zeros((extra - len(lines), lanes), jnp.float32))
    lines = jnp.concatenate(lines, axis=0).astype(jnp.bfloat16)
    for device in range(devices):
        outs[0][device, own:, :] = lines
    copy = pltpu.make_async_copy(
        outs[0].at[:, pl.ds(own, extra)], out_hbms[0].at[:, pl.ds(own, extra)], out_sems.at[0, blocks]
    )
    copy.start()
    sent.append(copy)
    for k in range(blocks):
        for copy in copies[k]:
            copy.wait()
        at = slice(k * rows, (k + 1) * rows)
        for index, part in enumerate(parts):
            half = part.half
            for device in range(devices):
                first = part.first + device * half
                for which, ref in enumerate((amp, phase)):
                    outs[index][device, at, which * half : (which + 1) * half] = ref[
                        at, first : first + half
                    ]
            block = pl.ds(k * rows, rows)
            copy = pltpu.make_async_copy(
                outs[index].at[:, block], out_hbms[index].at[:, block], out_sems.at[index, k]
            )
            copy.start()
            sent.append(copy)
    for copy in sent:
        copy.wait()


def hot_rows(labels, number):
    rows = lax.broadcasted_iota(jnp.int32, (labels, number.shape[1]), 0).astype(jnp.float32)
    return (rows == number).astype(jnp.float32).astype(jnp.bfloat16)


def solve_kernel(half, own, antennas, leads, *refs):
    if leads:
        x_ref, inverse_ref, gain_ref, sent_ref, index_ref, link_ref, sums = refs
    else:
        x_ref, inverse_ref, index_ref, link_ref, gain_ref, sent_ref, sums = refs
    devices, _, lanes = x_ref.shape
    sums[...] = jnp.zeros_like(sums)
    if leads:
        link_ref[...] = jnp.zeros_like(link_ref)

    def gather(device, carry):
        values = x_ref[device, 0:own, :]
        if leads:
            numbers = []
            for k in range(3):
                pieces = []
                for piece, (_, width) in enumerate(digit_groups(own, lanes)):
                    at = own + 6 * piece + 2 * k
                    block = x_ref[device, own:, :].astype(jnp.float32)
                    at -= own
                    pieces.append(
                        block[at : at + 1, :width] * LANES + block[at + 1 : at + 2, :width]
                    )
                numbers.append(join(pieces))
            index_ref[device] = jnp.concatenate(
                numbers + [jnp.zeros((5, own), jnp.float32)], axis=0
            )
        else:
            numbers = [index_ref[device, k : k + 1, :] for k in range(3)]
        group_hot = hot_rows(GROUP_ROWS, numbers[0])
        hots = [hot_rows(antennas, number) for number in numbers[1:]]
        hot = jnp.concatenate([group_hot] + hots, axis=0)
        sums[...] += jnp.dot(hot, values, preferred_element_type=jnp.float32)
        if leads:
            for k in range(2):
                link_ref[k] += lax.dot_general(
                    hots[k],
                    group_hot,
                    (((1,), (1,)), ((), ())),
                    preferred_element_type=jnp.float32,
                )
        return carry

    lax.fori_loop(0, devices, gather, 0)
    if leads:
        counts = jnp.sum(link_ref[0], axis=0, keepdims=True)
        share = 1.0 / jnp.maximum(counts, 1.0)
        firsts = link_ref[0] * share
        seconds = link_ref[1] * share
        link_ref[0] = firsts + seconds
        link_ref[1] = firsts - seconds
    low = lax.broadcasted_iota(jnp.int32, (antennas, lanes), 1) < half
    seconds = sums[GROUP_ROWS + antennas :, :]
    sides = sums[GROUP_ROWS : GROUP_ROWS + antennas, :] + jnp.where(low, seconds, -seconds)
    both = []
    for s in range(2):
        use = slice(s * half, (s + 1) * half) if half % LANES == 0 else slice(0, lanes)
        rhs = sides[:, use] - jnp.dot(
            link_ref[s],
            sums[:GROUP_ROWS, use],
            precision=HIGHEST,
            preferred_element_type=jnp.float32,
        )
        both.append(
            jnp.dot(
                inverse_ref[s], rhs, precision=HIGHEST, preferred_element_type=jnp.float32
            )
        )
    if half % LANES == 0:
        gain = jnp.concatenate(both, axis=1)
    else:
        gain = jnp.where(low, both[0], both[1])
    gain_ref[...] = gain
    sent_ref[0] = gain[: sent_ref.shape[1]].astype(jnp.bfloat16)


def reduced(angle):
    turns = jnp.floor(angle * 0.6366197723675814 + 0.5)
    left = angle - turns * 1.5703125
    left = left - turns * 4.83751296997070312e-4
    left = left - turns * 7.54978995489188216e-8
    square = left * left
    sine = ((-1.9515295891e-4 * square + 8.3321608736e-3) * square - 1.6666654611e-1) * square
    sine = sine * left + left
    cosine = (2.443315711809948e-5 * square - 1.388731625493765e-3) * square
    cosine = (cosine + 4.166664568298827e-2) * square * square - 0.5 * square + 1.0
    return turns.astype(jnp.int32), sine, cosine


def quarter(turns, sine, cosine):
    value = jnp.where((turns & 1) == 1, cosine, sine)
    return jnp.where((turns & 2) == 2, -value, value)


def swap(values, half):
    if 2 * half == LANES:
        return pltpu.roll(values, half, 1)
    return jnp.concatenate([values[:, half:], values[:, :half]], axis=1)


def calibrate_kernel(half, own, antennas, x_ref, index_ref, gain_ref, *refs):
    out_ref, split = refs[-2:]
    lanes = gain_ref.shape[1]

    @pl.when(pl.program_id(0) == 0)
    def _():
        low = lax.broadcasted_iota(jnp.int32, (antennas, lanes), 1) < half
        left = gain_ref[...]
        for k in range(3):
            part = left.astype(jnp.bfloat16)
            wide = part.astype(jnp.float32)
            split[k, :antennas, :] = part
            split[k, antennas:, :] = jnp.where(low, wide, -wide).astype(jnp.bfloat16)
            left = left - wide

    labels = lax.broadcasted_iota(jnp.int32, (own, antennas), 1).astype(jnp.float32)
    for device in range(x_ref.shape[0]):
        columns = jnp.transpose(index_ref[device])
        hot = jnp.concatenate(
            [
                (labels == columns[:, k : k + 1]).astype(jnp.float32).astype(jnp.bfloat16)
                for k in (1, 2)
            ],
            axis=1,
        )
        move = jnp.dot(hot, split[0], preferred_element_type=jnp.float32)
        for k in range(1, 3):
            move = move + jnp.dot(hot, split[k], preferred_element_type=jnp.float32)
        left = x_ref[device, 0:own, :].astype(jnp.float32) - move
        at = slice(device * own, (device + 1) * own)
        if half % LANES == 0:
            magnitude = jnp.exp(left[:, :half])
            turns, sine, cosine = reduced(left[:, half:])
            real = magnitude * quarter(turns + 1, sine, cosine)
            imaginary = magnitude * quarter(turns, sine, cosine)
            out_ref[at, :half] = real.astype(jnp.bfloat16)
            out_ref[at, half:] = imaginary.astype(jnp.bfloat16)
        else:
            lower = lax.broadcasted_iota(jnp.int32, left.shape, 1) < half
            turned = swap(left, half)
            magnitude = jnp.exp(jnp.where(lower, left, turned))
            turns, sine, cosine = reduced(jnp.where(lower, turned, left))
            turns = jnp.where(lower, turns + 1, turns)
            value = magnitude * quarter(turns, sine, cosine)
            out_ref[at, :] = value.astype(jnp.bfloat16)


def nothing(*refs):
    pass


def after(values, *others):
    return call(
        nothing,
        jax.ShapeDtypeStruct(values.shape, values.dtype),
        4,
        (0, 0),
        in_specs=[pl.BlockSpec(memory_space=pl.ANY)] * (1 + len(others)),
        out_specs=pl.BlockSpec(memory_space=pl.ANY),
        input_output_aliases={0: 0},
        name="after",
    )(values, *others)


def pass_on(held, devices, reach):
    return lax.ppermute(held, "bl", [(i, i ^ reach) for i in range(devices)])


def gather_far_first(values, devices):
    held, arrived = values, []
    reach = devices // 2
    while reach:
        if arrived:
            held = jnp.concatenate([held, arrived[-1]], axis=0)
        arrived.append(pass_on(held, devices, reach))
        reach //= 2
    return held, arrived


def entries_of(devices):
    apart = jnp.arange(devices, dtype=jnp.int32) ^ lax.axis_index("bl")
    entries = jnp.zeros_like(apart)
    reach, weight = devices // 2, 1
    while reach:
        entries = entries + weight * ((apart // reach) % 2)
        reach //= 2
        weight *= 2
    return entries


def spread_kernel(parts, antennas, tiles, entry_ref, *refs):
    gain_refs, out_ref = refs[: 2 * len(parts)], refs[-1]
    which = pl.program_id(0)

    def piece(part, device, lane, width):
        near, far = gain_refs[2 * part : 2 * part + 2]
        count = near.shape[0]
        entry = entry_ref[device]
        inside = lax.rem(entry, count)
        lanes = slice(lane, lane + width)
        value = jnp.where(entry < count, near[inside, :, lanes], far[inside, :, lanes])
        return value.astype(jnp.float32)

    for s in range(2):

        @pl.when(which == s)
        def _():
            for tile in range(tiles):
                values = join([piece(*where) for where in tile_pieces(parts, tile, s)])
                out_ref[pl.ds(tile, antennas, tiles), :] = values[:antennas]


def fill_kernel(parts, times, reach, mask_ref, times_ref, kernel_ref, *refs):
    cal_refs, (out_ref, mark_ref, rows, band, interleave) = refs[:-5], refs[-5:]
    step = pl.program_id(0)
    block, tiles = mask_ref.shape
    count = 2 * times * block
    span = (2 * reach + 2) * LANES

    @pl.when(step == 0)
    def _():
        mark_ref[...] = jnp.zeros_like(mark_ref)
        keep = (1 - mask_ref[...]).astype(jnp.float32)
        edge = reach * LANES
        inner = (reach + tiles) * LANES
        rows[:, :edge] = jnp.zeros((rows.shape[0], edge), rows.dtype)
        rows[:, inner:] = jnp.zeros((rows.shape[0], rows.shape[1] - inner), rows.dtype)
        for tile in range(tiles):
            lanes = slice((reach + tile) * LANES, (reach + tile + 1) * LANES)
            weight = jnp.broadcast_to(keep[:, tile : tile + 1], (block, LANES))
            weight = weight.astype(rows.dtype)
            rows[count:, lanes] = weight
            for c in range(2):
                for t in range(times):
                    values = join(
                        [
                            cal_refs[part][device, t, :, lane : lane + width]
                            for part, device, lane, width in tile_pieces(parts, tile, c)
                        ]
                    )
                    at = (c * times + t) * block
                    rows[at : at + block, lanes] = values * weight
        order = times * block
        place = lax.broadcasted_iota(jnp.int32, (order, order), 0)
        origin = lax.broadcasted_iota(jnp.int32, (order, order), 1)
        moved = (place % times) * block + place // times == origin
        interleave[...] = moved.astype(jnp.float32).astype(jnp.bfloat16)
        zeros = jnp.zeros((LANES, LANES), band.dtype)
        for source in range(2 * reach + 2):
            for target in range(2):
                offset = source - target
                inside = 0 <= offset <= 2 * reach
                band[
                    target * LANES : (target + 1) * LANES, source * LANES : (source + 1) * LANES
                ] = kernel_ref[offset] if inside else zeros

    at = pl.multiple_of(step * 2 * LANES, 2 * LANES)
    mixed = lax.dot_general(
        rows[:, pl.ds(at, span)],
        band[...],
        (((1,), (1,)), ((), ())),
        preferred_element_type=jnp.float32,
    )
    total = mixed[count:]
    kept = rows[:, pl.ds(pl.multiple_of(at + reach * LANES, LANES), 2 * LANES)]
    kept = kept.astype(jnp.float32)
    keep = kept[count:] > 0.5
    scales = []
    for t in range(times):
        scale = times_ref[t, 0]
        for u in range(1, times):
            scale = scale + times_ref[t, u]
        scales.append(1.0 / (scale * total))
    for c in range(2):
        values = []
        for t in range(times):
            value = None
            for u in range(times):
                at = (c * times + u) * block
                part = times_ref[t, u] * mixed[at : at + block]
                value = part if value is None else value + part
            at = (c * times + t) * block
            values.append(jnp.where(keep, kept[at : at + block], value * scales[t]))
        values = jnp.concatenate(values, axis=0)
        large = values.astype(jnp.bfloat16)
        small = (values - large.astype(jnp.float32)).astype(jnp.bfloat16)
        values = jnp.dot(interleave[...], large, preferred_element_type=jnp.float32) + jnp.dot(
            interleave[...], small, preferred_element_type=jnp.float32
        )
        out_ref[c] = values.reshape(block, times, 2 * LANES)


def on_device(
    devices,
    log_amplitude,
    phase,
    redundant_group_index,
    antenna_couples,
    tile_flag_mask,
    inverse,
    integration_kernel,
    channel_kernel,
):
    own, _, channels = log_amplitude.shape
    total = own * devices
    real_antennas = inverse.shape[1]
    antennas = round_up(real_antennas, LANES)
    sent_antennas = round_up(real_antennas, 16)
    times = integration_kernel.shape[0]
    block = tile_flag_mask.shape[0]
    reach = (channel_kernel.shape[0] - 1) // 2
    tiles = channels // LANES
    parts = parts_of(channels, devices)
    gap = antennas - real_antennas
    wide_inverse = jnp.pad(inverse, ((0, 0), (0, gap), (0, gap)))
    extra = [digit_rows(own, part.lanes) if k == 0 else 0 for k, part in enumerate(parts)]
    shapes = [(devices, own + more, part.lanes) for part, more in zip(parts, extra)]
    blocks = 4
    packed = call(
        functools.partial(pack_kernel, parts, devices),
        [jax.ShapeDtypeStruct(shape, jnp.bfloat16) for shape in shapes],
        60,
        (0, 8 * own * channels),
        in_specs=[
            pl.BlockSpec(memory_space=pltpu.VMEM),
            pl.BlockSpec(memory_space=pltpu.VMEM),
            pl.BlockSpec(memory_space=pl.ANY),
            pl.BlockSpec(memory_space=pl.ANY),
        ],
        out_specs=[pl.BlockSpec(memory_space=pl.ANY)] * len(parts),
        scratch_shapes=[pltpu.VMEM(shape, jnp.bfloat16) for shape in shapes]
        + [pltpu.VMEM((own, channels), jnp.bfloat16)] * 2
        + [
            pltpu.SemaphoreType.DMA((2, blocks)),
            pltpu.SemaphoreType.DMA((len(parts), blocks + 1)),
        ],
        name="pack",
    )(
        redundant_group_index.reshape(1, own),
        jnp.transpose(antenna_couples),
        log_amplitude.reshape(own, channels),
        phase.reshape(own, channels),
    )
    terms = [
        lax.all_to_all(values, "bl", split_axis=0, concat_axis=0, tiled=True) for values in packed
    ]

    spread = []
    gathered = []
    indices = links = None
    earlier = []
    large = total // 2048
    for k, (part, values) in enumerate(zip(parts, terms)):
        lanes = part.lanes
        shared = [
            jax.ShapeDtypeStruct((devices, 8, own), jnp.float32),
            jax.ShapeDtypeStruct((2, antennas, GROUP_ROWS), jnp.float32),
        ]
        results = call(
            functools.partial(solve_kernel, part.half, own, antennas, k == 0),
            [
                jax.ShapeDtypeStruct((antennas, lanes), jnp.float32),
                jax.ShapeDtypeStruct((1, sent_antennas, lanes), jnp.bfloat16),
            ]
            + (shared if k == 0 else []),
            min(56, 16 * large),
            (8 * total * (GROUP_ROWS + 2 * antennas) * lanes, 8 * total * lanes),
            scratch_shapes=[pltpu.VMEM((GROUP_ROWS + 2 * antennas, lanes), jnp.float32)],
            name="solve",
        )(values, wide_inverse, *([] if k == 0 else [indices, links]))
        gain, sent = results[:2]
        first = earlier[:1]
        if k == 0:
            indices, links = results[2:]
        calibrated = call(
            functools.partial(calibrate_kernel, part.half, own, antennas),
            jax.ShapeDtypeStruct((total, lanes), jnp.bfloat16),
            16,
            (16 * total * antennas * lanes, 8 * total * lanes),
            grid=(devices // 2,),
            in_specs=[
                pl.BlockSpec((2,) + values.shape[1:], lambda i: (i, 0, 0)),
                pl.BlockSpec((2, 8, own), lambda i: (i, 0, 0)),
                pl.BlockSpec((antennas, lanes), lambda i: (0, 0)),
            ]
            + [pl.BlockSpec(memory_space=pl.ANY)] * len(first),
            out_specs=pl.BlockSpec((2 * own, lanes), lambda i: (i, 0)),
            scratch_shapes=[pltpu.VMEM((3, 2 * antennas, lanes), jnp.bfloat16)],
            name="calibrate",
        )(values, indices, gain, *first)
        held, arrived = gather_far_first(sent, devices)
        if earlier:
            calibrated = after(calibrated, arrived[0], earlier[1])
        earlier = arrived
        gathered += [held, arrived[-1]]
        spread.append(
            lax.all_to_all(
                calibrated, ("bl", "ta"), split_axis=0, concat_axis=0, tiled=True
            ).reshape(devices, times, block, lanes)
        )

    filled, mark = call(
        functools.partial(fill_kernel, parts, times, reach),
        (
            jax.ShapeDtypeStruct((2, block, times, channels), jnp.float32),
            jax.ShapeDtypeStruct((8, LANES), jnp.float32),
        ),
        32,
        (32 * reach * block * times * channels * LANES, 16 * block * times * channels),
        grid=(tiles // 2,),
        in_specs=[
            pl.BlockSpec((block, tiles), lambda i: (0, 0)),
            pl.BlockSpec(memory_space=pltpu.SMEM),
            pl.BlockSpec(channel_kernel.shape, lambda i: (0, 0, 0)),
        ]
        + [pl.BlockSpec(values.shape, lambda i: (0, 0, 0, 0)) for values in spread],
        out_specs=(
            pl.BlockSpec((2, block, times, 2 * LANES), lambda i: (0, 0, 0, i)),
            pl.BlockSpec((8, LANES), lambda i: (0, 0)),
        ),
        scratch_shapes=[
            pltpu.VMEM(((2 * times + 1) * block, (tiles + 2 * reach) * LANES), jnp.bfloat16),
            pltpu.VMEM((2 * LANES, (2 * reach + 2) * LANES), jnp.bfloat16),
            pltpu.VMEM((times * block, times * block), jnp.bfloat16),
        ],
        name="fill",
    )(tile_flag_mask, integration_kernel, channel_kernel, *spread)
    gains = call(
        functools.partial(spread_kernel, parts, real_antennas, tiles),
        jax.ShapeDtypeStruct((2 * real_antennas * tiles, LANES), jnp.float32),
        32,
        (0, 12 * real_antennas * channels),
        grid=(2,),
        in_specs=[pl.BlockSpec(memory_space=pltpu.SMEM)]
        + [pl.BlockSpec(values.shape, lambda i: (0, 0, 0)) for values in gathered]
        + [pl.BlockSpec(memory_space=pl.ANY)],
        out_specs=pl.BlockSpec((real_antennas * tiles, LANES), lambda i: (i, 0)),
        name="gains",
    )(entries_of(devices), *gathered, mark)

    return gains.reshape(2, real_antennas, 1, channels), filled


def solution(mesh):
    in_specs = (
        P("bl", "ta", None),
        P("bl", "ta", None),
        P("bl"),
        P("bl", None),
        P(("bl", "ta"), None),
        P(),
        P(),
        P(),
    )
    out_specs = (P(None, None, "ta", None), P(None, ("bl", "ta"), None, None))
    return jax.shard_map(
        functools.partial(on_device, mesh.shape["bl"]),
        mesh=mesh,
        in_specs=in_specs,
        out_specs=out_specs,
        check_vma=False,
    )
```

```python
import functools

import jax
import jax.numpy as jnp
from jax import lax
from jax.experimental import pallas as pl
from jax.experimental.pallas import tpu as pltpu
from jax.sharding import PartitionSpec as P

NGRP = 224
GROUP_ROWS = 256
LANES = 128
HIGHEST = lax.Precision.HIGHEST


def round_up(value, unit):
    return -(-value // unit) * unit


class Part:
    def __init__(self, first, half):
        self.first = first
        self.half = half
        self.lanes = 2 * half


def parts_of(channels, devices):
    width = channels // devices
    whole = width // LANES * LANES
    parts = []
    if width - whole:
        parts.append(Part(devices * whole, width - whole))
    if whole:
        parts.append(Part(0, whole))
    return parts


def tile_pieces(parts, tile, which):
    at = tile * LANES
    _, index = max((part.first, k) for k, part in enumerate(parts) if part.first <= at)
    part = parts[index]
    at -= part.first
    end = at + LANES
    pieces = []
    while at < end:
        device, inside = divmod(at, part.half)
        width = min(part.half - inside, end - at)
        pieces.append((index, device, which * part.half + inside, width))
        at += width
    return pieces


def join(pieces):
    return pieces[0] if len(pieces) == 1 else jnp.concatenate(pieces, axis=-1)


def call(body, out_shape, vmem, work, **kwargs):
    flops, moved = work
    return pl.pallas_call(
        body,
        out_shape=out_shape,
        cost_estimate=pl.CostEstimate(flops=flops, bytes_accessed=moved, transcendentals=0),
        compiler_params=pltpu.CompilerParams(vmem_limit_bytes=vmem * 1024 * 1024),
        **kwargs,
    )


def digit_groups(own, lanes):
    return [(at, min(lanes, own - at)) for at in range(0, own, lanes)]


def digit_rows(own, lanes):
    return round_up(6 * len(digit_groups(own, lanes)), 16)


def pack_kernel(part, devices, leads, group_ref, couple_ref, amp_hbm, phase_hbm, out_hbm, *refs):
    out, amp, phase, in_sems, out_sems = refs
    own, span = amp.shape
    lanes, half = part.lanes, part.half
    blocks = in_sems.shape[1]
    rows = own // blocks
    copies = []
    for k in range(blocks):
        at = pl.ds(k * rows, rows)
        pair = [
            pltpu.make_async_copy(
                source.at[at, pl.ds(part.first, span)], target.at[at], in_sems.at[which, k]
            )
            for which, (source, target) in enumerate(((amp_hbm, amp), (phase_hbm, phase)))
        ]
        for copy in pair:
            copy.start()
        copies.append(pair)
    sent = []
    if leads:
        numbers = [group_ref[...], couple_ref[0:1, :], couple_ref[1:2, :]]
        digits = []
        for number in numbers:
            wide = number.astype(jnp.float32)
            high = jnp.floor(wide * (1.0 / LANES))
            digits += [high, wide - high * LANES]
        lines = []
        for first, width in digit_groups(own, lanes):
            for digit in digits:
                line = digit[:, first : first + width]
                if width < lanes:
                    line = jnp.concatenate(
                        [line, jnp.zeros((1, lanes - width), line.dtype)], axis=1
                    )
                lines.append(line)
        extra = digit_rows(own, lanes)
        lines.append(jnp.zeros((extra - len(lines), lanes), jnp.float32))
        lines = jnp.concatenate(lines, axis=0).astype(jnp.bfloat16)
        for device in range(devices):
            out[device, own:, :] = lines
        block = pl.ds(own, extra)
        copy = pltpu.make_async_copy(out.at[:, block], out_hbm.at[:, block], out_sems.at[blocks])
        copy.start()
        sent.append(copy)
    for k in range(blocks):
        for copy in copies[k]:
            copy.wait()
        at = slice(k * rows, (k + 1) * rows)
        for device in range(devices):
            for which, ref in enumerate((amp, phase)):
                out[device, at, which * half : (which + 1) * half] = ref[
                    at, device * half : (device + 1) * half
                ]
        block = pl.ds(k * rows, rows)
        copy = pltpu.make_async_copy(out.at[:, block], out_hbm.at[:, block], out_sems.at[k])
        copy.start()
        sent.append(copy)
    for copy in sent:
        copy.wait()


def hot_rows(labels, number):
    rows = lax.broadcasted_iota(jnp.int32, (labels, number.shape[1]), 0).astype(jnp.float32)
    return (rows == number).astype(jnp.float32).astype(jnp.bfloat16)


def solve_kernel(half, own, antennas, leads, *refs):
    if leads:
        x_ref, inverse_ref, gain_ref, sent_ref, index_ref, link_ref, sums = refs
    else:
        x_ref, inverse_ref, index_ref, link_ref, gain_ref, sent_ref, sums = refs
    devices, _, lanes = x_ref.shape
    sums[...] = jnp.zeros_like(sums)
    if leads:
        link_ref[...] = jnp.zeros_like(link_ref)

    def gather(device, carry):
        values = x_ref[device, 0:own, :]
        if leads:
            numbers = []
            for k in range(3):
                pieces = []
                for piece, (_, width) in enumerate(digit_groups(own, lanes)):
                    at = own + 6 * piece + 2 * k
                    block = x_ref[device, own:, :].astype(jnp.float32)
                    at -= own
                    pieces.append(
                        block[at : at + 1, :width] * LANES + block[at + 1 : at + 2, :width]
                    )
                numbers.append(join(pieces))
            index_ref[device] = jnp.concatenate(
                numbers + [jnp.zeros((5, own), jnp.float32)], axis=0
            )
        else:
            numbers = [index_ref[device, k : k + 1, :] for k in range(3)]
        group_hot = hot_rows(GROUP_ROWS, numbers[0])
        hots = [hot_rows(antennas, number) for number in numbers[1:]]
        hot = jnp.concatenate([group_hot] + hots, axis=0)
        sums[...] += jnp.dot(hot, values, preferred_element_type=jnp.float32)
        if leads:
            for k in range(2):
                link_ref[k] += lax.dot_general(
                    hots[k],
                    group_hot,
                    (((1,), (1,)), ((), ())),
                    preferred_element_type=jnp.float32,
                )
        return carry

    lax.fori_loop(0, devices, gather, 0, unroll=4)
    if leads:
        counts = jnp.sum(link_ref[0], axis=0, keepdims=True)
        share = 1.0 / jnp.maximum(counts, 1.0)
        firsts = link_ref[0] * share
        seconds = link_ref[1] * share
        link_ref[0] = firsts + seconds
        link_ref[1] = firsts - seconds
    low = lax.broadcasted_iota(jnp.int32, (antennas, lanes), 1) < half
    seconds = sums[GROUP_ROWS + antennas :, :]
    sides = sums[GROUP_ROWS : GROUP_ROWS + antennas, :] + jnp.where(low, seconds, -seconds)
    both = []
    for s in range(2):
        use = slice(s * half, (s + 1) * half) if half % LANES == 0 else slice(0, lanes)
        rhs = sides[:, use] - jnp.dot(
            link_ref[s],
            sums[:GROUP_ROWS, use],
            precision=HIGHEST,
            preferred_element_type=jnp.float32,
        )
        both.append(
            jnp.dot(
                inverse_ref[s], rhs, precision=HIGHEST, preferred_element_type=jnp.float32
            )
        )
    if half % LANES == 0:
        gain = jnp.concatenate(both, axis=1)
    else:
        gain = jnp.where(low, both[0], both[1])
    gain_ref[...] = gain
    sent_ref[0] = gain[: sent_ref.shape[1]].astype(jnp.bfloat16)


def reduced(angle):
    turns = jnp.floor(angle * 0.6366197723675814 + 0.5)
    left = angle - turns * 1.5703125
    left = left - turns * 4.83751296997070312e-4
    left = left - turns * 7.54978995489188216e-8
    square = left * left
    sine = ((-1.9515295891e-4 * square + 8.3321608736e-3) * square - 1.6666654611e-1) * square
    sine = sine * left + left
    cosine = (2.443315711809948e-5 * square - 1.388731625493765e-3) * square
    cosine = (cosine + 4.166664568298827e-2) * square * square - 0.5 * square + 1.0
    return turns.astype(jnp.int32), sine, cosine


def quarter(turns, sine, cosine):
    value = jnp.where((turns & 1) == 1, cosine, sine)
    return jnp.where((turns & 2) == 2, -value, value)


def swap(values, half):
    if 2 * half == LANES:
        return pltpu.roll(values, half, 1)
    return jnp.concatenate([values[:, half:], values[:, :half]], axis=1)


def calibrate_kernel(half, own, antennas, x_ref, index_ref, gain_ref, out_ref, split):
    lanes = gain_ref.shape[1]

    @pl.when(pl.program_id(0) == 0)
    def _():
        low = lax.broadcasted_iota(jnp.int32, (antennas, lanes), 1) < half
        left = gain_ref[...]
        for k in range(3):
            part = left.astype(jnp.bfloat16)
            wide = part.astype(jnp.float32)
            split[k, :antennas, :] = part
            split[k, antennas:, :] = jnp.where(low, wide, -wide).astype(jnp.bfloat16)
            left = left - wide

    labels = lax.broadcasted_iota(jnp.int32, (own, antennas), 1).astype(jnp.float32)
    for device in range(x_ref.shape[0]):
        columns = jnp.transpose(index_ref[device])
        hot = jnp.concatenate(
            [
                (labels == columns[:, k : k + 1]).astype(jnp.float32).astype(jnp.bfloat16)
                for k in (1, 2)
            ],
            axis=1,
        )
        move = jnp.dot(hot, split[0], preferred_element_type=jnp.float32)
        for k in range(1, 3):
            move = move + jnp.dot(hot, split[k], preferred_element_type=jnp.float32)
        left = x_ref[device, 0:own, :].astype(jnp.float32) - move
        at = slice(device * own, (device + 1) * own)
        if half % LANES == 0:
            magnitude = jnp.exp(left[:, :half])
            turns, sine, cosine = reduced(left[:, half:])
            real = magnitude * quarter(turns + 1, sine, cosine)
            imaginary = magnitude * quarter(turns, sine, cosine)
            out_ref[at, :half] = real.astype(jnp.bfloat16)
            out_ref[at, half:] = imaginary.astype(jnp.bfloat16)
        else:
            lower = lax.broadcasted_iota(jnp.int32, left.shape, 1) < half
            turned = swap(left, half)
            magnitude = jnp.exp(jnp.where(lower, left, turned))
            turns, sine, cosine = reduced(jnp.where(lower, turned, left))
            turns = jnp.where(lower, turns + 1, turns)
            value = magnitude * quarter(turns, sine, cosine)
            out_ref[at, :] = value.astype(jnp.bfloat16)


def nothing(*refs):
    pass


def after(values, *others):
    return call(
        nothing,
        jax.ShapeDtypeStruct(values.shape, values.dtype),
        4,
        (0, 0),
        in_specs=[pl.BlockSpec(memory_space=pl.ANY)] * (1 + len(others)),
        out_specs=pl.BlockSpec(memory_space=pl.ANY),
        input_output_aliases={0: 0},
        name="after",
    )(values, *others)


def pass_on(held, devices, reach):
    return lax.ppermute(held, "bl", [(i, i ^ reach) for i in range(devices)])


def gather_far_first(values, devices):
    held, arrived = values, []
    reach = devices // 2
    while reach:
        if arrived:
            held = jnp.concatenate([held, arrived[-1]], axis=0)
        arrived.append(pass_on(held, devices, reach))
        reach //= 2
    return held, arrived


def entries_of(devices):
    apart = jnp.arange(devices, dtype=jnp.int32) ^ lax.axis_index("bl")
    entries = jnp.zeros_like(apart)
    reach, weight = devices // 2, 1
    while reach:
        entries = entries + weight * ((apart // reach) % 2)
        reach //= 2
        weight *= 2
    return entries


def spread_kernel(parts, antennas, tiles, entry_ref, *refs):
    gain_refs, out_ref = refs[: 2 * len(parts)], refs[-1]
    which = pl.program_id(0)

    def piece(part, device, lane, width):
        near, far = gain_refs[2 * part : 2 * part + 2]
        count = near.shape[0]
        entry = entry_ref[device]
        inside = lax.rem(entry, count)
        lanes = slice(lane, lane + width)
        value = jnp.where(entry < count, near[inside, :, lanes], far[inside, :, lanes])
        return value.astype(jnp.float32)

    for s in range(2):

        @pl.when(which == s)
        def _():
            for tile in range(tiles):
                values = join([piece(*where) for where in tile_pieces(parts, tile, s)])
                out_ref[pl.ds(tile, antennas, tiles), :] = values[:antennas]


def fill_kernel(parts, times, reach, mask_ref, times_ref, kernel_ref, *refs):
    cal_refs, (out_ref, mark_ref, rows, band, interleave) = refs[:-5], refs[-5:]
    step = pl.program_id(0)
    block, tiles = mask_ref.shape
    count = 2 * times * block
    span = (2 * reach + 2) * LANES

    @pl.when(step == 0)
    def _():
        mark_ref[...] = jnp.zeros_like(mark_ref)
        keep = (1 - mask_ref[...]).astype(jnp.float32)
        edge = reach * LANES
        inner = (reach + tiles) * LANES
        rows[:, :edge] = jnp.zeros((rows.shape[0], edge), rows.dtype)
        rows[:, inner:] = jnp.zeros((rows.shape[0], rows.shape[1] - inner), rows.dtype)
        for tile in range(tiles):
            lanes = slice((reach + tile) * LANES, (reach + tile + 1) * LANES)
            weight = jnp.broadcast_to(keep[:, tile : tile + 1], (block, LANES))
            weight = weight.astype(rows.dtype)
            rows[count:, lanes] = weight
            for c in range(2):
                for t in range(times):
                    values = join(
                        [
                            cal_refs[part][device, t, :, lane : lane + width]
                            for part, device, lane, width in tile_pieces(parts, tile, c)
                        ]
                    )
                    at = (c * times + t) * block
                    rows[at : at + block, lanes] = values * weight
        order = times * block
        place = lax.broadcasted_iota(jnp.int32, (order, order), 0)
        origin = lax.broadcasted_iota(jnp.int32, (order, order), 1)
        moved = (place % times) * block + place // times == origin
        interleave[...] = moved.astype(jnp.float32).astype(jnp.bfloat16)
        zeros = jnp.zeros((LANES, LANES), band.dtype)
        for source in range(2 * reach + 2):
            for target in range(2):
                offset = source - target
                inside = 0 <= offset <= 2 * reach
                band[
                    source * LANES : (source + 1) * LANES, target * LANES : (target + 1) * LANES
                ] = kernel_ref[offset] if inside else zeros

    scales = []
    for t in range(times):
        scale = times_ref[t, 0]
        for u in range(1, times):
            scale = scale + times_ref[t, u]
        scales.append(scale)
    width = out_ref.shape[3]
    for pair in range(width // (2 * LANES)):
        lanes = slice(pair * 2 * LANES, (pair + 1) * 2 * LANES)
        at = pl.multiple_of(step * width + pair * 2 * LANES, 2 * LANES)
        mixed = jnp.dot(
            rows[:, pl.ds(at, span)], band[...], preferred_element_type=jnp.float32
        )
        total = 1.0 / mixed[count:]
        kept = rows[:, pl.ds(pl.multiple_of(at + reach * LANES, LANES), 2 * LANES)]
        kept = kept.astype(jnp.float32)
        keep = kept[count:] > 0.5
        for c in range(2):
            values = []
            for t in range(times):
                value = None
                for u in range(times):
                    first = (c * times + u) * block
                    part = times_ref[t, u] * mixed[first : first + block]
                    value = part if value is None else value + part
                first = (c * times + t) * block
                values.append(
                    jnp.where(
                        keep, kept[first : first + block], value * (total * (1.0 / scales[t]))
                    )
                )
            values = jnp.concatenate(values, axis=0)
            large = values.astype(jnp.bfloat16)
            small = (values - large.astype(jnp.float32)).astype(jnp.bfloat16)
            values = jnp.dot(
                interleave[...], large, preferred_element_type=jnp.float32
            ) + jnp.dot(interleave[...], small, preferred_element_type=jnp.float32)
            out_ref[c, :, :, lanes] = values.reshape(block, times, 2 * LANES)


def on_device(
    devices,
    log_amplitude,
    phase,
    redundant_group_index,
    antenna_couples,
    tile_flag_mask,
    inverse,
    integration_kernel,
    channel_kernel,
):
    own, _, channels = log_amplitude.shape
    total = own * devices
    real_antennas = inverse.shape[1]
    antennas = round_up(real_antennas, LANES)
    sent_antennas = round_up(real_antennas, 16)
    times = integration_kernel.shape[0]
    block = tile_flag_mask.shape[0]
    reach = (channel_kernel.shape[0] - 1) // 2
    tiles = channels // LANES
    parts = parts_of(channels, devices)
    gap = antennas - real_antennas
    wide_inverse = jnp.pad(inverse, ((0, 0), (0, gap), (0, gap)))
    extra = [digit_rows(own, part.lanes) if k == 0 else 0 for k, part in enumerate(parts)]
    shapes = [(devices, own + more, part.lanes) for part, more in zip(parts, extra)]
    blocks = 4
    packed = []
    for k, (part, shape) in enumerate(zip(parts, shapes)):
        packed.append(
            call(
                functools.partial(pack_kernel, part, devices, k == 0),
                jax.ShapeDtypeStruct(shape, jnp.bfloat16),
                60,
                (0, 8 * own * part.half * devices),
                in_specs=[
                    pl.BlockSpec(memory_space=pltpu.VMEM),
                    pl.BlockSpec(memory_space=pltpu.VMEM),
                    pl.BlockSpec(memory_space=pl.ANY),
                    pl.BlockSpec(memory_space=pl.ANY),
                ],
                out_specs=pl.BlockSpec(memory_space=pl.ANY),
                scratch_shapes=[pltpu.VMEM(shape, jnp.bfloat16)]
                + [pltpu.VMEM((own, devices * part.half), jnp.bfloat16)] * 2
                + [
                    pltpu.SemaphoreType.DMA((2, blocks)),
                    pltpu.SemaphoreType.DMA((blocks + 1,)),
                ],
                name="pack",
            )(
                redundant_group_index.reshape(1, own),
                jnp.transpose(antenna_couples),
                log_amplitude.reshape(own, channels),
                phase.reshape(own, channels),
            )
        )
    terms = [
        lax.all_to_all(values, "bl", split_axis=0, concat_axis=0, tiled=True) for values in packed
    ]

    ready = []
    chains = []
    indices = links = None
    large = total // 2048
    for k, (part, values) in enumerate(zip(parts, terms)):
        lanes = part.lanes
        shared = [
            jax.ShapeDtypeStruct((devices, 8, own), jnp.float32),
            jax.ShapeDtypeStruct((2, antennas, GROUP_ROWS), jnp.float32),
        ]
        results = call(
            functools.partial(solve_kernel, part.half, own, antennas, k == 0),
            [
                jax.ShapeDtypeStruct((antennas, lanes), jnp.float32),
                jax.ShapeDtypeStruct((1, sent_antennas, lanes), jnp.bfloat16),
            ]
            + (shared if k == 0 else []),
            min(56, 16 * large),
            (8 * total * (GROUP_ROWS + 2 * antennas) * lanes, 8 * total * lanes),
            scratch_shapes=[pltpu.VMEM((GROUP_ROWS + 2 * antennas, lanes), jnp.float32)],
            name="solve",
        )(values, wide_inverse, *([] if k == 0 else [indices, links]))
        gain, sent = results[:2]
        if k == 0:
            indices, links = results[2:]
        calibrated = call(
            functools.partial(calibrate_kernel, part.half, own, antennas),
            jax.ShapeDtypeStruct((total, lanes), jnp.bfloat16),
            16,
            (16 * total * antennas * lanes, 8 * total * lanes),
            grid=(devices // 2,),
            in_specs=[
                pl.BlockSpec((2,) + values.shape[1:], lambda i: (i, 0, 0)),
                pl.BlockSpec((2, 8, own), lambda i: (i, 0, 0)),
                pl.BlockSpec((antennas, lanes), lambda i: (0, 0)),
            ],
            out_specs=pl.BlockSpec((2 * own, lanes), lambda i: (i, 0)),
            scratch_shapes=[pltpu.VMEM((3, 2 * antennas, lanes), jnp.bfloat16)],
            name="calibrate",
        )(values, indices, gain)
        ready.append(calibrated)
        chains.append(gather_far_first(sent, devices))

    spread = [None] * len(parts)
    for k in reversed(range(len(parts))):
        values = ready[k]
        if len(parts) > 1 and k:
            values = after(values, chains[k][1][0], chains[0][1][1])
        elif len(parts) > 1:
            values = after(values, spread[1], *[held for held, _ in chains])
        spread[k] = lax.all_to_all(
            values, ("bl", "ta"), split_axis=0, concat_axis=0, tiled=True
        )
    spread = [
        values.reshape(devices, times, block, part.lanes) for values, part in zip(spread, parts)
    ]
    gathered = [values for held, arrived in chains for values in (held, arrived[-1])]

    filled, mark = call(
        functools.partial(fill_kernel, parts, times, reach),
        (
            jax.ShapeDtypeStruct((2, block, times, channels), jnp.float32),
            jax.ShapeDtypeStruct((8, LANES), jnp.float32),
        ),
        32,
        (32 * reach * block * times * channels * LANES, 16 * block * times * channels),
        grid=(tiles // 4,),
        in_specs=[
            pl.BlockSpec((block, tiles), lambda i: (0, 0)),
            pl.BlockSpec(memory_space=pltpu.SMEM),
            pl.BlockSpec(channel_kernel.shape, lambda i: (0, 0, 0)),
        ]
        + [pl.BlockSpec(values.shape, lambda i: (0, 0, 0, 0)) for values in spread],
        out_specs=(
            pl.BlockSpec((2, block, times, 4 * LANES), lambda i: (0, 0, 0, i)),
            pl.BlockSpec((8, LANES), lambda i: (0, 0)),
        ),
        scratch_shapes=[
            pltpu.VMEM(((2 * times + 1) * block, (tiles + 2 * reach) * LANES), jnp.bfloat16),
            pltpu.VMEM(((2 * reach + 2) * LANES, 2 * LANES), jnp.bfloat16),
            pltpu.VMEM((times * block, times * block), jnp.bfloat16),
        ],
        name="fill",
    )(tile_flag_mask, integration_kernel, jnp.swapaxes(channel_kernel, 1, 2), *spread)
    gains = call(
        functools.partial(spread_kernel, parts, real_antennas, tiles),
        jax.ShapeDtypeStruct((2 * real_antennas * tiles, LANES), jnp.float32),
        32,
        (0, 12 * real_antennas * channels),
        grid=(2,),
        in_specs=[pl.BlockSpec(memory_space=pltpu.SMEM)]
        + [pl.BlockSpec(values.shape, lambda i: (0, 0, 0)) for values in gathered]
        + [pl.BlockSpec(memory_space=pl.ANY)],
        out_specs=pl.BlockSpec((real_antennas * tiles, LANES), lambda i: (i, 0)),
        name="gains",
    )(entries_of(devices), *gathered, mark)

    return gains.reshape(2, real_antennas, 1, channels), filled


def solution(mesh):
    in_specs = (
        P("bl", "ta", None),
        P("bl", "ta", None),
        P("bl"),
        P("bl", None),
        P(("bl", "ta"), None),
        P(),
        P(),
        P(),
    )
    out_specs = (P(None, None, "ta", None), P(None, ("bl", "ta"), None, None))
    return jax.shard_map(
        functools.partial(on_device, mesh.shape["bl"]),
        mesh=mesh,
        in_specs=in_specs,
        out_specs=out_specs,
        check_vma=False,
    )
```

```python
import functools

import jax
import jax.numpy as jnp
from jax import lax
from jax.experimental import pallas as pl
from jax.experimental.pallas import tpu as pltpu
from jax.sharding import PartitionSpec as P

NGRP = 224
GROUP_ROWS = 256
LANES = 128
HIGHEST = lax.Precision.HIGHEST


def round_up(value, unit):
    return -(-value // unit) * unit


class Part:
    def __init__(self, first, half, at):
        self.first = first
        self.half = half
        self.at = at
        self.lanes = 2 * half


def parts_of(channels, devices):
    width = channels // devices
    whole = width // LANES * LANES
    parts = []
    if whole:
        parts.append(Part(0, whole, 0))
    if width - whole:
        parts.append(Part(devices * whole, width - whole, 2 * whole))
    return parts


def tile_pieces(parts, tile, which):
    at = tile * LANES
    index = max(k for k, part in enumerate(parts) if part.first <= at)
    part = parts[index]
    at -= part.first
    end = at + LANES
    pieces = []
    while at < end:
        device, inside = divmod(at, part.half)
        width = min(part.half - inside, end - at)
        pieces.append((index, device, which * part.half + inside, width))
        at += width
    return pieces


def join(pieces):
    return pieces[0] if len(pieces) == 1 else jnp.concatenate(pieces, axis=-1)


def call(body, out_shape, vmem, work, **kwargs):
    flops, moved = work
    return pl.pallas_call(
        body,
        out_shape=out_shape,
        cost_estimate=pl.CostEstimate(flops=flops, bytes_accessed=moved, transcendentals=0),
        compiler_params=pltpu.CompilerParams(vmem_limit_bytes=vmem * 1024 * 1024),
        **kwargs,
    )


def digit_groups(own, lanes):
    return [(at, min(lanes, own - at)) for at in range(0, own, lanes)]


def digit_rows(own, lanes):
    return round_up(6 * len(digit_groups(own, lanes)), 16)


def pack_kernel(parts, group_ref, couple_ref, amp_hbm, phase_hbm, out_hbm, *refs):
    out, amp, phase, in_sems, out_sems = refs
    own = amp.shape[0]
    devices, _, lanes = out.shape
    blocks = in_sems.shape[1]
    rows = own // blocks
    copies = []
    for k in range(blocks):
        at = pl.ds(k * rows, rows)
        pair = [
            pltpu.make_async_copy(
                source.at[at], target.at[at], in_sems.at[which, k]
            )
            for which, (source, target) in enumerate(((amp_hbm, amp), (phase_hbm, phase)))
        ]
        for copy in pair:
            copy.start()
        copies.append(pair)
    sent = []
    numbers = [group_ref[...], couple_ref[0:1, :], couple_ref[1:2, :]]
    digits = []
    for number in numbers:
        wide = number.astype(jnp.float32)
        high = jnp.floor(wide * (1.0 / LANES))
        digits += [high, wide - high * LANES]
    lines = []
    for first, width in digit_groups(own, lanes):
        for digit in digits:
            line = digit[:, first : first + width]
            if width < lanes:
                line = jnp.concatenate(
                    [line, jnp.zeros((1, lanes - width), line.dtype)], axis=1
                )
            lines.append(line)
    extra = digit_rows(own, lanes)
    lines.append(jnp.zeros((extra - len(lines), lanes), jnp.float32))
    lines = jnp.concatenate(lines, axis=0).astype(jnp.bfloat16)
    for device in range(devices):
        out[device, own:, :] = lines
    block = pl.ds(own, extra)
    copy = pltpu.make_async_copy(out.at[:, block], out_hbm.at[:, block], out_sems.at[blocks])
    copy.start()
    sent.append(copy)
    for k in range(blocks):
        for copy in copies[k]:
            copy.wait()
        at = slice(k * rows, (k + 1) * rows)
        for part in parts:
            half = part.half
            for device in range(devices):
                first = part.first + device * half
                for which, ref in enumerate((amp, phase)):
                    lane = part.at + which * half
                    out[device, at, lane : lane + half] = ref[at, first : first + half]
        block = pl.ds(k * rows, rows)
        copy = pltpu.make_async_copy(out.at[:, block], out_hbm.at[:, block], out_sems.at[k])
        copy.start()
        sent.append(copy)
    for copy in sent:
        copy.wait()


def hot_rows(labels, number):
    rows = lax.broadcasted_iota(jnp.int32, (labels, number.shape[1]), 0).astype(jnp.float32)
    return (rows == number).astype(jnp.float32).astype(jnp.bfloat16)


def solve_kernel(parts, own, x_ref, inverse_ref, gain_ref, sent_ref, index_ref, sums, link):
    devices, _, lanes = x_ref.shape
    antennas = gain_ref.shape[0]
    sums[...] = jnp.zeros_like(sums)
    link[...] = jnp.zeros_like(link)

    def gather(device, carry):
        digits = x_ref[device, own:, :].astype(jnp.float32)
        numbers = []
        for k in range(3):
            pieces = []
            for piece, (_, width) in enumerate(digit_groups(own, lanes)):
                at = 6 * piece + 2 * k
                pieces.append(
                    digits[at : at + 1, :width] * LANES + digits[at + 1 : at + 2, :width]
                )
            numbers.append(join(pieces))
        index_ref[device] = jnp.concatenate(numbers + [jnp.zeros((5, own), jnp.float32)], axis=0)
        group_hot = hot_rows(GROUP_ROWS, numbers[0])
        hots = [hot_rows(antennas, number) for number in numbers[1:]]
        hot = jnp.concatenate([group_hot] + hots, axis=0)
        sums[...] += jnp.dot(
            hot, x_ref[device, 0:own, :], preferred_element_type=jnp.float32
        )
        link[...] += lax.dot_general(
            hot[GROUP_ROWS:],
            group_hot,
            (((1,), (1,)), ((), ())),
            preferred_element_type=jnp.float32,
        )
        return carry

    lax.fori_loop(0, devices, gather, 0, unroll=4)
    firsts, seconds = link[:antennas, :], link[antennas:, :]
    share = 1.0 / jnp.maximum(jnp.sum(firsts, axis=0, keepdims=True), 1.0)
    for s, sign in enumerate((1.0, -1.0)):
        own_lanes = []
        for part in parts:
            if part.half % LANES == 0:
                own_lanes.append(slice(part.at + s * part.half, part.at + (s + 1) * part.half))
            else:
                own_lanes.append(slice(part.at, part.at + part.lanes))
        group_sums, first_sums, second_sums = (
            join([sums[rows, use] for use in own_lanes])
            for rows in (
                slice(0, GROUP_ROWS),
                slice(GROUP_ROWS, GROUP_ROWS + antennas),
                slice(GROUP_ROWS + antennas, GROUP_ROWS + 2 * antennas),
            )
        )
        rhs = (first_sums + sign * second_sums) - jnp.dot(
            (firsts + sign * seconds) * share,
            group_sums,
            precision=HIGHEST,
            preferred_element_type=jnp.float32,
        )
        gain = jnp.dot(
            inverse_ref[s], rhs, precision=HIGHEST, preferred_element_type=jnp.float32
        )
        at = 0
        for part, use in zip(parts, own_lanes):
            width = use.stop - use.start
            values = gain[:, at : at + width]
            if s and width == part.lanes:
                low = lax.broadcasted_iota(jnp.int32, values.shape, 1) < part.half
                values = jnp.where(low, gain_ref[:, use], values)
            gain_ref[:, use] = values
            at += width
    sent_ref[0] = gain_ref[: sent_ref.shape[1], :].astype(jnp.bfloat16)


def reduced(angle):
    turns = jnp.floor(angle * 0.6366197723675814 + 0.5)
    left = angle - turns * 1.5703125
    left = left - turns * 4.83751296997070312e-4
    left = left - turns * 7.54978995489188216e-8
    square = left * left
    sine = ((-1.9515295891e-4 * square + 8.3321608736e-3) * square - 1.6666654611e-1) * square
    sine = sine * left + left
    cosine = (2.443315711809948e-5 * square - 1.388731625493765e-3) * square
    cosine = (cosine + 4.166664568298827e-2) * square * square - 0.5 * square + 1.0
    return turns.astype(jnp.int32), sine, cosine


def quarter(turns, sine, cosine):
    value = jnp.where((turns & 1) == 1, cosine, sine)
    return jnp.where((turns & 2) == 2, -value, value)


def swap(values, half):
    if 2 * half == LANES:
        return pltpu.roll(values, half, 1)
    return jnp.concatenate([values[:, half:], values[:, :half]], axis=1)


def calibrate_kernel(half, own, antennas, x_ref, index_ref, gain_ref, out_ref, split):
    lanes = gain_ref.shape[1]

    @pl.when(pl.program_id(0) == 0)
    def _():
        low = lax.broadcasted_iota(jnp.int32, (antennas, lanes), 1) < half
        left = gain_ref[...]
        for k in range(3):
            part = left.astype(jnp.bfloat16)
            wide = part.astype(jnp.float32)
            split[k, :antennas, :] = part
            split[k, antennas:, :] = jnp.where(low, wide, -wide).astype(jnp.bfloat16)
            left = left - wide

    labels = lax.broadcasted_iota(jnp.int32, (own, antennas), 1).astype(jnp.float32)
    for device in range(x_ref.shape[0]):
        columns = jnp.transpose(index_ref[device])
        hot = jnp.concatenate(
            [
                (labels == columns[:, k : k + 1]).astype(jnp.float32).astype(jnp.bfloat16)
                for k in (1, 2)
            ],
            axis=1,
        )
        move = jnp.dot(hot, split[0], preferred_element_type=jnp.float32)
        for k in range(1, 3):
            move = move + jnp.dot(hot, split[k], preferred_element_type=jnp.float32)
        left = x_ref[device, 0:own, :].astype(jnp.float32) - move
        at = slice(device * own, (device + 1) * own)
        if half % LANES == 0:
            magnitude = jnp.exp(left[:, :half])
            turns, sine, cosine = reduced(left[:, half:])
            real = magnitude * quarter(turns + 1, sine, cosine)
            imaginary = magnitude * quarter(turns, sine, cosine)
            out_ref[at, :half] = real.astype(jnp.bfloat16)
            out_ref[at, half:] = imaginary.astype(jnp.bfloat16)
        else:
            lower = lax.broadcasted_iota(jnp.int32, left.shape, 1) < half
            turned = swap(left, half)
            magnitude = jnp.exp(jnp.where(lower, left, turned))
            turns, sine, cosine = reduced(jnp.where(lower, turned, left))
            turns = jnp.where(lower, turns + 1, turns)
            value = magnitude * quarter(turns, sine, cosine)
            out_ref[at, :] = value.astype(jnp.bfloat16)


def nothing(*refs):
    pass


def after(values, *others):
    return call(
        nothing,
        jax.ShapeDtypeStruct(values.shape, values.dtype),
        4,
        (0, 0),
        in_specs=[pl.BlockSpec(memory_space=pl.ANY)] * (1 + len(others)),
        out_specs=pl.BlockSpec(memory_space=pl.ANY),
        input_output_aliases={0: 0},
        name="after",
    )(values, *others)


def pass_on(held, devices, reach):
    return lax.ppermute(held, "bl", [(i, i ^ reach) for i in range(devices)])


def entries_of(devices):
    apart = jnp.arange(devices, dtype=jnp.int32) ^ lax.axis_index("bl")
    entries = jnp.zeros_like(apart)
    reach, weight = devices // 2, 1
    while reach > 2:
        entries = entries + weight * ((apart // reach) % 2)
        reach //= 2
        weight *= 2
    return jnp.stack([apart % 4, entries])


def spread_kernel(parts, antennas, tiles, entry_ref, *refs):
    gain_refs, out_ref = refs[:4], refs[-1]
    which = pl.program_id(0)

    def piece(part, device, lane, width):
        source, entry = entry_ref[0, device], entry_ref[1, device]
        lane += parts[part].at
        value = gain_refs[0][entry, :, lane : lane + width]
        for k in range(1, 4):
            value = jnp.where(source == k, gain_refs[k][entry, :, lane : lane + width], value)
        return value.astype(jnp.float32)

    for s in range(2):

        @pl.when(which == s)
        def _():
            for tile in range(tiles):
                values = join([piece(*where) for where in tile_pieces(parts, tile, s)])
                out_ref[pl.ds(tile, antennas, tiles), :] = values[:antennas]


def fill_kernel(parts, times, reach, mask_ref, times_ref, kernel_ref, *refs):
    cal_refs, (out_ref, mark_ref, rows, band, interleave) = refs[:-5], refs[-5:]
    step = pl.program_id(0)
    block, tiles = mask_ref.shape
    count = 2 * times * block
    span = (2 * reach + 2) * LANES

    @pl.when(step == 0)
    def _():
        mark_ref[...] = jnp.zeros_like(mark_ref)
        keep = (1 - mask_ref[...]).astype(jnp.float32)
        edge = reach * LANES
        inner = (reach + tiles) * LANES
        rows[:, :edge] = jnp.zeros((rows.shape[0], edge), rows.dtype)
        rows[:, inner:] = jnp.zeros((rows.shape[0], rows.shape[1] - inner), rows.dtype)
        for tile in range(tiles):
            lanes = slice((reach + tile) * LANES, (reach + tile + 1) * LANES)
            weight = jnp.broadcast_to(keep[:, tile : tile + 1], (block, LANES))
            weight = weight.astype(rows.dtype)
            rows[count:, lanes] = weight
            for c in range(2):
                for t in range(times):
                    values = join(
                        [
                            cal_refs[part][device, t, :, lane : lane + width]
                            for part, device, lane, width in tile_pieces(parts, tile, c)
                        ]
                    )
                    at = (c * times + t) * block
                    rows[at : at + block, lanes] = values * weight
        order = times * block
        place = lax.broadcasted_iota(jnp.int32, (order, order), 0)
        origin = lax.broadcasted_iota(jnp.int32, (order, order), 1)
        moved = (place % times) * block + place // times == origin
        interleave[...] = moved.astype(jnp.float32).astype(jnp.bfloat16)
        band[...] = jnp.zeros(band.shape, band.dtype)
        for offset in range(2 * reach + 1):
            turned = jnp.transpose(kernel_ref[offset].astype(jnp.float32)).astype(band.dtype)
            for target in range(2):
                first = (offset + target) * LANES
                band[first : first + LANES, target * LANES : (target + 1) * LANES] = turned

    scales = []
    for t in range(times):
        scale = times_ref[t, 0]
        for u in range(1, times):
            scale = scale + times_ref[t, u]
        scales.append(scale)
    width = out_ref.shape[3]
    for pair in range(width // (2 * LANES)):
        lanes = slice(pair * 2 * LANES, (pair + 1) * 2 * LANES)
        at = pl.multiple_of(step * width + pair * 2 * LANES, 2 * LANES)
        mixed = jnp.dot(
            rows[:, pl.ds(at, span)], band[...], preferred_element_type=jnp.float32
        )
        total = 1.0 / mixed[count:]
        kept = rows[:, pl.ds(pl.multiple_of(at + reach * LANES, LANES), 2 * LANES)]
        kept = kept.astype(jnp.float32)
        keep = kept[count:] > 0.5
        for c in range(2):
            values = []
            for t in range(times):
                value = None
                for u in range(times):
                    first = (c * times + u) * block
                    part = times_ref[t, u] * mixed[first : first + block]
                    value = part if value is None else value + part
                first = (c * times + t) * block
                values.append(
                    jnp.where(
                        keep, kept[first : first + block], value * (total * (1.0 / scales[t]))
                    )
                )
            values = jnp.concatenate(values, axis=0)
            large = values.astype(jnp.bfloat16)
            small = (values - large.astype(jnp.float32)).astype(jnp.bfloat16)
            values = jnp.dot(
                interleave[...], large, preferred_element_type=jnp.float32
            ) + jnp.dot(interleave[...], small, preferred_element_type=jnp.float32)
            out_ref[c, :, :, lanes] = values.reshape(block, times, 2 * LANES)


def on_device(
    devices,
    log_amplitude,
    phase,
    redundant_group_index,
    antenna_couples,
    tile_flag_mask,
    inverse,
    integration_kernel,
    channel_kernel,
):
    own, _, channels = log_amplitude.shape
    total = own * devices
    real_antennas = inverse.shape[1]
    antennas = round_up(real_antennas, LANES)
    sent_antennas = round_up(real_antennas, 16)
    times = integration_kernel.shape[0]
    block = tile_flag_mask.shape[0]
    reach = (channel_kernel.shape[0] - 1) // 2
    tiles = channels // LANES
    parts = parts_of(channels, devices)
    gap = antennas - real_antennas
    wide_inverse = jnp.pad(inverse, ((0, 0), (0, gap), (0, gap)))
    lanes = sum(part.lanes for part in parts)
    extra = digit_rows(own, lanes)
    shape = (devices, own + extra, lanes)
    blocks = 4
    packed = call(
        functools.partial(pack_kernel, parts),
        jax.ShapeDtypeStruct(shape, jnp.bfloat16),
        60,
        (0, 8 * own * channels),
        in_specs=[
            pl.BlockSpec(memory_space=pltpu.VMEM),
            pl.BlockSpec(memory_space=pltpu.VMEM),
            pl.BlockSpec(memory_space=pl.ANY),
            pl.BlockSpec(memory_space=pl.ANY),
        ],
        out_specs=pl.BlockSpec(memory_space=pl.ANY),
        scratch_shapes=[pltpu.VMEM(shape, jnp.bfloat16)]
        + [pltpu.VMEM((own, channels), jnp.bfloat16)] * 2
        + [pltpu.SemaphoreType.DMA((2, blocks)), pltpu.SemaphoreType.DMA((blocks + 1,))],
        name="pack",
    )(
        redundant_group_index.reshape(1, own),
        jnp.transpose(antenna_couples),
        log_amplitude.reshape(own, channels),
        phase.reshape(own, channels),
    )
    terms = lax.all_to_all(packed, "bl", split_axis=0, concat_axis=0, tiled=True)

    large = total // 2048
    down_rows = GROUP_ROWS + 2 * antennas
    gain, sent, indices = call(
        functools.partial(solve_kernel, parts, own),
        [
            jax.ShapeDtypeStruct((antennas, lanes), jnp.float32),
            jax.ShapeDtypeStruct((1, sent_antennas, lanes), jnp.bfloat16),
            jax.ShapeDtypeStruct((devices, 8, own), jnp.float32),
        ],
        min(56, 20 * large),
        (8 * total * down_rows * lanes, 8 * total * lanes),
        scratch_shapes=[
            pltpu.VMEM((down_rows, lanes), jnp.float32),
            pltpu.VMEM((2 * antennas, GROUP_ROWS), jnp.float32),
        ],
        name="solve",
    )(terms, wide_inverse)

    held = sent
    hop = devices // 2
    while hop > 2:
        held = jnp.concatenate([held, pass_on(held, devices, hop)], axis=0)
        hop //= 2
    near = pass_on(held, devices, 2)
    gathered = [held, pass_on(held, devices, 1), near, pass_on(near, devices, 1)]

    spread = []
    for part in parts:
        column = part.at // part.lanes
        calibrated = call(
            functools.partial(calibrate_kernel, part.half, own, antennas),
            jax.ShapeDtypeStruct((total, part.lanes), jnp.bfloat16),
            16,
            (16 * total * antennas * part.lanes, 8 * total * part.lanes),
            grid=(devices // 2,),
            in_specs=[
                pl.BlockSpec((2, own + extra, part.lanes), lambda i, c=column: (i, 0, c)),
                pl.BlockSpec((2, 8, own), lambda i: (i, 0, 0)),
                pl.BlockSpec((antennas, part.lanes), lambda i, c=column: (0, c)),
            ],
            out_specs=pl.BlockSpec((2 * own, part.lanes), lambda i: (i, 0)),
            scratch_shapes=[pltpu.VMEM((3, 2 * antennas, part.lanes), jnp.bfloat16)],
            name="calibrate",
        )(terms, indices, gain)
        if spread:
            calibrated = after(calibrated, spread[0], gathered[1], gathered[2])
        else:
            calibrated = after(calibrated, held)
        spread.append(
            lax.all_to_all(calibrated, ("bl", "ta"), split_axis=0, concat_axis=0, tiled=True)
        )
    spread = [
        values.reshape(devices, times, block, part.lanes) for values, part in zip(spread, parts)
    ]

    filled, mark = call(
        functools.partial(fill_kernel, parts, times, reach),
        (
            jax.ShapeDtypeStruct((2, block, times, channels), jnp.float32),
            jax.ShapeDtypeStruct((8, LANES), jnp.float32),
        ),
        32,
        (32 * reach * block * times * channels * LANES, 16 * block * times * channels),
        grid=(tiles // 4,),
        in_specs=[
            pl.BlockSpec((block, tiles), lambda i: (0, 0)),
            pl.BlockSpec(memory_space=pltpu.SMEM),
            pl.BlockSpec(channel_kernel.shape, lambda i: (0, 0, 0)),
        ]
        + [pl.BlockSpec(values.shape, lambda i: (0, 0, 0, 0)) for values in spread],
        out_specs=(
            pl.BlockSpec((2, block, times, 4 * LANES), lambda i: (0, 0, 0, i)),
            pl.BlockSpec((8, LANES), lambda i: (0, 0)),
        ),
        scratch_shapes=[
            pltpu.VMEM(((2 * times + 1) * block, (tiles + 2 * reach) * LANES), jnp.bfloat16),
            pltpu.VMEM(((2 * reach + 2) * LANES, 2 * LANES), jnp.bfloat16),
            pltpu.VMEM((times * block, times * block), jnp.bfloat16),
        ],
        name="fill",
    )(tile_flag_mask, integration_kernel, channel_kernel, *spread)
    gains = call(
        functools.partial(spread_kernel, parts, real_antennas, tiles),
        jax.ShapeDtypeStruct((2 * real_antennas * tiles, LANES), jnp.float32),
        32,
        (0, 12 * real_antennas * channels),
        grid=(2,),
        in_specs=[pl.BlockSpec(memory_space=pltpu.SMEM)]
        + [pl.BlockSpec(values.shape, lambda i: (0, 0, 0)) for values in gathered]
        + [pl.BlockSpec(memory_space=pl.ANY)],
        out_specs=pl.BlockSpec((real_antennas * tiles, LANES), lambda i: (i, 0)),
        name="gains",
    )(entries_of(devices), *gathered, mark)

    return gains.reshape(2, real_antennas, 1, channels), filled


def solution(mesh):
    in_specs = (
        P("bl", "ta", None),
        P("bl", "ta", None),
        P("bl"),
        P("bl", None),
        P(("bl", "ta"), None),
        P(),
        P(),
        P(),
    )
    out_specs = (P(None, None, "ta", None), P(None, ("bl", "ta"), None, None))
    return jax.shard_map(
        functools.partial(on_device, mesh.shape["bl"]),
        mesh=mesh,
        in_specs=in_specs,
        out_specs=out_specs,
        check_vma=False,
    )
```

```python
import functools

import jax
import jax.numpy as jnp
from jax import lax
from jax.experimental import pallas as pl
from jax.experimental.pallas import tpu as pltpu
from jax.sharding import PartitionSpec as P

NGRP = 224
GROUP_ROWS = 256
LANES = 128
HIGHEST = lax.Precision.HIGHEST


def round_up(value, unit):
    return -(-value // unit) * unit


class Part:
    def __init__(self, first, half, at):
        self.first = first
        self.half = half
        self.at = at
        self.lanes = 2 * half


def parts_of(channels, devices):
    width = channels // devices
    whole = width // LANES * LANES
    parts = []
    if whole:
        parts.append(Part(0, whole, 0))
    if width - whole:
        parts.append(Part(devices * whole, width - whole, 2 * whole))
    return parts


def tile_pieces(parts, tile, which):
    at = tile * LANES
    index = max(k for k, part in enumerate(parts) if part.first <= at)
    part = parts[index]
    at -= part.first
    end = at + LANES
    pieces = []
    while at < end:
        device, inside = divmod(at, part.half)
        width = min(part.half - inside, end - at)
        pieces.append((index, device, which * part.half + inside, width))
        at += width
    return pieces


def lanes_of(parts, which):
    slices = []
    for part in parts:
        if part.half % LANES == 0:
            slices.append(slice(part.at + which * part.half, part.at + (which + 1) * part.half))
        else:
            slices.append(slice(part.at, part.at + part.lanes))
    return slices


def join(pieces):
    return pieces[0] if len(pieces) == 1 else jnp.concatenate(pieces, axis=-1)


def call(body, out_shape, vmem, work, **kwargs):
    flops, moved = work
    return pl.pallas_call(
        body,
        out_shape=out_shape,
        cost_estimate=pl.CostEstimate(flops=flops, bytes_accessed=moved, transcendentals=0),
        compiler_params=pltpu.CompilerParams(vmem_limit_bytes=vmem * 1024 * 1024),
        **kwargs,
    )


def digit_groups(own, lanes):
    return [(at, min(lanes, own - at)) for at in range(0, own, lanes)]


def digit_rows(own, lanes):
    return round_up(6 * len(digit_groups(own, lanes)), 16)


def pack_kernel(parts, group_ref, couple_ref, amp_hbm, phase_hbm, out_hbm, *refs):
    out, amp, phase, in_sems, out_sems = refs
    own = amp.shape[0]
    devices, _, lanes = out.shape
    blocks = in_sems.shape[1]
    rows = own // blocks
    copies = []
    for k in range(blocks):
        at = pl.ds(k * rows, rows)
        pair = [
            pltpu.make_async_copy(
                source.at[at], target.at[at], in_sems.at[which, k]
            )
            for which, (source, target) in enumerate(((amp_hbm, amp), (phase_hbm, phase)))
        ]
        for copy in pair:
            copy.start()
        copies.append(pair)
    sent = []
    numbers = [group_ref[...], couple_ref[0:1, :], couple_ref[1:2, :]]
    digits = []
    for number in numbers:
        wide = number.astype(jnp.float32)
        high = jnp.floor(wide * (1.0 / LANES))
        digits += [high, wide - high * LANES]
    lines = []
    for first, width in digit_groups(own, lanes):
        for digit in digits:
            line = digit[:, first : first + width]
            if width < lanes:
                line = jnp.concatenate(
                    [line, jnp.zeros((1, lanes - width), line.dtype)], axis=1
                )
            lines.append(line)
    extra = digit_rows(own, lanes)
    lines.append(jnp.zeros((extra - len(lines), lanes), jnp.float32))
    lines = jnp.concatenate(lines, axis=0).astype(jnp.bfloat16)
    for device in range(devices):
        out[device, own:, :] = lines
    block = pl.ds(own, extra)
    copy = pltpu.make_async_copy(out.at[:, block], out_hbm.at[:, block], out_sems.at[blocks])
    copy.start()
    sent.append(copy)
    for k in range(blocks):
        for copy in copies[k]:
            copy.wait()
        at = slice(k * rows, (k + 1) * rows)
        for part in parts:
            half = part.half
            for device in range(devices):
                first = part.first + device * half
                for which, ref in enumerate((amp, phase)):
                    lane = part.at + which * half
                    out[device, at, lane : lane + half] = ref[at, first : first + half]
        block = pl.ds(k * rows, rows)
        copy = pltpu.make_async_copy(out.at[:, block], out_hbm.at[:, block], out_sems.at[k])
        copy.start()
        sent.append(copy)
    for copy in sent:
        copy.wait()


def hot_rows(labels, number):
    rows = lax.broadcasted_iota(jnp.int32, (labels, number.shape[1]), 0).astype(jnp.float32)
    return (rows == number).astype(jnp.float32)


def solve_kernel(parts, own, x_ref, inverse_ref, gain_ref, sent_ref, index_ref, sums, link):
    devices, _, lanes = x_ref.shape
    antennas = gain_ref.shape[0]
    sums[...] = jnp.zeros_like(sums)
    link[...] = jnp.zeros_like(link)

    def gather(device, carry):
        digits = x_ref[device, own:, :].astype(jnp.float32)
        numbers = []
        for k in range(3):
            pieces = []
            for piece, (_, width) in enumerate(digit_groups(own, lanes)):
                at = 6 * piece + 2 * k
                pieces.append(
                    digits[at : at + 1, :width] * LANES + digits[at + 1 : at + 2, :width]
                )
            numbers.append(join(pieces))
        index_ref[device] = jnp.concatenate(numbers + [jnp.zeros((5, own), jnp.float32)], axis=0)
        group_hot = hot_rows(GROUP_ROWS, numbers[0]).astype(jnp.bfloat16)
        first, second = [hot_rows(antennas, number) for number in numbers[1:]]
        for s, couple in enumerate((first + second, first - second)):
            hot = jnp.concatenate([group_hot, couple.astype(jnp.bfloat16)], axis=0)
            values = join([x_ref[device, 0:own, use] for use in lanes_of(parts, s)])
            sums[s] += jnp.dot(hot, values, preferred_element_type=jnp.float32)
            link[s] += lax.dot_general(
                hot[GROUP_ROWS:],
                group_hot,
                (((1,), (1,)), ((), ())),
                preferred_element_type=jnp.float32,
            )
        return carry

    lax.fori_loop(0, devices, gather, 0, unroll=4)
    counts = 0.5 * jnp.sum(link[0], axis=0, keepdims=True)
    share = 1.0 / jnp.maximum(counts, 1.0)
    for s in range(2):
        rhs = sums[s, GROUP_ROWS:, :] - jnp.dot(
            link[s] * share,
            sums[s, :GROUP_ROWS, :],
            precision=HIGHEST,
            preferred_element_type=jnp.float32,
        )
        gain = jnp.dot(
            inverse_ref[s], rhs, precision=HIGHEST, preferred_element_type=jnp.float32
        )
        at = 0
        for part, use in zip(parts, lanes_of(parts, s)):
            width = use.stop - use.start
            values = gain[:, at : at + width]
            if s and width == part.lanes:
                low = lax.broadcasted_iota(jnp.int32, values.shape, 1) < part.half
                values = jnp.where(low, gain_ref[:, use], values)
            gain_ref[:, use] = values
            at += width
    sent_ref[0] = gain_ref[: sent_ref.shape[1], :].astype(jnp.bfloat16)


def reduced(angle):
    turns = jnp.floor(angle * 0.6366197723675814 + 0.5)
    left = angle - turns * 1.5703125
    left = left - turns * 4.83751296997070312e-4
    left = left - turns * 7.54978995489188216e-8
    square = left * left
    sine = ((-1.9515295891e-4 * square + 8.3321608736e-3) * square - 1.6666654611e-1) * square
    sine = sine * left + left
    cosine = (2.443315711809948e-5 * square - 1.388731625493765e-3) * square
    cosine = (cosine + 4.166664568298827e-2) * square * square - 0.5 * square + 1.0
    return turns.astype(jnp.int32), sine, cosine


def quarter(turns, sine, cosine):
    value = jnp.where((turns & 1) == 1, cosine, sine)
    return jnp.where((turns & 2) == 2, -value, value)


def swap(values, half):
    if 2 * half == LANES:
        return pltpu.roll(values, half, 1)
    return jnp.concatenate([values[:, half:], values[:, :half]], axis=1)


def calibrate_kernel(parts, own, x_ref, index_ref, gain_ref, out_ref, split):
    antennas = gain_ref.shape[0]

    @pl.when(pl.program_id(0) == 0)
    def _():
        for s in range(2):
            left = join([gain_ref[:, use] for use in lanes_of(parts, s)])
            for k in range(3):
                part = left.astype(jnp.bfloat16)
                split[s, k] = part
                left = left - part.astype(jnp.float32)

    labels = lax.broadcasted_iota(jnp.int32, (own, antennas), 1).astype(jnp.float32)
    for device in range(x_ref.shape[0]):
        columns = jnp.transpose(index_ref[device])
        first, second = [
            (labels == columns[:, k : k + 1]).astype(jnp.float32) for k in (1, 2)
        ]
        moves = []
        for s, couple in enumerate((first + second, first - second)):
            hot = couple.astype(jnp.bfloat16)
            move = jnp.dot(hot, split[s, 0], preferred_element_type=jnp.float32)
            for k in range(1, 3):
                move = move + jnp.dot(hot, split[s, k], preferred_element_type=jnp.float32)
            moves.append(move)
        rows = slice(device * own, (device + 1) * own)
        at = 0
        for part in parts:
            half, lanes = part.half, part.lanes
            first_lanes = slice(part.at, part.at + half)
            second_lanes = slice(part.at + half, part.at + lanes)
            if half % LANES == 0:
                here = slice(at, at + half)
                left = x_ref[device, 0:own, first_lanes].astype(jnp.float32) - moves[0][:, here]
                magnitude = jnp.exp(left)
                left = x_ref[device, 0:own, second_lanes].astype(jnp.float32) - moves[1][:, here]
                turns, sine, cosine = reduced(left)
                real = magnitude * quarter(turns + 1, sine, cosine)
                imaginary = magnitude * quarter(turns, sine, cosine)
                out_ref[rows, first_lanes] = real.astype(jnp.bfloat16)
                out_ref[rows, second_lanes] = imaginary.astype(jnp.bfloat16)
                at += half
            else:
                here = slice(at, at + lanes)
                both = slice(part.at, part.at + lanes)
                left = x_ref[device, 0:own, both].astype(jnp.float32)
                lower = lax.broadcasted_iota(jnp.int32, left.shape, 1) < half
                left = left - jnp.where(lower, moves[0][:, here], moves[1][:, here])
                turned = swap(left, half)
                magnitude = jnp.exp(jnp.where(lower, left, turned))
                turns, sine, cosine = reduced(jnp.where(lower, turned, left))
                turns = jnp.where(lower, turns + 1, turns)
                value = magnitude * quarter(turns, sine, cosine)
                out_ref[rows, both] = value.astype(jnp.bfloat16)
                at += lanes


def nothing(*refs):
    pass


def after(values, *others):
    return call(
        nothing,
        jax.ShapeDtypeStruct(values.shape, values.dtype),
        4,
        (0, 0),
        in_specs=[pl.BlockSpec(memory_space=pl.ANY)] * (1 + len(others)),
        out_specs=pl.BlockSpec(memory_space=pl.ANY),
        input_output_aliases={0: 0},
        name="after",
    )(values, *others)


def pass_on(held, devices, reach):
    return lax.ppermute(held, "bl", [(i, i ^ reach) for i in range(devices)])


def entries_of(devices):
    apart = jnp.arange(devices, dtype=jnp.int32) ^ lax.axis_index("bl")
    entries = jnp.zeros_like(apart)
    reach, weight = devices // 2, 1
    while reach > 2:
        entries = entries + weight * ((apart // reach) % 2)
        reach //= 2
        weight *= 2
    return jnp.stack([apart % 4, entries])


def spread_kernel(parts, antennas, tiles, entry_ref, *refs):
    gain_refs, out_ref = refs[:4], refs[-1]
    which = pl.program_id(0)

    def piece(part, device, lane, width):
        source, entry = entry_ref[0, device], entry_ref[1, device]
        lane += parts[part].at
        value = gain_refs[0][entry, :, lane : lane + width]
        for k in range(1, 4):
            value = jnp.where(source == k, gain_refs[k][entry, :, lane : lane + width], value)
        return value.astype(jnp.float32)

    for s in range(2):

        @pl.when(which == s)
        def _():
            for tile in range(tiles):
                values = join([piece(*where) for where in tile_pieces(parts, tile, s)])
                out_ref[pl.ds(tile, antennas, tiles), :] = values[:antennas]


def fill_kernel(parts, times, reach, mask_ref, times_ref, kernel_ref, *refs):
    cal_ref, (out_ref, mark_ref, rows, band, interleave) = refs[0], refs[-5:]
    step = pl.program_id(0)
    block, tiles = mask_ref.shape
    count = 2 * times * block
    span = (2 * reach + 2) * LANES

    @pl.when(step == 0)
    def _():
        mark_ref[...] = jnp.zeros_like(mark_ref)
        keep = (1 - mask_ref[...]).astype(jnp.float32)
        edge = reach * LANES
        inner = (reach + tiles) * LANES
        rows[:, :edge] = jnp.zeros((rows.shape[0], edge), rows.dtype)
        rows[:, inner:] = jnp.zeros((rows.shape[0], rows.shape[1] - inner), rows.dtype)
        for tile in range(tiles):
            lanes = slice((reach + tile) * LANES, (reach + tile + 1) * LANES)
            weight = jnp.broadcast_to(keep[:, tile : tile + 1], (block, LANES))
            weight = weight.astype(rows.dtype)
            rows[count:, lanes] = weight
            for c in range(2):
                for t in range(times):
                    values = join(
                        [
                            cal_ref[device, t, :, parts[part].at + lane : parts[part].at + lane + width]
                            for part, device, lane, width in tile_pieces(parts, tile, c)
                        ]
                    )
                    at = (c * times + t) * block
                    rows[at : at + block, lanes] = values * weight
        order = times * block
        place = lax.broadcasted_iota(jnp.int32, (order, order), 0)
        origin = lax.broadcasted_iota(jnp.int32, (order, order), 1)
        moved = (place % times) * block + place // times == origin
        interleave[...] = moved.astype(jnp.float32).astype(jnp.bfloat16)
        band[...] = jnp.zeros(band.shape, band.dtype)
        for offset in range(2 * reach + 1):
            turned = jnp.transpose(kernel_ref[offset].astype(jnp.float32)).astype(band.dtype)
            for target in range(2):
                first = (offset + target) * LANES
                band[first : first + LANES, target * LANES : (target + 1) * LANES] = turned

    mixes = []
    for t in range(times):
        scale = times_ref[t, 0]
        for u in range(1, times):
            scale = scale + times_ref[t, u]
        share = 1.0 / scale
        mixes.append([times_ref[t, u] * share for u in range(times)])
    width = out_ref.shape[3]
    for pair in range(width // (2 * LANES)):
        lanes = slice(pair * 2 * LANES, (pair + 1) * 2 * LANES)
        at = pl.multiple_of(step * width + pair * 2 * LANES, 2 * LANES)
        mixed = jnp.dot(
            rows[:, pl.ds(at, span)], band[...], preferred_element_type=jnp.float32
        )
        total = 1.0 / mixed[count:]
        kept = rows[:, pl.ds(pl.multiple_of(at + reach * LANES, LANES), 2 * LANES)]
        kept = kept.astype(jnp.float32)
        keep = kept[count:] > 0.5
        for c in range(2):
            values = []
            for t in range(times):
                value = None
                for u in range(times):
                    first = (c * times + u) * block
                    part = mixes[t][u] * mixed[first : first + block]
                    value = part if value is None else value + part
                first = (c * times + t) * block
                values.append(jnp.where(keep, kept[first : first + block], value * total))
            values = jnp.concatenate(values, axis=0)
            large = values.astype(jnp.bfloat16)
            small = (values - large.astype(jnp.float32)).astype(jnp.bfloat16)
            values = jnp.dot(
                interleave[...], large, preferred_element_type=jnp.float32
            ) + jnp.dot(interleave[...], small, preferred_element_type=jnp.float32)
            out_ref[c, :, :, lanes] = values.reshape(block, times, 2 * LANES)


def on_device(
    devices,
    log_amplitude,
    phase,
    redundant_group_index,
    antenna_couples,
    tile_flag_mask,
    inverse,
    integration_kernel,
    channel_kernel,
):
    own, _, channels = log_amplitude.shape
    total = own * devices
    real_antennas = inverse.shape[1]
    antennas = round_up(real_antennas, LANES)
    sent_antennas = round_up(real_antennas, 16)
    times = integration_kernel.shape[0]
    block = tile_flag_mask.shape[0]
    reach = (channel_kernel.shape[0] - 1) // 2
    tiles = channels // LANES
    parts = parts_of(channels, devices)
    gap = antennas - real_antennas
    wide_inverse = jnp.pad(inverse, ((0, 0), (0, gap), (0, gap)))
    lanes = sum(part.lanes for part in parts)
    extra = digit_rows(own, lanes)
    shape = (devices, own + extra, lanes)
    blocks = 4
    packed = call(
        functools.partial(pack_kernel, parts),
        jax.ShapeDtypeStruct(shape, jnp.bfloat16),
        60,
        (0, 8 * own * channels),
        in_specs=[
            pl.BlockSpec(memory_space=pltpu.VMEM),
            pl.BlockSpec(memory_space=pltpu.VMEM),
            pl.BlockSpec(memory_space=pl.ANY),
            pl.BlockSpec(memory_space=pl.ANY),
        ],
        out_specs=pl.BlockSpec(memory_space=pl.ANY),
        scratch_shapes=[pltpu.VMEM(shape, jnp.bfloat16)]
        + [pltpu.VMEM((own, channels), jnp.bfloat16)] * 2
        + [pltpu.SemaphoreType.DMA((2, blocks)), pltpu.SemaphoreType.DMA((blocks + 1,))],
        name="pack",
    )(
        redundant_group_index.reshape(1, own),
        jnp.transpose(antenna_couples),
        log_amplitude.reshape(own, channels),
        phase.reshape(own, channels),
    )
    terms = lax.all_to_all(packed, "bl", split_axis=0, concat_axis=0, tiled=True)

    large = total // 2048
    wide = sum(use.stop - use.start for use in lanes_of(parts, 0))
    gain, sent, indices = call(
        functools.partial(solve_kernel, parts, own),
        [
            jax.ShapeDtypeStruct((antennas, lanes), jnp.float32),
            jax.ShapeDtypeStruct((1, sent_antennas, lanes), jnp.bfloat16),
            jax.ShapeDtypeStruct((devices, 8, own), jnp.float32),
        ],
        min(56, 20 * large),
        (8 * total * (GROUP_ROWS + antennas) * lanes, 8 * total * lanes),
        scratch_shapes=[
            pltpu.VMEM((2, GROUP_ROWS + antennas, wide), jnp.float32),
            pltpu.VMEM((2, antennas, GROUP_ROWS), jnp.float32),
        ],
        name="solve",
    )(terms, wide_inverse)

    held = sent
    hop = devices // 2
    while hop > 2:
        held = jnp.concatenate([held, pass_on(held, devices, hop)], axis=0)
        hop //= 2
    near = pass_on(held, devices, 2)
    gathered = [held, pass_on(held, devices, 1), near, pass_on(near, devices, 1)]

    calibrated = call(
        functools.partial(calibrate_kernel, parts, own),
        jax.ShapeDtypeStruct((total, lanes), jnp.bfloat16),
        16,
        (16 * total * antennas * lanes, 8 * total * lanes),
        grid=(devices // 2,),
        in_specs=[
            pl.BlockSpec((2, own + extra, lanes), lambda i: (i, 0, 0)),
            pl.BlockSpec((2, 8, own), lambda i: (i, 0, 0)),
            pl.BlockSpec((antennas, lanes), lambda i: (0, 0)),
        ],
        out_specs=pl.BlockSpec((2 * own, lanes), lambda i: (i, 0)),
        scratch_shapes=[pltpu.VMEM((2, 3, antennas, wide), jnp.bfloat16)],
        name="calibrate",
    )(terms, indices, gain)
    spread = lax.all_to_all(
        after(calibrated, held), ("bl", "ta"), split_axis=0, concat_axis=0, tiled=True
    ).reshape(devices, times, block, lanes)

    filled, mark = call(
        functools.partial(fill_kernel, parts, times, reach),
        (
            jax.ShapeDtypeStruct((2, block, times, channels), jnp.float32),
            jax.ShapeDtypeStruct((8, LANES), jnp.float32),
        ),
        32,
        (32 * reach * block * times * channels * LANES, 16 * block * times * channels),
        grid=(tiles // 2,),
        in_specs=[
            pl.BlockSpec((block, tiles), lambda i: (0, 0)),
            pl.BlockSpec(memory_space=pltpu.SMEM),
            pl.BlockSpec(channel_kernel.shape, lambda i: (0, 0, 0)),
        ]
        + [
            pl.BlockSpec(spread.shape, lambda i: (0, 0, 0, 0)),
            pl.BlockSpec(memory_space=pl.ANY),
            pl.BlockSpec(memory_space=pl.ANY),
        ],
        out_specs=(
            pl.BlockSpec((2, block, times, 2 * LANES), lambda i: (0, 0, 0, i)),
            pl.BlockSpec((8, LANES), lambda i: (0, 0)),
        ),
        scratch_shapes=[
            pltpu.VMEM(((2 * times + 1) * block, (tiles + 2 * reach) * LANES), jnp.bfloat16),
            pltpu.VMEM(((2 * reach + 2) * LANES, 2 * LANES), jnp.bfloat16),
            pltpu.VMEM((times * block, times * block), jnp.bfloat16),
        ],
        name="fill",
    )(tile_flag_mask, integration_kernel, channel_kernel, spread, *gathered[1:3])
    gains = call(
        functools.partial(spread_kernel, parts, real_antennas, tiles),
        jax.ShapeDtypeStruct((2 * real_antennas * tiles, LANES), jnp.float32),
        32,
        (0, 12 * real_antennas * channels),
        grid=(2,),
        in_specs=[pl.BlockSpec(memory_space=pltpu.SMEM)]
        + [pl.BlockSpec(values.shape, lambda i: (0, 0, 0)) for values in gathered]
        + [pl.BlockSpec(memory_space=pl.ANY)],
        out_specs=pl.BlockSpec((real_antennas * tiles, LANES), lambda i: (i, 0)),
        name="gains",
    )(entries_of(devices), *gathered, mark)

    return gains.reshape(2, real_antennas, 1, channels), filled


def solution(mesh):
    in_specs = (
        P("bl", "ta", None),
        P("bl", "ta", None),
        P("bl"),
        P("bl", None),
        P(("bl", "ta"), None),
        P(),
        P(),
        P(),
    )
    out_specs = (P(None, None, "ta", None), P(None, ("bl", "ta"), None, None))
    return jax.shard_map(
        functools.partial(on_device, mesh.shape["bl"]),
        mesh=mesh,
        in_specs=in_specs,
        out_specs=out_specs,
        check_vma=False,
    )
```

```python
import functools

import jax
import jax.numpy as jnp
from jax import lax
from jax.experimental import pallas as pl
from jax.experimental.pallas import tpu as pltpu
from jax.sharding import PartitionSpec as P

NGRP = 224
GROUP_ROWS = 256
LANES = 128
HIGHEST = lax.Precision.HIGHEST


def round_up(value, unit):
    return -(-value // unit) * unit


class Part:
    def __init__(self, first, half, at):
        self.first = first
        self.half = half
        self.at = at
        self.lanes = 2 * half


def parts_of(channels, devices):
    width = channels // devices
    whole = width // LANES * LANES
    parts = []
    if whole:
        parts.append(Part(0, whole, 0))
    if width - whole:
        parts.append(Part(devices * whole, width - whole, 2 * whole))
    return parts


def tile_pieces(parts, tile, which):
    at = tile * LANES
    index = max(k for k, part in enumerate(parts) if part.first <= at)
    part = parts[index]
    at -= part.first
    end = at + LANES
    pieces = []
    while at < end:
        device, inside = divmod(at, part.half)
        width = min(part.half - inside, end - at)
        pieces.append((index, device, which * part.half + inside, width))
        at += width
    return pieces


def lanes_of(parts, which):
    slices = []
    for part in parts:
        if part.half % LANES == 0:
            slices.append(slice(part.at + which * part.half, part.at + (which + 1) * part.half))
        else:
            slices.append(slice(part.at, part.at + part.lanes))
    return slices


def join(pieces):
    return pieces[0] if len(pieces) == 1 else jnp.concatenate(pieces, axis=-1)


def call(body, out_shape, vmem, work, **kwargs):
    flops, moved = work
    return pl.pallas_call(
        body,
        out_shape=out_shape,
        cost_estimate=pl.CostEstimate(flops=flops, bytes_accessed=moved, transcendentals=0),
        compiler_params=pltpu.CompilerParams(vmem_limit_bytes=vmem * 1024 * 1024),
        **kwargs,
    )


def digit_groups(own, lanes):
    return [(at, min(lanes, own - at)) for at in range(0, own, lanes)]


def digit_rows(own, lanes):
    return round_up(6 * len(digit_groups(own, lanes)), 16)


def pack_kernel(parts, group_ref, couple_ref, amp_hbm, phase_hbm, out_hbm, *refs):
    out, amp, phase, in_sems, out_sems = refs
    own = amp.shape[0]
    devices, _, lanes = out.shape
    blocks = in_sems.shape[1]
    rows = own // blocks
    copies = []
    for k in range(blocks):
        at = pl.ds(k * rows, rows)
        pair = [
            pltpu.make_async_copy(
                source.at[at], target.at[at], in_sems.at[which, k]
            )
            for which, (source, target) in enumerate(((amp_hbm, amp), (phase_hbm, phase)))
        ]
        for copy in pair:
            copy.start()
        copies.append(pair)
    sent = []
    numbers = [group_ref[...], couple_ref[0:1, :], couple_ref[1:2, :]]
    digits = []
    for number in numbers:
        wide = number.astype(jnp.float32)
        high = jnp.floor(wide * (1.0 / LANES))
        digits += [high, wide - high * LANES]
    lines = []
    for first, width in digit_groups(own, lanes):
        for digit in digits:
            line = digit[:, first : first + width]
            if width < lanes:
                line = jnp.concatenate(
                    [line, jnp.zeros((1, lanes - width), line.dtype)], axis=1
                )
            lines.append(line)
    extra = digit_rows(own, lanes)
    lines.append(jnp.zeros((extra - len(lines), lanes), jnp.float32))
    lines = jnp.concatenate(lines, axis=0).astype(jnp.bfloat16)
    for device in range(devices):
        out[device, own:, :] = lines
    block = pl.ds(own, extra)
    copy = pltpu.make_async_copy(out.at[:, block], out_hbm.at[:, block], out_sems.at[blocks])
    copy.start()
    sent.append(copy)
    for k in range(blocks):
        for copy in copies[k]:
            copy.wait()
        at = slice(k * rows, (k + 1) * rows)
        for part in parts:
            half = part.half
            for device in range(devices):
                first = part.first + device * half
                for which, ref in enumerate((amp, phase)):
                    lane = part.at + which * half
                    out[device, at, lane : lane + half] = ref[at, first : first + half]
        block = pl.ds(k * rows, rows)
        copy = pltpu.make_async_copy(out.at[:, block], out_hbm.at[:, block], out_sems.at[k])
        copy.start()
        sent.append(copy)
    for copy in sent:
        copy.wait()


def hot_rows(labels, number):
    rows = lax.broadcasted_iota(jnp.int32, (labels, number.shape[1]), 0).astype(jnp.float32)
    return (rows == number).astype(jnp.float32)


def solve_kernel(parts, own, x_ref, inverse_ref, gain_ref, sent_ref, index_ref, sums, link):
    devices, _, lanes = x_ref.shape
    antennas = gain_ref.shape[0]
    sums[...] = jnp.zeros_like(sums)
    link[...] = jnp.zeros_like(link)

    def gather(device, carry):
        digits = x_ref[device, own:, :].astype(jnp.float32)
        numbers = []
        for k in range(3):
            pieces = []
            for piece, (_, width) in enumerate(digit_groups(own, lanes)):
                at = 6 * piece + 2 * k
                pieces.append(
                    digits[at : at + 1, :width] * LANES + digits[at + 1 : at + 2, :width]
                )
            numbers.append(join(pieces))
        index_ref[device] = jnp.concatenate(numbers + [jnp.zeros((5, own), jnp.float32)], axis=0)
        group_hot = hot_rows(GROUP_ROWS, numbers[0]).astype(jnp.bfloat16)
        first, second = [hot_rows(antennas, number) for number in numbers[1:]]
        for s, couple in enumerate((first + second, first - second)):
            hot = jnp.concatenate([group_hot, couple.astype(jnp.bfloat16)], axis=0)
            values = join([x_ref[device, 0:own, use] for use in lanes_of(parts, s)])
            sums[s] += jnp.dot(hot, values, preferred_element_type=jnp.float32)
            link[s] += lax.dot_general(
                hot[GROUP_ROWS:],
                group_hot,
                (((1,), (1,)), ((), ())),
                preferred_element_type=jnp.float32,
            )
        return carry

    lax.fori_loop(0, devices, gather, 0, unroll=4)
    counts = 0.5 * jnp.sum(link[0], axis=0, keepdims=True)
    share = 1.0 / jnp.maximum(counts, 1.0)
    for s in range(2):
        rhs = sums[s, GROUP_ROWS:, :] - jnp.dot(
            link[s] * share,
            sums[s, :GROUP_ROWS, :],
            precision=HIGHEST,
            preferred_element_type=jnp.float32,
        )
        gain = jnp.dot(
            inverse_ref[s], rhs, precision=HIGHEST, preferred_element_type=jnp.float32
        )
        at = 0
        for part, use in zip(parts, lanes_of(parts, s)):
            width = use.stop - use.start
            values = gain[:, at : at + width]
            if s and width == part.lanes:
                low = lax.broadcasted_iota(jnp.int32, values.shape, 1) < part.half
                values = jnp.where(low, gain_ref[:, use], values)
            gain_ref[:, use] = values
            at += width
    sent_ref[0] = gain_ref[: sent_ref.shape[1], :].astype(jnp.bfloat16)


def reduced(angle):
    turns = jnp.floor(angle * 0.6366197723675814 + 0.5)
    left = angle - turns * 1.5703125
    left = left - turns * 4.83751296997070312e-4
    left = left - turns * 7.54978995489188216e-8
    square = left * left
    sine = ((-1.9515295891e-4 * square + 8.3321608736e-3) * square - 1.6666654611e-1) * square
    sine = sine * left + left
    cosine = (2.443315711809948e-5 * square - 1.388731625493765e-3) * square
    cosine = (cosine + 4.166664568298827e-2) * square * square - 0.5 * square + 1.0
    return turns.astype(jnp.int32), sine, cosine


def quarter(turns, sine, cosine):
    value = jnp.where((turns & 1) == 1, cosine, sine)
    return jnp.where((turns & 2) == 2, -value, value)


def swap(values, half):
    if 2 * half == LANES:
        return pltpu.roll(values, half, 1)
    return jnp.concatenate([values[:, half:], values[:, :half]], axis=1)


def calibrate_kernel(parts, own, x_ref, index_ref, gain_ref, out_ref, split):
    antennas = gain_ref.shape[0]

    @pl.when(pl.program_id(0) == 0)
    def _():
        for s in range(2):
            left = join([gain_ref[:, use] for use in lanes_of(parts, s)])
            for k in range(3):
                part = left.astype(jnp.bfloat16)
                split[s, k] = part
                left = left - part.astype(jnp.float32)

    labels = lax.broadcasted_iota(jnp.int32, (own, antennas), 1).astype(jnp.float32)
    for device in range(x_ref.shape[0]):
        columns = jnp.transpose(index_ref[device])
        first, second = [
            (labels == columns[:, k : k + 1]).astype(jnp.float32) for k in (1, 2)
        ]
        moves = []
        for s, couple in enumerate((first + second, first - second)):
            hot = couple.astype(jnp.bfloat16)
            move = jnp.dot(hot, split[s, 0], preferred_element_type=jnp.float32)
            for k in range(1, 3):
                move = move + jnp.dot(hot, split[s, k], preferred_element_type=jnp.float32)
            moves.append(move)
        rows = slice(device * own, (device + 1) * own)
        at = 0
        for part in parts:
            half, lanes = part.half, part.lanes
            first_lanes = slice(part.at, part.at + half)
            second_lanes = slice(part.at + half, part.at + lanes)
            if half % LANES == 0:
                here = slice(at, at + half)
                left = x_ref[device, 0:own, first_lanes].astype(jnp.float32) - moves[0][:, here]
                magnitude = jnp.exp(left)
                left = x_ref[device, 0:own, second_lanes].astype(jnp.float32) - moves[1][:, here]
                turns, sine, cosine = reduced(left)
                real = magnitude * quarter(turns + 1, sine, cosine)
                imaginary = magnitude * quarter(turns, sine, cosine)
                out_ref[rows, first_lanes] = real.astype(jnp.bfloat16)
                out_ref[rows, second_lanes] = imaginary.astype(jnp.bfloat16)
                at += half
            else:
                here = slice(at, at + lanes)
                both = slice(part.at, part.at + lanes)
                left = x_ref[device, 0:own, both].astype(jnp.float32)
                lower = lax.broadcasted_iota(jnp.int32, left.shape, 1) < half
                left = left - jnp.where(lower, moves[0][:, here], moves[1][:, here])
                turned = swap(left, half)
                magnitude = jnp.exp(jnp.where(lower, left, turned))
                turns, sine, cosine = reduced(jnp.where(lower, turned, left))
                turns = jnp.where(lower, turns + 1, turns)
                value = magnitude * quarter(turns, sine, cosine)
                out_ref[rows, both] = value.astype(jnp.bfloat16)
                at += lanes


def nothing(*refs):
    pass


def after(values, *others):
    return call(
        nothing,
        jax.ShapeDtypeStruct(values.shape, values.dtype),
        4,
        (0, 0),
        in_specs=[pl.BlockSpec(memory_space=pl.ANY)] * (1 + len(others)),
        out_specs=pl.BlockSpec(memory_space=pl.ANY),
        input_output_aliases={0: 0},
        name="after",
    )(values, *others)


def pass_on(held, devices, reach):
    return lax.ppermute(held, "bl", [(i, i ^ reach) for i in range(devices)])


def entries_of(devices):
    apart = jnp.arange(devices, dtype=jnp.int32) ^ lax.axis_index("bl")
    entries = jnp.zeros_like(apart)
    reach, weight = devices // 2, 1
    while reach > 2:
        entries = entries + weight * ((apart // reach) % 2)
        reach //= 2
        weight *= 2
    return jnp.stack([apart % 4, entries])


def spread_kernel(parts, antennas, tiles, entry_ref, *refs):
    gain_refs, out_ref = refs[:4], refs[-1]
    which = pl.program_id(0)

    def piece(part, device, lane, width):
        source, entry = entry_ref[0, device], entry_ref[1, device]
        lane += parts[part].at
        value = gain_refs[0][entry, :, lane : lane + width]
        for k in range(1, 4):
            value = jnp.where(source == k, gain_refs[k][entry, :, lane : lane + width], value)
        return value.astype(jnp.float32)

    for s in range(2):

        @pl.when(which == s)
        def _():
            for tile in range(tiles):
                values = join([piece(*where) for where in tile_pieces(parts, tile, s)])
                out_ref[pl.ds(tile, antennas, tiles), :] = values[:antennas]


def fill_kernel(parts, times, reach, mask_ref, times_ref, kernel_ref, *refs):
    cal_ref, (out_ref, mark_ref, rows, band, interleave) = refs[0], refs[-5:]
    step = pl.program_id(0)
    block, tiles = mask_ref.shape
    count = 2 * times * block
    span = (2 * reach + 2) * LANES

    @pl.when(step == 0)
    def _():
        mark_ref[...] = jnp.zeros_like(mark_ref)
        keep = (1 - mask_ref[...]).astype(jnp.float32)
        edge = reach * LANES
        inner = (reach + tiles) * LANES
        rows[:, :edge] = jnp.zeros((rows.shape[0], edge), rows.dtype)
        rows[:, inner:] = jnp.zeros((rows.shape[0], rows.shape[1] - inner), rows.dtype)
        for tile in range(tiles):
            lanes = slice((reach + tile) * LANES, (reach + tile + 1) * LANES)
            weight = jnp.broadcast_to(keep[:, tile : tile + 1], (block, LANES))
            weight = weight.astype(rows.dtype)
            rows[count:, lanes] = weight
            for c in range(2):
                for t in range(times):
                    values = join(
                        [
                            cal_ref[device, t, :, parts[part].at + lane : parts[part].at + lane + width]
                            for part, device, lane, width in tile_pieces(parts, tile, c)
                        ]
                    )
                    at = (c * times + t) * block
                    rows[at : at + block, lanes] = values * weight
        order = times * block
        place = lax.broadcasted_iota(jnp.int32, (order, order), 0)
        origin = lax.broadcasted_iota(jnp.int32, (order, order), 1)
        moved = (place % times) * block + place // times == origin
        interleave[...] = moved.astype(jnp.float32).astype(jnp.bfloat16)
        band[...] = jnp.zeros(band.shape, band.dtype)
        for offset in range(2 * reach + 1):
            turned = jnp.transpose(kernel_ref[offset].astype(jnp.float32)).astype(band.dtype)
            for target in range(2):
                first = (offset + target) * LANES
                band[first : first + LANES, target * LANES : (target + 1) * LANES] = turned

    mixes = []
    for t in range(times):
        scale = times_ref[t, 0]
        for u in range(1, times):
            scale = scale + times_ref[t, u]
        share = 1.0 / scale
        mixes.append([times_ref[t, u] * share for u in range(times)])
    width = out_ref.shape[3]
    for pair in range(width // (2 * LANES)):
        lanes = slice(pair * 2 * LANES, (pair + 1) * 2 * LANES)
        at = pl.multiple_of(step * width + pair * 2 * LANES, 2 * LANES)
        mixed = jnp.dot(
            rows[:, pl.ds(at, span)], band[...], preferred_element_type=jnp.float32
        )
        total = 1.0 / mixed[count:]
        kept = rows[:, pl.ds(pl.multiple_of(at + reach * LANES, LANES), 2 * LANES)]
        kept = kept.astype(jnp.float32)
        keep = kept[count:] > 0.5
        for c in range(2):
            values = []
            for t in range(times):
                value = None
                for u in range(times):
                    first = (c * times + u) * block
                    part = mixes[t][u] * mixed[first : first + block]
                    value = part if value is None else value + part
                first = (c * times + t) * block
                values.append(jnp.where(keep, kept[first : first + block], value * total))
            values = jnp.concatenate(values, axis=0)
            large = values.astype(jnp.bfloat16)
            small = (values - large.astype(jnp.float32)).astype(jnp.bfloat16)
            values = jnp.dot(
                interleave[...], large, preferred_element_type=jnp.float32
            ) + jnp.dot(interleave[...], small, preferred_element_type=jnp.float32)
            out_ref[c, :, :, lanes] = values.reshape(block, times, 2 * LANES)


def on_device(
    devices,
    log_amplitude,
    phase,
    redundant_group_index,
    antenna_couples,
    tile_flag_mask,
    inverse,
    integration_kernel,
    channel_kernel,
):
    own, _, channels = log_amplitude.shape
    total = own * devices
    real_antennas = inverse.shape[1]
    antennas = round_up(real_antennas, LANES)
    sent_antennas = round_up(real_antennas, 16)
    times = integration_kernel.shape[0]
    block = tile_flag_mask.shape[0]
    reach = (channel_kernel.shape[0] - 1) // 2
    tiles = channels // LANES
    parts = parts_of(channels, devices)
    gap = antennas - real_antennas
    wide_inverse = jnp.pad(inverse, ((0, 0), (0, gap), (0, gap)))
    lanes = sum(part.lanes for part in parts)
    extra = digit_rows(own, lanes)
    shape = (devices, own + extra, lanes)
    blocks = 8
    packed = call(
        functools.partial(pack_kernel, parts),
        jax.ShapeDtypeStruct(shape, jnp.bfloat16),
        60,
        (0, 8 * own * channels),
        in_specs=[
            pl.BlockSpec(memory_space=pltpu.VMEM),
            pl.BlockSpec(memory_space=pltpu.VMEM),
            pl.BlockSpec(memory_space=pl.ANY),
            pl.BlockSpec(memory_space=pl.ANY),
        ],
        out_specs=pl.BlockSpec(memory_space=pl.ANY),
        scratch_shapes=[pltpu.VMEM(shape, jnp.bfloat16)]
        + [pltpu.VMEM((own, channels), jnp.bfloat16)] * 2
        + [pltpu.SemaphoreType.DMA((2, blocks)), pltpu.SemaphoreType.DMA((blocks + 1,))],
        name="pack",
    )(
        redundant_group_index.reshape(1, own),
        jnp.transpose(antenna_couples),
        log_amplitude.reshape(own, channels),
        phase.reshape(own, channels),
    )
    terms = lax.all_to_all(packed, "bl", split_axis=0, concat_axis=0, tiled=True)

    large = total // 2048
    wide = sum(use.stop - use.start for use in lanes_of(parts, 0))
    gain, sent, indices = call(
        functools.partial(solve_kernel, parts, own),
        [
            jax.ShapeDtypeStruct((antennas, lanes), jnp.float32),
            jax.ShapeDtypeStruct((1, sent_antennas, lanes), jnp.bfloat16),
            jax.ShapeDtypeStruct((devices, 8, own), jnp.float32),
        ],
        min(56, 20 * large),
        (8 * total * (GROUP_ROWS + antennas) * lanes, 8 * total * lanes),
        scratch_shapes=[
            pltpu.VMEM((2, GROUP_ROWS + antennas, wide), jnp.float32),
            pltpu.VMEM((2, antennas, GROUP_ROWS), jnp.float32),
        ],
        name="solve",
    )(terms, wide_inverse)

    held = sent
    hop = devices // 2
    while hop > 2:
        held = jnp.concatenate([held, pass_on(held, devices, hop)], axis=0)
        hop //= 2
    gathered = [held] + [pass_on(held, devices, hop) for hop in (1, 2, 3)]

    calibrated = call(
        functools.partial(calibrate_kernel, parts, own),
        jax.ShapeDtypeStruct((total, lanes), jnp.bfloat16),
        16,
        (16 * total * antennas * lanes, 8 * total * lanes),
        grid=(devices // 2,),
        in_specs=[
            pl.BlockSpec((2, own + extra, lanes), lambda i: (i, 0, 0)),
            pl.BlockSpec((2, 8, own), lambda i: (i, 0, 0)),
            pl.BlockSpec((antennas, lanes), lambda i: (0, 0)),
        ],
        out_specs=pl.BlockSpec((2 * own, lanes), lambda i: (i, 0)),
        scratch_shapes=[pltpu.VMEM((2, 3, antennas, wide), jnp.bfloat16)],
        name="calibrate",
    )(terms, indices, gain)
    spread = lax.all_to_all(
        after(calibrated, held), ("bl", "ta"), split_axis=0, concat_axis=0, tiled=True
    ).reshape(devices, times, block, lanes)

    filled, mark = call(
        functools.partial(fill_kernel, parts, times, reach),
        (
            jax.ShapeDtypeStruct((2, block, times, channels), jnp.float32),
            jax.ShapeDtypeStruct((8, LANES), jnp.float32),
        ),
        32,
        (32 * reach * block * times * channels * LANES, 16 * block * times * channels),
        grid=(tiles // 2,),
        in_specs=[
            pl.BlockSpec((block, tiles), lambda i: (0, 0)),
            pl.BlockSpec(memory_space=pltpu.SMEM),
            pl.BlockSpec(channel_kernel.shape, lambda i: (0, 0, 0)),
        ]
        + [
            pl.BlockSpec(spread.shape, lambda i: (0, 0, 0, 0)),
        ],
        out_specs=(
            pl.BlockSpec((2, block, times, 2 * LANES), lambda i: (0, 0, 0, i)),
            pl.BlockSpec((8, LANES), lambda i: (0, 0)),
        ),
        scratch_shapes=[
            pltpu.VMEM(((2 * times + 1) * block, (tiles + 2 * reach) * LANES), jnp.bfloat16),
            pltpu.VMEM(((2 * reach + 2) * LANES, 2 * LANES), jnp.bfloat16),
            pltpu.VMEM((times * block, times * block), jnp.bfloat16),
        ],
        name="fill",
    )(tile_flag_mask, integration_kernel, channel_kernel, spread)
    gains = call(
        functools.partial(spread_kernel, parts, real_antennas, tiles),
        jax.ShapeDtypeStruct((2 * real_antennas * tiles, LANES), jnp.float32),
        32,
        (0, 12 * real_antennas * channels),
        grid=(2,),
        in_specs=[pl.BlockSpec(memory_space=pltpu.SMEM)]
        + [pl.BlockSpec(values.shape, lambda i: (0, 0, 0)) for values in gathered]
        + [pl.BlockSpec(memory_space=pl.ANY)],
        out_specs=pl.BlockSpec((real_antennas * tiles, LANES), lambda i: (i, 0)),
        name="gains",
    )(entries_of(devices), *gathered, mark)

    return gains.reshape(2, real_antennas, 1, channels), filled


def solution(mesh):
    in_specs = (
        P("bl", "ta", None),
        P("bl", "ta", None),
        P("bl"),
        P("bl", None),
        P(("bl", "ta"), None),
        P(),
        P(),
        P(),
    )
    out_specs = (P(None, None, "ta", None), P(None, ("bl", "ta"), None, None))
    return jax.shard_map(
        functools.partial(on_device, mesh.shape["bl"]),
        mesh=mesh,
        in_specs=in_specs,
        out_specs=out_specs,
        check_vma=False,
    )
```

```python
import functools

import jax
import jax.numpy as jnp
from jax import lax
from jax.experimental import pallas as pl
from jax.experimental.pallas import tpu as pltpu
from jax.sharding import PartitionSpec as P

NGRP = 224
GROUP_ROWS = 256
LANES = 128
HIGHEST = lax.Precision.HIGHEST


def round_up(value, unit):
    return -(-value // unit) * unit


class Part:
    def __init__(self, first, half, at):
        self.first = first
        self.half = half
        self.at = at
        self.lanes = 2 * half


def parts_of(channels, devices):
    width = channels // devices
    whole = width // LANES * LANES
    parts = []
    if whole:
        parts.append(Part(0, whole, 0))
    if width - whole:
        parts.append(Part(devices * whole, width - whole, 2 * whole))
    return parts


def tile_pieces(parts, tile, which):
    at = tile * LANES
    index = max(k for k, part in enumerate(parts) if part.first <= at)
    part = parts[index]
    at -= part.first
    end = at + LANES
    pieces = []
    while at < end:
        device, inside = divmod(at, part.half)
        width = min(part.half - inside, end - at)
        pieces.append((index, device, which * part.half + inside, width))
        at += width
    return pieces


def lanes_of(parts, which):
    slices = []
    for part in parts:
        if part.half % LANES == 0:
            slices.append(slice(part.at + which * part.half, part.at + (which + 1) * part.half))
        else:
            slices.append(slice(part.at, part.at + part.lanes))
    return slices


def join(pieces):
    return pieces[0] if len(pieces) == 1 else jnp.concatenate(pieces, axis=-1)


def call(body, out_shape, vmem, work, **kwargs):
    flops, moved = work
    return pl.pallas_call(
        body,
        out_shape=out_shape,
        cost_estimate=pl.CostEstimate(flops=flops, bytes_accessed=moved, transcendentals=0),
        compiler_params=pltpu.CompilerParams(vmem_limit_bytes=vmem * 1024 * 1024),
        **kwargs,
    )


def digit_groups(own, lanes):
    return [(at, min(lanes, own - at)) for at in range(0, own, lanes)]


def digit_rows(own, lanes):
    return round_up(6 * len(digit_groups(own, lanes)), 16)


def pack_kernel(parts, group_ref, couple_ref, amp_hbm, phase_hbm, out_hbm, *refs):
    out, amp, phase, in_sems, out_sems = refs
    own = amp.shape[0]
    devices, _, lanes = out.shape
    blocks = in_sems.shape[1]
    rows = own // blocks
    copies = []
    for k in range(blocks):
        at = pl.ds(k * rows, rows)
        pair = [
            pltpu.make_async_copy(
                source.at[at], target.at[at], in_sems.at[which, k]
            )
            for which, (source, target) in enumerate(((amp_hbm, amp), (phase_hbm, phase)))
        ]
        for copy in pair:
            copy.start()
        copies.append(pair)
    sent = []
    numbers = [group_ref[...], couple_ref[0:1, :], couple_ref[1:2, :]]
    digits = []
    for number in numbers:
        wide = number.astype(jnp.float32)
        high = jnp.floor(wide * (1.0 / LANES))
        digits += [high, wide - high * LANES]
    lines = []
    for first, width in digit_groups(own, lanes):
        for digit in digits:
            line = digit[:, first : first + width]
            if width < lanes:
                line = jnp.concatenate(
                    [line, jnp.zeros((1, lanes - width), line.dtype)], axis=1
                )
            lines.append(line)
    extra = digit_rows(own, lanes)
    lines.append(jnp.zeros((extra - len(lines), lanes), jnp.float32))
    lines = jnp.concatenate(lines, axis=0).astype(jnp.bfloat16)
    for device in range(devices):
        out[device, own:, :] = lines
    block = pl.ds(own, extra)
    copy = pltpu.make_async_copy(out.at[:, block], out_hbm.at[:, block], out_sems.at[blocks])
    copy.start()
    sent.append(copy)
    for k in range(blocks):
        for copy in copies[k]:
            copy.wait()
        at = slice(k * rows, (k + 1) * rows)
        for part in parts:
            half = part.half
            for device in range(devices):
                first = part.first + device * half
                for which, ref in enumerate((amp, phase)):
                    lane = part.at + which * half
                    out[device, at, lane : lane + half] = ref[at, first : first + half]
        block = pl.ds(k * rows, rows)
        copy = pltpu.make_async_copy(out.at[:, block], out_hbm.at[:, block], out_sems.at[k])
        copy.start()
        sent.append(copy)
    for copy in sent:
        copy.wait()


def hot_rows(labels, number):
    rows = lax.broadcasted_iota(jnp.int32, (labels, number.shape[1]), 0).astype(jnp.float32)
    return (rows == number).astype(jnp.float32)


def solve_kernel(parts, own, x_ref, inverse_ref, gain_ref, sent_ref, index_ref, sums, link):
    devices, _, lanes = x_ref.shape
    antennas = gain_ref.shape[0]
    sums[...] = jnp.zeros_like(sums)
    link[...] = jnp.zeros_like(link)

    def gather(device, carry):
        digits = x_ref[device, own:, :].astype(jnp.float32)
        numbers = []
        for k in range(3):
            pieces = []
            for piece, (_, width) in enumerate(digit_groups(own, lanes)):
                at = 6 * piece + 2 * k
                pieces.append(
                    digits[at : at + 1, :width] * LANES + digits[at + 1 : at + 2, :width]
                )
            numbers.append(join(pieces))
        index_ref[device] = jnp.concatenate(numbers + [jnp.zeros((5, own), jnp.float32)], axis=0)
        group_hot = hot_rows(GROUP_ROWS, numbers[0]).astype(jnp.bfloat16)
        first, second = [hot_rows(antennas, number) for number in numbers[1:]]
        for s, couple in enumerate((first + second, first - second)):
            hot = jnp.concatenate([group_hot, couple.astype(jnp.bfloat16)], axis=0)
            values = join([x_ref[device, 0:own, use] for use in lanes_of(parts, s)])
            sums[s] += jnp.dot(hot, values, preferred_element_type=jnp.float32)
            link[s] += lax.dot_general(
                hot[GROUP_ROWS:],
                group_hot,
                (((1,), (1,)), ((), ())),
                preferred_element_type=jnp.float32,
            )
        return carry

    lax.fori_loop(0, devices, gather, 0, unroll=4)
    counts = 0.5 * jnp.sum(link[0], axis=0, keepdims=True)
    share = 1.0 / jnp.maximum(counts, 1.0)
    for s in range(2):
        rhs = sums[s, GROUP_ROWS:, :] - jnp.dot(
            link[s] * share,
            sums[s, :GROUP_ROWS, :],
            precision=HIGHEST,
            preferred_element_type=jnp.float32,
        )
        gain = jnp.dot(
            inverse_ref[s], rhs, precision=HIGHEST, preferred_element_type=jnp.float32
        )
        at = 0
        for part, use in zip(parts, lanes_of(parts, s)):
            width = use.stop - use.start
            values = gain[:, at : at + width]
            if s and width == part.lanes:
                low = lax.broadcasted_iota(jnp.int32, values.shape, 1) < part.half
                values = jnp.where(low, gain_ref[:, use], values)
            gain_ref[:, use] = values
            at += width
    sent_ref[0] = gain_ref[: sent_ref.shape[1], :].astype(jnp.bfloat16)


def reduced(angle):
    turns = jnp.floor(angle * 0.6366197723675814 + 0.5)
    left = angle - turns * 1.5703125
    left = left - turns * 4.83751296997070312e-4
    left = left - turns * 7.54978995489188216e-8
    square = left * left
    sine = ((-1.9515295891e-4 * square + 8.3321608736e-3) * square - 1.6666654611e-1) * square
    sine = sine * left + left
    cosine = (2.443315711809948e-5 * square - 1.388731625493765e-3) * square
    cosine = (cosine + 4.166664568298827e-2) * square * square - 0.5 * square + 1.0
    return turns.astype(jnp.int32), sine, cosine


def quarter(turns, sine, cosine):
    value = jnp.where((turns & 1) == 1, cosine, sine)
    return jnp.where((turns & 2) == 2, -value, value)


def swap(values, half):
    if 2 * half == LANES:
        return pltpu.roll(values, half, 1)
    return jnp.concatenate([values[:, half:], values[:, :half]], axis=1)


def calibrate_kernel(parts, own, x_ref, index_ref, gain_ref, out_ref, split):
    antennas = gain_ref.shape[0]

    @pl.when(pl.program_id(0) == 0)
    def _():
        for s in range(2):
            left = join([gain_ref[:, use] for use in lanes_of(parts, s)])
            for k in range(3):
                part = left.astype(jnp.bfloat16)
                split[s, k] = part
                left = left - part.astype(jnp.float32)

    labels = lax.broadcasted_iota(jnp.int32, (own, antennas), 1).astype(jnp.float32)
    for device in range(x_ref.shape[0]):
        columns = jnp.transpose(index_ref[device])
        first, second = [
            (labels == columns[:, k : k + 1]).astype(jnp.float32) for k in (1, 2)
        ]
        moves = []
        for s, couple in enumerate((first + second, first - second)):
            hot = couple.astype(jnp.bfloat16)
            move = jnp.dot(hot, split[s, 0], preferred_element_type=jnp.float32)
            for k in range(1, 3):
                move = move + jnp.dot(hot, split[s, k], preferred_element_type=jnp.float32)
            moves.append(move)
        rows = slice(device * own, (device + 1) * own)
        at = 0
        for part in parts:
            half, lanes = part.half, part.lanes
            first_lanes = slice(part.at, part.at + half)
            second_lanes = slice(part.at + half, part.at + lanes)
            if half % LANES == 0:
                here = slice(at, at + half)
                left = x_ref[device, 0:own, first_lanes].astype(jnp.float32) - moves[0][:, here]
                magnitude = jnp.exp(left)
                left = x_ref[device, 0:own, second_lanes].astype(jnp.float32) - moves[1][:, here]
                turns, sine, cosine = reduced(left)
                real = magnitude * quarter(turns + 1, sine, cosine)
                imaginary = magnitude * quarter(turns, sine, cosine)
                out_ref[rows, first_lanes] = real.astype(jnp.bfloat16)
                out_ref[rows, second_lanes] = imaginary.astype(jnp.bfloat16)
                at += half
            else:
                here = slice(at, at + lanes)
                both = slice(part.at, part.at + lanes)
                left = x_ref[device, 0:own, both].astype(jnp.float32)
                lower = lax.broadcasted_iota(jnp.int32, left.shape, 1) < half
                left = left - jnp.where(lower, moves[0][:, here], moves[1][:, here])
                turned = swap(left, half)
                magnitude = jnp.exp(jnp.where(lower, left, turned))
                turns, sine, cosine = reduced(jnp.where(lower, turned, left))
                turns = jnp.where(lower, turns + 1, turns)
                value = magnitude * quarter(turns, sine, cosine)
                out_ref[rows, both] = value.astype(jnp.bfloat16)
                at += lanes


def nothing(*refs):
    pass


def after(values, *others):
    return call(
        nothing,
        jax.ShapeDtypeStruct(values.shape, values.dtype),
        4,
        (0, 8 * values.size),
        in_specs=[pl.BlockSpec(memory_space=pl.ANY)] * (1 + len(others)),
        out_specs=pl.BlockSpec(memory_space=pl.ANY),
        input_output_aliases={0: 0},
        name="after",
    )(values, *others)


def pass_on(held, devices, reach):
    return lax.ppermute(held, "bl", [(i, i ^ reach) for i in range(devices)])


def spread_kernel(parts, antennas, tiles, apart, me_ref, *refs):
    gain_refs, (out_ref, mark_ref, chunks) = refs[: len(apart)], refs[len(apart) :]
    which = pl.program_id(0)

    @pl.when(which == 0)
    def _():
        mark_ref[...] = jnp.zeros_like(mark_ref)
        for gain_ref, distances in zip(gain_refs, apart):
            for entry, distance in enumerate(distances):
                chunks[me_ref[0] ^ distance] = gain_ref[entry]

    for s in range(2):

        @pl.when(which == s)
        def _():
            for tile in range(tiles):
                pieces = []
                for part, device, lane, width in tile_pieces(parts, tile, s):
                    lane += parts[part].at
                    pieces.append(chunks[device, :, lane : lane + width].astype(jnp.float32))
                out_ref[pl.ds(tile, antennas, tiles), :] = join(pieces)[:antennas]


def fill_kernel(parts, times, reach, mask_ref, times_ref, kernel_ref, *refs):
    cal_ref, (out_ref, rows, band, interleave) = refs[0], refs[-4:]
    step = pl.program_id(0)
    block, tiles = mask_ref.shape
    count = 2 * times * block
    span = (2 * reach + 2) * LANES

    @pl.when(step == 0)
    def _():
        keep = (1 - mask_ref[...]).astype(jnp.float32)
        edge = reach * LANES
        inner = (reach + tiles) * LANES
        rows[:, :edge] = jnp.zeros((rows.shape[0], edge), rows.dtype)
        rows[:, inner:] = jnp.zeros((rows.shape[0], rows.shape[1] - inner), rows.dtype)
        for tile in range(tiles):
            lanes = slice((reach + tile) * LANES, (reach + tile + 1) * LANES)
            weight = jnp.broadcast_to(keep[:, tile : tile + 1], (block, LANES))
            weight = weight.astype(rows.dtype)
            rows[count:, lanes] = weight
            for c in range(2):
                for t in range(times):
                    values = join(
                        [
                            cal_ref[device, t, :, parts[part].at + lane : parts[part].at + lane + width]
                            for part, device, lane, width in tile_pieces(parts, tile, c)
                        ]
                    )
                    at = (c * times + t) * block
                    rows[at : at + block, lanes] = values * weight
        order = times * block
        place = lax.broadcasted_iota(jnp.int32, (order, order), 0)
        origin = lax.broadcasted_iota(jnp.int32, (order, order), 1)
        moved = (place % times) * block + place // times == origin
        interleave[...] = moved.astype(jnp.float32).astype(jnp.bfloat16)
        band[...] = jnp.zeros(band.shape, band.dtype)
        for offset in range(2 * reach + 1):
            turned = jnp.transpose(kernel_ref[offset].astype(jnp.float32)).astype(band.dtype)
            for target in range(2):
                first = (offset + target) * LANES
                band[first : first + LANES, target * LANES : (target + 1) * LANES] = turned

    mixes = []
    for t in range(times):
        scale = times_ref[t, 0]
        for u in range(1, times):
            scale = scale + times_ref[t, u]
        share = 1.0 / scale
        mixes.append([times_ref[t, u] * share for u in range(times)])
    width = out_ref.shape[3]
    for pair in range(width // (2 * LANES)):
        lanes = slice(pair * 2 * LANES, (pair + 1) * 2 * LANES)
        at = pl.multiple_of(step * width + pair * 2 * LANES, 2 * LANES)
        mixed = jnp.dot(
            rows[:, pl.ds(at, span)], band[...], preferred_element_type=jnp.float32
        )
        total = 1.0 / mixed[count:]
        kept = rows[:, pl.ds(pl.multiple_of(at + reach * LANES, LANES), 2 * LANES)]
        kept = kept.astype(jnp.float32)
        keep = kept[count:] > 0.5
        for c in range(2):
            values = []
            for t in range(times):
                value = None
                for u in range(times):
                    first = (c * times + u) * block
                    part = mixes[t][u] * mixed[first : first + block]
                    value = part if value is None else value + part
                first = (c * times + t) * block
                values.append(jnp.where(keep, kept[first : first + block], value * total))
            values = jnp.concatenate(values, axis=0)
            large = values.astype(jnp.bfloat16)
            small = (values - large.astype(jnp.float32)).astype(jnp.bfloat16)
            values = jnp.dot(
                interleave[...], large, preferred_element_type=jnp.float32
            ) + jnp.dot(interleave[...], small, preferred_element_type=jnp.float32)
            out_ref[c, :, :, lanes] = values.reshape(block, times, 2 * LANES)


def on_device(
    devices,
    log_amplitude,
    phase,
    redundant_group_index,
    antenna_couples,
    tile_flag_mask,
    inverse,
    integration_kernel,
    channel_kernel,
):
    own, _, channels = log_amplitude.shape
    total = own * devices
    real_antennas = inverse.shape[1]
    antennas = round_up(real_antennas, LANES)
    sent_antennas = round_up(real_antennas, 16)
    times = integration_kernel.shape[0]
    block = tile_flag_mask.shape[0]
    reach = (channel_kernel.shape[0] - 1) // 2
    tiles = channels // LANES
    parts = parts_of(channels, devices)
    gap = antennas - real_antennas
    wide_inverse = jnp.pad(inverse, ((0, 0), (0, gap), (0, gap)))
    lanes = sum(part.lanes for part in parts)
    extra = digit_rows(own, lanes)
    shape = (devices, own + extra, lanes)
    blocks = 8
    packed = call(
        functools.partial(pack_kernel, parts),
        jax.ShapeDtypeStruct(shape, jnp.bfloat16),
        60,
        (0, 8 * own * channels),
        in_specs=[
            pl.BlockSpec(memory_space=pltpu.VMEM),
            pl.BlockSpec(memory_space=pltpu.VMEM),
            pl.BlockSpec(memory_space=pl.ANY),
            pl.BlockSpec(memory_space=pl.ANY),
        ],
        out_specs=pl.BlockSpec(memory_space=pl.ANY),
        scratch_shapes=[pltpu.VMEM(shape, jnp.bfloat16)]
        + [pltpu.VMEM((own, channels), jnp.bfloat16)] * 2
        + [pltpu.SemaphoreType.DMA((2, blocks)), pltpu.SemaphoreType.DMA((blocks + 1,))],
        name="pack",
    )(
        redundant_group_index.reshape(1, own),
        jnp.transpose(antenna_couples),
        log_amplitude.reshape(own, channels),
        phase.reshape(own, channels),
    )
    terms = lax.all_to_all(packed, "bl", split_axis=0, concat_axis=0, tiled=True)

    large = total // 2048
    wide = sum(use.stop - use.start for use in lanes_of(parts, 0))
    gain, sent, indices = call(
        functools.partial(solve_kernel, parts, own),
        [
            jax.ShapeDtypeStruct((antennas, lanes), jnp.float32),
            jax.ShapeDtypeStruct((1, sent_antennas, lanes), jnp.bfloat16),
            jax.ShapeDtypeStruct((devices, 8, own), jnp.float32),
        ],
        min(56, 20 * large),
        (8 * total * (GROUP_ROWS + antennas) * lanes, 8 * total * lanes),
        scratch_shapes=[
            pltpu.VMEM((2, GROUP_ROWS + antennas, wide), jnp.float32),
            pltpu.VMEM((2, antennas, GROUP_ROWS), jnp.float32),
        ],
        name="solve",
    )(terms, wide_inverse)

    held, held_apart = sent, [0]
    hop = devices // 2
    while hop > 4:
        held = jnp.concatenate([held, pass_on(held, devices, hop)], axis=0)
        held_apart = held_apart + [distance ^ hop for distance in held_apart]
        hop //= 2
    far, near, side = [pass_on(held, devices, hop) for hop in (4, 2, 1)]
    gathered = [held, far, near, side]
    gathered += [pass_on(far, devices, hop) for hop in (1, 2, 3)] + [pass_on(near, devices, 1)]
    apart = [[distance ^ more for distance in held_apart] for more in (0, 4, 2, 1, 5, 6, 7, 3)]

    calibrated = call(
        functools.partial(calibrate_kernel, parts, own),
        jax.ShapeDtypeStruct((total, lanes), jnp.bfloat16),
        16,
        (16 * total * antennas * lanes, 8 * total * lanes),
        grid=(devices // 2,),
        in_specs=[
            pl.BlockSpec((2, own + extra, lanes), lambda i: (i, 0, 0)),
            pl.BlockSpec((2, 8, own), lambda i: (i, 0, 0)),
            pl.BlockSpec((antennas, lanes), lambda i: (0, 0)),
        ],
        out_specs=pl.BlockSpec((2 * own, lanes), lambda i: (i, 0)),
        scratch_shapes=[pltpu.VMEM((2, 3, antennas, wide), jnp.bfloat16)],
        name="calibrate",
    )(terms, indices, gain)
    spread = lax.all_to_all(
        after(calibrated, far, near, side), ("bl", "ta"), split_axis=0, concat_axis=0, tiled=True
    ).reshape(devices, times, block, lanes)

    gains, mark = call(
        functools.partial(spread_kernel, parts, real_antennas, tiles, apart),
        (
            jax.ShapeDtypeStruct((2 * real_antennas * tiles, LANES), jnp.float32),
            jax.ShapeDtypeStruct((8, LANES), jnp.float32),
        ),
        32,
        (0, 12 * real_antennas * channels),
        grid=(2,),
        in_specs=[pl.BlockSpec(memory_space=pltpu.SMEM)]
        + [pl.BlockSpec(values.shape, lambda i: (0, 0, 0)) for values in gathered],
        out_specs=(
            pl.BlockSpec((real_antennas * tiles, LANES), lambda i: (i, 0)),
            pl.BlockSpec((8, LANES), lambda i: (0, 0)),
        ),
        scratch_shapes=[pltpu.VMEM((devices, sent_antennas, lanes), jnp.bfloat16)],
        name="gains",
    )(lax.axis_index("bl").astype(jnp.int32).reshape(1), *gathered)

    filled = call(
        functools.partial(fill_kernel, parts, times, reach),
        jax.ShapeDtypeStruct((2, block, times, channels), jnp.float32),
        32,
        (32 * reach * block * times * channels * LANES, 16 * block * times * channels),
        grid=(tiles // 2,),
        in_specs=[
            pl.BlockSpec((block, tiles), lambda i: (0, 0)),
            pl.BlockSpec(memory_space=pltpu.SMEM),
            pl.BlockSpec(channel_kernel.shape, lambda i: (0, 0, 0)),
        ]
        + [
            pl.BlockSpec(spread.shape, lambda i: (0, 0, 0, 0)),
            pl.BlockSpec(memory_space=pl.ANY),
        ],
        out_specs=pl.BlockSpec((2, block, times, 2 * LANES), lambda i: (0, 0, 0, i)),
        scratch_shapes=[
            pltpu.VMEM(((2 * times + 1) * block, (tiles + 2 * reach) * LANES), jnp.bfloat16),
            pltpu.VMEM(((2 * reach + 2) * LANES, 2 * LANES), jnp.bfloat16),
            pltpu.VMEM((times * block, times * block), jnp.bfloat16),
        ],
        name="fill",
    )(tile_flag_mask, integration_kernel, channel_kernel, spread, mark)
    return gains.reshape(2, real_antennas, 1, channels), filled


def solution(mesh):
    in_specs = (
        P("bl", "ta", None),
        P("bl", "ta", None),
        P("bl"),
        P("bl", None),
        P(("bl", "ta"), None),
        P(),
        P(),
        P(),
    )
    out_specs = (P(None, None, "ta", None), P(None, ("bl", "ta"), None, None))
    return jax.shard_map(
        functools.partial(on_device, mesh.shape["bl"]),
        mesh=mesh,
        in_specs=in_specs,
        out_specs=out_specs,
        check_vma=False,
    )
```

```python
import functools

import jax
import jax.numpy as jnp
from jax import lax
from jax.experimental import pallas as pl
from jax.experimental.pallas import tpu as pltpu
from jax.sharding import PartitionSpec as P

NGRP = 224
GROUP_ROWS = 256
LANES = 128
HIGHEST = lax.Precision.HIGHEST


def round_up(value, unit):
    return -(-value // unit) * unit


class Part:
    def __init__(self, first, half, at):
        self.first = first
        self.half = half
        self.at = at
        self.lanes = 2 * half


def parts_of(channels, devices):
    width = channels // devices
    whole = width // LANES * LANES
    parts = []
    if whole:
        parts.append(Part(0, whole, 0))
    if width - whole:
        parts.append(Part(devices * whole, width - whole, 2 * whole))
    return parts


def tile_pieces(parts, tile, which):
    at = tile * LANES
    index = max(k for k, part in enumerate(parts) if part.first <= at)
    part = parts[index]
    at -= part.first
    end = at + LANES
    pieces = []
    while at < end:
        device, inside = divmod(at, part.half)
        width = min(part.half - inside, end - at)
        pieces.append((index, device, which * part.half + inside, width))
        at += width
    return pieces


def lanes_of(parts, which):
    slices = []
    for part in parts:
        if part.half % LANES == 0:
            slices.append(slice(part.at + which * part.half, part.at + (which + 1) * part.half))
        else:
            slices.append(slice(part.at, part.at + part.lanes))
    return slices


def join(pieces):
    return pieces[0] if len(pieces) == 1 else jnp.concatenate(pieces, axis=-1)


def call(body, out_shape, vmem, work, **kwargs):
    flops, moved = work
    return pl.pallas_call(
        body,
        out_shape=out_shape,
        cost_estimate=pl.CostEstimate(flops=flops, bytes_accessed=moved, transcendentals=0),
        compiler_params=pltpu.CompilerParams(vmem_limit_bytes=vmem * 1024 * 1024),
        **kwargs,
    )


def digit_groups(own, lanes):
    return [(at, min(lanes, own - at)) for at in range(0, own, lanes)]


def digit_rows(own, lanes):
    return round_up(6 * len(digit_groups(own, lanes)), 16)


def pack_kernel(parts, group_ref, couple_ref, amp_hbm, phase_hbm, out_hbm, *refs):
    out, amp, phase, in_sems, out_sems = refs
    own = amp.shape[0]
    devices, _, lanes = out.shape
    blocks = in_sems.shape[1]
    rows = own // blocks
    copies = []
    for k in range(blocks):
        at = pl.ds(k * rows, rows)
        pair = [
            pltpu.make_async_copy(
                source.at[at], target.at[at], in_sems.at[which, k]
            )
            for which, (source, target) in enumerate(((amp_hbm, amp), (phase_hbm, phase)))
        ]
        for copy in pair:
            copy.start()
        copies.append(pair)
    sent = []
    numbers = [group_ref[...], couple_ref[0:1, :], couple_ref[1:2, :]]
    digits = []
    for number in numbers:
        wide = number.astype(jnp.float32)
        high = jnp.floor(wide * (1.0 / LANES))
        digits += [high, wide - high * LANES]
    lines = []
    for first, width in digit_groups(own, lanes):
        for digit in digits:
            line = digit[:, first : first + width]
            if width < lanes:
                line = jnp.concatenate(
                    [line, jnp.zeros((1, lanes - width), line.dtype)], axis=1
                )
            lines.append(line)
    extra = digit_rows(own, lanes)
    lines.append(jnp.zeros((extra - len(lines), lanes), jnp.float32))
    lines = jnp.concatenate(lines, axis=0).astype(jnp.bfloat16)
    for device in range(devices):
        out[device, own:, :] = lines
    block = pl.ds(own, extra)
    copy = pltpu.make_async_copy(out.at[:, block], out_hbm.at[:, block], out_sems.at[blocks])
    copy.start()
    sent.append(copy)
    for k in range(blocks):
        for copy in copies[k]:
            copy.wait()
        at = slice(k * rows, (k + 1) * rows)
        for part in parts:
            half = part.half
            for device in range(devices):
                first = part.first + device * half
                for which, ref in enumerate((amp, phase)):
                    lane = part.at + which * half
                    out[device, at, lane : lane + half] = ref[at, first : first + half]
        block = pl.ds(k * rows, rows)
        copy = pltpu.make_async_copy(out.at[:, block], out_hbm.at[:, block], out_sems.at[k])
        copy.start()
        sent.append(copy)
    for copy in sent:
        copy.wait()


def hot_rows(labels, number):
    rows = lax.broadcasted_iota(jnp.int32, (labels, number.shape[1]), 0).astype(jnp.float32)
    return (rows == number).astype(jnp.float32)


def solve_kernel(parts, own, x_ref, inverse_ref, order_ref, gain_ref, sent_ref, index_ref, sums, link):
    devices, _, lanes = x_ref.shape
    antennas = gain_ref.shape[0]
    sums[...] = jnp.zeros_like(sums)
    link[...] = jnp.zeros_like(link)

    def gather(device, carry):
        digits = x_ref[device, own:, :].astype(jnp.float32)
        numbers = []
        for k in range(3):
            pieces = []
            for piece, (_, width) in enumerate(digit_groups(own, lanes)):
                at = 6 * piece + 2 * k
                pieces.append(
                    digits[at : at + 1, :width] * LANES + digits[at + 1 : at + 2, :width]
                )
            numbers.append(join(pieces))
        index_ref[device] = jnp.concatenate(numbers + [jnp.zeros((5, own), jnp.float32)], axis=0)
        group_hot = hot_rows(GROUP_ROWS, numbers[0]).astype(jnp.bfloat16)
        first, second = [hot_rows(antennas, number) for number in numbers[1:]]
        for s, couple in enumerate((first + second, first - second)):
            hot = jnp.concatenate([group_hot, couple.astype(jnp.bfloat16)], axis=0)
            values = join([x_ref[device, 0:own, use] for use in lanes_of(parts, s)])
            sums[s] += jnp.dot(hot, values, preferred_element_type=jnp.float32)
            link[s] += lax.dot_general(
                hot[GROUP_ROWS:],
                group_hot,
                (((1,), (1,)), ((), ())),
                preferred_element_type=jnp.float32,
            )
        return carry

    lax.fori_loop(0, devices, gather, 0, unroll=4)
    counts = 0.5 * jnp.sum(link[0], axis=0, keepdims=True)
    share = 1.0 / jnp.maximum(counts, 1.0)
    for s in range(2):
        rhs = sums[s, GROUP_ROWS:, :] - jnp.dot(
            link[s] * share,
            sums[s, :GROUP_ROWS, :],
            precision=HIGHEST,
            preferred_element_type=jnp.float32,
        )
        gain = jnp.dot(
            inverse_ref[s], rhs, precision=HIGHEST, preferred_element_type=jnp.float32
        )
        at = 0
        for part, use in zip(parts, lanes_of(parts, s)):
            width = use.stop - use.start
            values = gain[:, at : at + width]
            if s and width == part.lanes:
                low = lax.broadcasted_iota(jnp.int32, values.shape, 1) < part.half
                values = jnp.where(low, gain_ref[:, use], values)
            gain_ref[:, use] = values
            at += width
    sent_ref[0] = gain_ref[: sent_ref.shape[1], :].astype(jnp.bfloat16)


def reduced(angle):
    turns = jnp.floor(angle * 0.6366197723675814 + 0.5)
    left = angle - turns * 1.5703125
    left = left - turns * 4.83751296997070312e-4
    left = left - turns * 7.54978995489188216e-8
    square = left * left
    sine = ((-1.9515295891e-4 * square + 8.3321608736e-3) * square - 1.6666654611e-1) * square
    sine = sine * left + left
    cosine = (2.443315711809948e-5 * square - 1.388731625493765e-3) * square
    cosine = (cosine + 4.166664568298827e-2) * square * square - 0.5 * square + 1.0
    return turns.astype(jnp.int32), sine, cosine


def quarter(turns, sine, cosine):
    value = jnp.where((turns & 1) == 1, cosine, sine)
    return jnp.where((turns & 2) == 2, -value, value)


def swap(values, half):
    if 2 * half == LANES:
        return pltpu.roll(values, half, 1)
    return jnp.concatenate([values[:, half:], values[:, :half]], axis=1)


def calibrate_kernel(parts, own, x_ref, index_ref, gain_ref, out_ref, split):
    antennas = gain_ref.shape[0]

    @pl.when(pl.program_id(0) == 0)
    def _():
        for s in range(2):
            left = join([gain_ref[:, use] for use in lanes_of(parts, s)])
            for k in range(3):
                part = left.astype(jnp.bfloat16)
                split[s, k] = part
                left = left - part.astype(jnp.float32)

    labels = lax.broadcasted_iota(jnp.int32, (own, antennas), 1).astype(jnp.float32)
    for device in range(x_ref.shape[0]):
        columns = jnp.transpose(index_ref[device])
        first, second = [
            (labels == columns[:, k : k + 1]).astype(jnp.float32) for k in (1, 2)
        ]
        moves = []
        for s, couple in enumerate((first + second, first - second)):
            hot = couple.astype(jnp.bfloat16)
            move = jnp.dot(hot, split[s, 0], preferred_element_type=jnp.float32)
            for k in range(1, 3):
                move = move + jnp.dot(hot, split[s, k], preferred_element_type=jnp.float32)
            moves.append(move)
        rows = slice(device * own, (device + 1) * own)
        at = 0
        for part in parts:
            half, lanes = part.half, part.lanes
            first_lanes = slice(part.at, part.at + half)
            second_lanes = slice(part.at + half, part.at + lanes)
            if half % LANES == 0:
                here = slice(at, at + half)
                left = x_ref[device, 0:own, first_lanes].astype(jnp.float32) - moves[0][:, here]
                magnitude = jnp.exp(left)
                left = x_ref[device, 0:own, second_lanes].astype(jnp.float32) - moves[1][:, here]
                turns, sine, cosine = reduced(left)
                real = magnitude * quarter(turns + 1, sine, cosine)
                imaginary = magnitude * quarter(turns, sine, cosine)
                out_ref[rows, first_lanes] = real.astype(jnp.bfloat16)
                out_ref[rows, second_lanes] = imaginary.astype(jnp.bfloat16)
                at += half
            else:
                here = slice(at, at + lanes)
                both = slice(part.at, part.at + lanes)
                left = x_ref[device, 0:own, both].astype(jnp.float32)
                lower = lax.broadcasted_iota(jnp.int32, left.shape, 1) < half
                left = left - jnp.where(lower, moves[0][:, here], moves[1][:, here])
                turned = swap(left, half)
                magnitude = jnp.exp(jnp.where(lower, left, turned))
                turns, sine, cosine = reduced(jnp.where(lower, turned, left))
                turns = jnp.where(lower, turns + 1, turns)
                value = magnitude * quarter(turns, sine, cosine)
                out_ref[rows, both] = value.astype(jnp.bfloat16)
                at += lanes


def nothing(*refs):
    pass


def after(values, *others):
    return call(
        nothing,
        jax.ShapeDtypeStruct(values.shape, values.dtype),
        4,
        (0, 8 * values.size),
        in_specs=[pl.BlockSpec(memory_space=pl.ANY)] * (1 + len(others)),
        out_specs=pl.BlockSpec(memory_space=pl.ANY),
        input_output_aliases={0: 0},
        name="after",
    )(values, *others)


def pass_on(held, devices, reach):
    return lax.ppermute(held, "bl", [(i, i ^ reach) for i in range(devices)])


def spread_kernel(parts, antennas, tiles, apart, me_ref, *refs):
    gain_refs, (out_ref, chunks) = refs[: len(apart)], refs[-2:]
    which = pl.program_id(0)

    @pl.when(which == 0)
    def _():
        for gain_ref, distances in zip(gain_refs, apart):
            for entry, distance in enumerate(distances):
                chunks[me_ref[0] ^ distance] = gain_ref[entry]

    for s in range(2):

        @pl.when(which == s)
        def _():
            for tile in range(tiles):
                pieces = []
                for part, device, lane, width in tile_pieces(parts, tile, s):
                    lane += parts[part].at
                    pieces.append(chunks[device, :, lane : lane + width].astype(jnp.float32))
                out_ref[pl.ds(tile, antennas, tiles), :] = join(pieces)[:antennas]


def prepare_kernel(times, reach, mask_ref, kernel_ref, band_ref, order_ref, share_ref, weights):
    block, tiles = mask_ref.shape
    keep = (1 - mask_ref[...]).astype(jnp.float32)
    weights[...] = jnp.zeros_like(weights)
    for tile in range(tiles):
        weight = jnp.broadcast_to(keep[:, tile : tile + 1], (block, LANES))
        weights[:, (reach + tile) * LANES : (reach + tile + 1) * LANES] = weight.astype(
            weights.dtype
        )
    place = lax.broadcasted_iota(jnp.int32, order_ref.shape, 0)
    origin = lax.broadcasted_iota(jnp.int32, order_ref.shape, 1)
    moved = (place % times) * block + place // times == origin
    order_ref[...] = moved.astype(jnp.float32).astype(jnp.bfloat16)
    band_ref[...] = jnp.zeros_like(band_ref)
    for offset in range(2 * reach + 1):
        turned = jnp.transpose(kernel_ref[offset].astype(jnp.float32)).astype(band_ref.dtype)
        for target in range(2):
            first = (offset + target) * LANES
            band_ref[first : first + LANES, target * LANES : (target + 1) * LANES] = turned
    span, width = band_ref.shape
    for at in range(0, tiles * LANES, width):
        mixed = jnp.dot(
            weights[:, at : at + span], band_ref[...], preferred_element_type=jnp.float32
        )
        kept = weights[:, at + reach * LANES : at + reach * LANES + width].astype(jnp.float32)
        share_ref[:, at : at + width] = jnp.where(kept > 0.5, 0.0, 1.0 / mixed)


def fill_kernel(
    parts, times, reach, mask_ref, times_ref, band_ref, order_ref, share_ref, cal_ref, *refs
):
    out_ref, mark_ref, rows = refs
    step = pl.program_id(0)
    block, tiles = mask_ref.shape
    span, width = band_ref.shape

    @pl.when(step == 0)
    def _():
        mark_ref[...] = jnp.zeros_like(mark_ref)
        keep = (1 - mask_ref[...]).astype(jnp.float32)
        edge = reach * LANES
        inner = (reach + tiles) * LANES
        rows[:, :edge] = jnp.zeros((rows.shape[0], edge), rows.dtype)
        rows[:, inner:] = jnp.zeros((rows.shape[0], rows.shape[1] - inner), rows.dtype)
        for tile in range(tiles):
            lanes = slice((reach + tile) * LANES, (reach + tile + 1) * LANES)
            weight = jnp.broadcast_to(keep[:, tile : tile + 1], (block, LANES))
            weight = weight.astype(rows.dtype)
            for c in range(2):
                for t in range(times):
                    values = []
                    for part, device, lane, wide in tile_pieces(parts, tile, c):
                        lane += parts[part].at
                        values.append(cal_ref[device, t, :, lane : lane + wide])
                    at = (c * times + t) * block
                    rows[at : at + block, lanes] = join(values) * weight

    mixes = []
    for t in range(times):
        scale = times_ref[t, 0]
        for u in range(1, times):
            scale = scale + times_ref[t, u]
        share = 1.0 / scale
        mixes.append([times_ref[t, u] * share for u in range(times)])
    at = pl.multiple_of(step * width, width)
    mixed = jnp.dot(
        rows[:, pl.ds(at, span)], band_ref[...], preferred_element_type=jnp.float32
    )
    kept = rows[:, pl.ds(pl.multiple_of(at + reach * LANES, LANES), width)].astype(jnp.float32)
    share = share_ref[...]
    flagged = share > 0.0
    for c in range(2):
        values = []
        for t in range(times):
            value = None
            for u in range(times):
                first = (c * times + u) * block
                part = mixes[t][u] * mixed[first : first + block]
                value = part if value is None else value + part
            first = (c * times + t) * block
            values.append(jnp.where(flagged, value * share, kept[first : first + block]))
        values = jnp.concatenate(values, axis=0)
        large = values.astype(jnp.bfloat16)
        small = (values - large.astype(jnp.float32)).astype(jnp.bfloat16)
        values = jnp.dot(
            order_ref[...], large, preferred_element_type=jnp.float32
        ) + jnp.dot(order_ref[...], small, preferred_element_type=jnp.float32)
        out_ref[c] = values.reshape(block, times, width)


def on_device(
    devices,
    log_amplitude,
    phase,
    redundant_group_index,
    antenna_couples,
    tile_flag_mask,
    inverse,
    integration_kernel,
    channel_kernel,
):
    own, _, channels = log_amplitude.shape
    total = own * devices
    real_antennas = inverse.shape[1]
    antennas = round_up(real_antennas, LANES)
    sent_antennas = round_up(real_antennas, 16)
    times = integration_kernel.shape[0]
    block = tile_flag_mask.shape[0]
    reach = (channel_kernel.shape[0] - 1) // 2
    tiles = channels // LANES
    parts = parts_of(channels, devices)
    gap = antennas - real_antennas
    wide_inverse = jnp.pad(inverse, ((0, 0), (0, gap), (0, gap)))
    lanes = sum(part.lanes for part in parts)
    extra = digit_rows(own, lanes)
    shape = (devices, own + extra, lanes)
    blocks = 8
    packed = call(
        functools.partial(pack_kernel, parts),
        jax.ShapeDtypeStruct(shape, jnp.bfloat16),
        60,
        (0, 8 * own * channels),
        in_specs=[
            pl.BlockSpec(memory_space=pltpu.VMEM),
            pl.BlockSpec(memory_space=pltpu.VMEM),
            pl.BlockSpec(memory_space=pl.ANY),
            pl.BlockSpec(memory_space=pl.ANY),
        ],
        out_specs=pl.BlockSpec(memory_space=pl.ANY),
        scratch_shapes=[pltpu.VMEM(shape, jnp.bfloat16)]
        + [pltpu.VMEM((own, channels), jnp.bfloat16)] * 2
        + [pltpu.SemaphoreType.DMA((2, blocks)), pltpu.SemaphoreType.DMA((blocks + 1,))],
        name="pack",
    )(
        redundant_group_index.reshape(1, own),
        jnp.transpose(antenna_couples),
        log_amplitude.reshape(own, channels),
        phase.reshape(own, channels),
    )
    terms = lax.all_to_all(packed, "bl", split_axis=0, concat_axis=0, tiled=True)

    large = total // 2048
    wide = sum(use.stop - use.start for use in lanes_of(parts, 0))
    span, width = (2 * reach + 2) * LANES, 2 * LANES
    band, order, share = call(
        functools.partial(prepare_kernel, times, reach),
        (
            jax.ShapeDtypeStruct((span, width), jnp.bfloat16),
            jax.ShapeDtypeStruct((times * block, times * block), jnp.bfloat16),
            jax.ShapeDtypeStruct((block, channels), jnp.float32),
        ),
        16,
        (2 * block * channels * span, 4 * span * width),
        scratch_shapes=[pltpu.VMEM((block, (tiles + 2 * reach) * LANES), jnp.bfloat16)],
        name="prepare",
    )(tile_flag_mask, channel_kernel)

    gain, sent, indices = call(
        functools.partial(solve_kernel, parts, own),
        [
            jax.ShapeDtypeStruct((antennas, lanes), jnp.float32),
            jax.ShapeDtypeStruct((1, sent_antennas, lanes), jnp.bfloat16),
            jax.ShapeDtypeStruct((devices, 8, own), jnp.float32),
        ],
        min(56, 20 * large),
        (8 * total * (GROUP_ROWS + antennas) * lanes, 8 * total * lanes),
        in_specs=[
            pl.BlockSpec(memory_space=pltpu.VMEM),
            pl.BlockSpec(memory_space=pltpu.VMEM),
            pl.BlockSpec(memory_space=pl.ANY),
        ],
        scratch_shapes=[
            pltpu.VMEM((2, GROUP_ROWS + antennas, wide), jnp.float32),
            pltpu.VMEM((2, antennas, GROUP_ROWS), jnp.float32),
        ],
        name="solve",
    )(terms, wide_inverse, order)

    held, held_apart = sent, [0]
    hop = devices // 2
    while hop > 4:
        held = jnp.concatenate([held, pass_on(held, devices, hop)], axis=0)
        held_apart = held_apart + [distance ^ hop for distance in held_apart]
        hop //= 2
    far, near, side = [pass_on(held, devices, hop) for hop in (4, 2, 1)]
    gathered = [held, far, near, side]
    gathered += [pass_on(far, devices, hop) for hop in (1, 2, 3)] + [pass_on(near, devices, 1)]
    apart = [[distance ^ more for distance in held_apart] for more in (0, 4, 2, 1, 5, 6, 7, 3)]

    calibrated = call(
        functools.partial(calibrate_kernel, parts, own),
        jax.ShapeDtypeStruct((total, lanes), jnp.bfloat16),
        16,
        (16 * total * antennas * lanes, 8 * total * lanes),
        grid=(devices // 2,),
        in_specs=[
            pl.BlockSpec((2, own + extra, lanes), lambda i: (i, 0, 0)),
            pl.BlockSpec((2, 8, own), lambda i: (i, 0, 0)),
            pl.BlockSpec((antennas, lanes), lambda i: (0, 0)),
        ],
        out_specs=pl.BlockSpec((2 * own, lanes), lambda i: (i, 0)),
        scratch_shapes=[pltpu.VMEM((2, 3, antennas, wide), jnp.bfloat16)],
        name="calibrate",
    )(terms, indices, gain)
    spread = lax.all_to_all(
        after(calibrated, far, near, side), ("bl", "ta"), split_axis=0, concat_axis=0, tiled=True
    ).reshape(devices, times, block, lanes)

    filled, mark = call(
        functools.partial(fill_kernel, parts, times, reach),
        (
            jax.ShapeDtypeStruct((2, block, times, channels), jnp.float32),
            jax.ShapeDtypeStruct((8, LANES), jnp.float32),
        ),
        32,
        (32 * reach * block * times * channels * LANES, 16 * block * times * channels),
        grid=(tiles // 2,),
        in_specs=[
            pl.BlockSpec((block, tiles), lambda i: (0, 0)),
            pl.BlockSpec(memory_space=pltpu.SMEM),
            pl.BlockSpec(band.shape, lambda i: (0, 0)),
            pl.BlockSpec(order.shape, lambda i: (0, 0)),
            pl.BlockSpec((block, width), lambda i: (0, i)),
            pl.BlockSpec(spread.shape, lambda i: (0, 0, 0, 0)),
        ],
        out_specs=(
            pl.BlockSpec((2, block, times, width), lambda i: (0, 0, 0, i)),
            pl.BlockSpec((8, LANES), lambda i: (0, 0)),
        ),
        scratch_shapes=[
            pltpu.VMEM((2 * times * block, (tiles + 2 * reach) * LANES), jnp.bfloat16),
        ],
        name="fill",
    )(tile_flag_mask, integration_kernel, band, order, share, spread)

    gains = call(
        functools.partial(spread_kernel, parts, real_antennas, tiles, apart),
        jax.ShapeDtypeStruct((2 * real_antennas * tiles, LANES), jnp.float32),
        32,
        (0, 12 * real_antennas * channels),
        grid=(2,),
        in_specs=[pl.BlockSpec(memory_space=pltpu.SMEM)]
        + [pl.BlockSpec(values.shape, lambda i: (0, 0, 0)) for values in gathered]
        + [pl.BlockSpec(memory_space=pl.ANY)],
        out_specs=pl.BlockSpec((real_antennas * tiles, LANES), lambda i: (i, 0)),
        scratch_shapes=[pltpu.VMEM((devices, sent_antennas, lanes), jnp.bfloat16)],
        name="gains",
    )(lax.axis_index("bl").astype(jnp.int32).reshape(1), *gathered, mark)

    return gains.reshape(2, real_antennas, 1, channels), filled


def solution(mesh):
    in_specs = (
        P("bl", "ta", None),
        P("bl", "ta", None),
        P("bl"),
        P("bl", None),
        P(("bl", "ta"), None),
        P(),
        P(),
        P(),
    )
    out_specs = (P(None, None, "ta", None), P(None, ("bl", "ta"), None, None))
    return jax.shard_map(
        functools.partial(on_device, mesh.shape["bl"]),
        mesh=mesh,
        in_specs=in_specs,
        out_specs=out_specs,
        check_vma=False,
    )
```

```python
import functools

import jax
import jax.numpy as jnp
from jax import lax
from jax.experimental import pallas as pl
from jax.experimental.pallas import tpu as pltpu
from jax.sharding import PartitionSpec as P

NGRP = 224
GROUP_ROWS = 256
LANES = 128
HIGHEST = lax.Precision.HIGHEST


def round_up(value, unit):
    return -(-value // unit) * unit


class Part:
    def __init__(self, first, half, at):
        self.first = first
        self.half = half
        self.at = at
        self.lanes = 2 * half


def parts_of(channels, devices):
    width = channels // devices
    whole = width // LANES * LANES
    parts = []
    if whole:
        parts.append(Part(0, whole, 0))
    if width - whole:
        parts.append(Part(devices * whole, width - whole, 2 * whole))
    return parts


def tile_pieces(parts, tile, which):
    at = tile * LANES
    index = max(k for k, part in enumerate(parts) if part.first <= at)
    part = parts[index]
    at -= part.first
    end = at + LANES
    pieces = []
    while at < end:
        device, inside = divmod(at, part.half)
        width = min(part.half - inside, end - at)
        pieces.append((index, device, which * part.half + inside, width))
        at += width
    return pieces


def lanes_of(parts, which):
    slices = []
    for part in parts:
        if part.half % LANES == 0:
            slices.append(slice(part.at + which * part.half, part.at + (which + 1) * part.half))
        else:
            slices.append(slice(part.at, part.at + part.lanes))
    return slices


def join(pieces):
    return pieces[0] if len(pieces) == 1 else jnp.concatenate(pieces, axis=-1)


def call(body, out_shape, vmem, work, **kwargs):
    flops, moved = work
    return pl.pallas_call(
        body,
        out_shape=out_shape,
        cost_estimate=pl.CostEstimate(flops=flops, bytes_accessed=moved, transcendentals=0),
        compiler_params=pltpu.CompilerParams(vmem_limit_bytes=vmem * 1024 * 1024),
        **kwargs,
    )


def digit_groups(own, lanes):
    return [(at, min(lanes, own - at)) for at in range(0, own, lanes)]


def digit_rows(own, lanes):
    return round_up(6 * len(digit_groups(own, lanes)), 16)


def pack_kernel(parts, group_ref, couple_ref, amp_hbm, phase_hbm, out_hbm, *refs):
    out, amp, phase, in_sems, out_sems = refs
    own = amp.shape[0]
    devices, _, lanes = out.shape
    blocks = in_sems.shape[1]
    rows = own // blocks
    copies = []
    for k in range(blocks):
        at = pl.ds(k * rows, rows)
        pair = [
            pltpu.make_async_copy(
                source.at[at], target.at[at], in_sems.at[which, k]
            )
            for which, (source, target) in enumerate(((amp_hbm, amp), (phase_hbm, phase)))
        ]
        for copy in pair:
            copy.start()
        copies.append(pair)
    sent = []
    numbers = [group_ref[...], couple_ref[0:1, :], couple_ref[1:2, :]]
    digits = []
    for number in numbers:
        wide = number.astype(jnp.float32)
        high = jnp.floor(wide * (1.0 / LANES))
        digits += [high, wide - high * LANES]
    lines = []
    for first, width in digit_groups(own, lanes):
        for digit in digits:
            line = digit[:, first : first + width]
            if width < lanes:
                line = jnp.concatenate(
                    [line, jnp.zeros((1, lanes - width), line.dtype)], axis=1
                )
            lines.append(line)
    extra = digit_rows(own, lanes)
    lines.append(jnp.zeros((extra - len(lines), lanes), jnp.float32))
    lines = jnp.concatenate(lines, axis=0).astype(jnp.bfloat16)
    for device in range(devices):
        out[device, own:, :] = lines
    block = pl.ds(own, extra)
    copy = pltpu.make_async_copy(out.at[:, block], out_hbm.at[:, block], out_sems.at[blocks])
    copy.start()
    sent.append(copy)
    for k in range(blocks):
        for copy in copies[k]:
            copy.wait()
        at = slice(k * rows, (k + 1) * rows)
        for part in parts:
            half = part.half
            for device in range(devices):
                first = part.first + device * half
                for which, ref in enumerate((amp, phase)):
                    lane = part.at + which * half
                    out[device, at, lane : lane + half] = ref[at, first : first + half]
        block = pl.ds(k * rows, rows)
        copy = pltpu.make_async_copy(out.at[:, block], out_hbm.at[:, block], out_sems.at[k])
        copy.start()
        sent.append(copy)
    for copy in sent:
        copy.wait()


def hot_rows(labels, number):
    rows = lax.broadcasted_iota(jnp.int32, (labels, number.shape[1]), 0).astype(jnp.float32)
    return (rows == number).astype(jnp.float32)


def solve_kernel(parts, own, x_ref, inverse_ref, gain_ref, sent_ref, index_ref, sums, link):
    devices, _, lanes = x_ref.shape
    antennas = gain_ref.shape[0]
    sums[...] = jnp.zeros_like(sums)
    link[...] = jnp.zeros_like(link)

    def gather(device, carry):
        digits = x_ref[device, own:, :].astype(jnp.float32)
        numbers = []
        for k in range(3):
            pieces = []
            for piece, (_, width) in enumerate(digit_groups(own, lanes)):
                at = 6 * piece + 2 * k
                pieces.append(
                    digits[at : at + 1, :width] * LANES + digits[at + 1 : at + 2, :width]
                )
            numbers.append(join(pieces))
        index_ref[device] = jnp.concatenate(numbers + [jnp.zeros((5, own), jnp.float32)], axis=0)
        group_hot = hot_rows(GROUP_ROWS, numbers[0]).astype(jnp.bfloat16)
        first, second = [hot_rows(antennas, number) for number in numbers[1:]]
        for s, couple in enumerate((first + second, first - second)):
            hot = jnp.concatenate([group_hot, couple.astype(jnp.bfloat16)], axis=0)
            values = join([x_ref[device, 0:own, use] for use in lanes_of(parts, s)])
            sums[s] += jnp.dot(hot, values, preferred_element_type=jnp.float32)
            link[s] += lax.dot_general(
                hot[GROUP_ROWS:],
                group_hot,
                (((1,), (1,)), ((), ())),
                preferred_element_type=jnp.float32,
            )
        return carry

    lax.fori_loop(0, devices, gather, 0, unroll=4)
    counts = 0.5 * jnp.sum(link[0], axis=0, keepdims=True)
    share = 1.0 / jnp.maximum(counts, 1.0)
    for s in range(2):
        rhs = sums[s, GROUP_ROWS:, :] - jnp.dot(
            link[s] * share,
            sums[s, :GROUP_ROWS, :],
            precision=HIGHEST,
            preferred_element_type=jnp.float32,
        )
        gain = jnp.dot(
            inverse_ref[s], rhs, precision=HIGHEST, preferred_element_type=jnp.float32
        )
        at = 0
        for part, use in zip(parts, lanes_of(parts, s)):
            width = use.stop - use.start
            values = gain[:, at : at + width]
            if s and width == part.lanes:
                low = lax.broadcasted_iota(jnp.int32, values.shape, 1) < part.half
                values = jnp.where(low, gain_ref[:, use], values)
            gain_ref[:, use] = values
            at += width
    sent_ref[0] = gain_ref[: sent_ref.shape[1], :].astype(jnp.bfloat16)


def reduced(angle):
    turns = jnp.floor(angle * 0.6366197723675814 + 0.5)
    left = angle - turns * 1.5703125
    left = left - turns * 4.83751296997070312e-4
    left = left - turns * 7.54978995489188216e-8
    square = left * left
    sine = ((-1.9515295891e-4 * square + 8.3321608736e-3) * square - 1.6666654611e-1) * square
    sine = sine * left + left
    cosine = (2.443315711809948e-5 * square - 1.388731625493765e-3) * square
    cosine = (cosine + 4.166664568298827e-2) * square * square - 0.5 * square + 1.0
    return turns.astype(jnp.int32), sine, cosine


def quarter(turns, sine, cosine):
    value = jnp.where((turns & 1) == 1, cosine, sine)
    return jnp.where((turns & 2) == 2, -value, value)


def swap(values, half):
    if 2 * half == LANES:
        return pltpu.roll(values, half, 1)
    return jnp.concatenate([values[:, half:], values[:, :half]], axis=1)


def calibrate_kernel(parts, own, x_ref, index_ref, gain_ref, out_ref, split):
    antennas = gain_ref.shape[0]

    @pl.when(pl.program_id(0) == 0)
    def _():
        for s in range(2):
            left = join([gain_ref[:, use] for use in lanes_of(parts, s)])
            for k in range(3):
                part = left.astype(jnp.bfloat16)
                split[s, k] = part
                left = left - part.astype(jnp.float32)

    labels = lax.broadcasted_iota(jnp.int32, (own, antennas), 1).astype(jnp.float32)
    for device in range(x_ref.shape[0]):
        columns = jnp.transpose(index_ref[device])
        first, second = [
            (labels == columns[:, k : k + 1]).astype(jnp.float32) for k in (1, 2)
        ]
        moves = []
        for s, couple in enumerate((first + second, first - second)):
            hot = couple.astype(jnp.bfloat16)
            move = jnp.dot(hot, split[s, 0], preferred_element_type=jnp.float32)
            for k in range(1, 3):
                move = move + jnp.dot(hot, split[s, k], preferred_element_type=jnp.float32)
            moves.append(move)
        rows = slice(device * own, (device + 1) * own)
        at = 0
        for part in parts:
            half, lanes = part.half, part.lanes
            first_lanes = slice(part.at, part.at + half)
            second_lanes = slice(part.at + half, part.at + lanes)
            if half % LANES == 0:
                here = slice(at, at + half)
                left = x_ref[device, 0:own, first_lanes].astype(jnp.float32) - moves[0][:, here]
                magnitude = jnp.exp(left)
                left = x_ref[device, 0:own, second_lanes].astype(jnp.float32) - moves[1][:, here]
                turns, sine, cosine = reduced(left)
                real = magnitude * quarter(turns + 1, sine, cosine)
                imaginary = magnitude * quarter(turns, sine, cosine)
                out_ref[rows, first_lanes] = real.astype(jnp.bfloat16)
                out_ref[rows, second_lanes] = imaginary.astype(jnp.bfloat16)
                at += half
            else:
                here = slice(at, at + lanes)
                both = slice(part.at, part.at + lanes)
                left = x_ref[device, 0:own, both].astype(jnp.float32)
                lower = lax.broadcasted_iota(jnp.int32, left.shape, 1) < half
                left = left - jnp.where(lower, moves[0][:, here], moves[1][:, here])
                turned = swap(left, half)
                magnitude = jnp.exp(jnp.where(lower, left, turned))
                turns, sine, cosine = reduced(jnp.where(lower, turned, left))
                turns = jnp.where(lower, turns + 1, turns)
                value = magnitude * quarter(turns, sine, cosine)
                out_ref[rows, both] = value.astype(jnp.bfloat16)
                at += lanes


def nothing(*refs):
    pass


def after(values, *others):
    return call(
        nothing,
        jax.ShapeDtypeStruct(values.shape, values.dtype),
        4,
        (0, 8 * values.size),
        in_specs=[pl.BlockSpec(memory_space=pl.ANY)] * (1 + len(others)),
        out_specs=pl.BlockSpec(memory_space=pl.ANY),
        input_output_aliases={0: 0},
        name="after",
    )(values, *others)


def pass_on(held, devices, reach):
    return lax.ppermute(held, "bl", [(i, i ^ reach) for i in range(devices)])


def spread_kernel(parts, antennas, tiles, apart, me_ref, *refs):
    gain_refs, (out_ref, chunks) = refs[: len(apart)], refs[-2:]
    which = pl.program_id(0)

    @pl.when(which == 0)
    def _():
        for gain_ref, distances in zip(gain_refs, apart):
            for entry, distance in enumerate(distances):
                chunks[me_ref[0] ^ distance] = gain_ref[entry]

    for s in range(2):

        @pl.when(which == s)
        def _():
            for tile in range(tiles):
                pieces = []
                for part, device, lane, width in tile_pieces(parts, tile, s):
                    lane += parts[part].at
                    pieces.append(chunks[device, :, lane : lane + width].astype(jnp.float32))
                out_ref[pl.ds(tile, antennas, tiles), :] = join(pieces)[:antennas]


def fill_kernel(parts, times, reach, mask_ref, times_ref, kernel_ref, *refs):
    cal_ref, (out_ref, mark_ref, rows, band, interleave) = refs[0], refs[1:]
    step = pl.program_id(0)
    block, tiles = mask_ref.shape
    count = 2 * times * block
    span = (2 * reach + 2) * LANES

    @pl.when(step == 0)
    def _():
        mark_ref[...] = jnp.zeros_like(mark_ref)
        keep = (1 - mask_ref[...]).astype(jnp.float32)
        edge = reach * LANES
        inner = (reach + tiles) * LANES
        rows[:, :edge] = jnp.zeros((rows.shape[0], edge), rows.dtype)
        rows[:, inner:] = jnp.zeros((rows.shape[0], rows.shape[1] - inner), rows.dtype)
        for tile in range(tiles):
            lanes = slice((reach + tile) * LANES, (reach + tile + 1) * LANES)
            weight = jnp.broadcast_to(keep[:, tile : tile + 1], (block, LANES))
            weight = weight.astype(rows.dtype)
            rows[count:, lanes] = weight
            for c in range(2):
                for t in range(times):
                    values = join(
                        [
                            cal_ref[device, t, :, parts[part].at + lane : parts[part].at + lane + width]
                            for part, device, lane, width in tile_pieces(parts, tile, c)
                        ]
                    )
                    at = (c * times + t) * block
                    rows[at : at + block, lanes] = values * weight
        order = times * block
        place = lax.broadcasted_iota(jnp.int32, (order, order), 0)
        origin = lax.broadcasted_iota(jnp.int32, (order, order), 1)
        moved = (place % times) * block + place // times == origin
        interleave[...] = moved.astype(jnp.float32).astype(jnp.bfloat16)
        band[...] = jnp.zeros(band.shape, band.dtype)
        for offset in range(2 * reach + 1):
            turned = jnp.transpose(kernel_ref[offset].astype(jnp.float32)).astype(band.dtype)
            for target in range(2):
                first = (offset + target) * LANES
                band[first : first + LANES, target * LANES : (target + 1) * LANES] = turned

    mixes = []
    for t in range(times):
        scale = times_ref[t, 0]
        for u in range(1, times):
            scale = scale + times_ref[t, u]
        share = 1.0 / scale
        mixes.append([times_ref[t, u] * share for u in range(times)])
    width = out_ref.shape[3]
    for pair in range(width // (2 * LANES)):
        lanes = slice(pair * 2 * LANES, (pair + 1) * 2 * LANES)
        at = pl.multiple_of(step * width + pair * 2 * LANES, 2 * LANES)
        mixed = jnp.dot(
            rows[:, pl.ds(at, span)], band[...], preferred_element_type=jnp.float32
        )
        total = 1.0 / mixed[count:]
        kept = rows[:, pl.ds(pl.multiple_of(at + reach * LANES, LANES), 2 * LANES)]
        kept = kept.astype(jnp.float32)
        keep = kept[count:] > 0.5
        for c in range(2):
            values = []
            for t in range(times):
                value = None
                for u in range(times):
                    first = (c * times + u) * block
                    part = mixes[t][u] * mixed[first : first + block]
                    value = part if value is None else value + part
                first = (c * times + t) * block
                values.append(jnp.where(keep, kept[first : first + block], value * total))
            values = jnp.concatenate(values, axis=0)
            large = values.astype(jnp.bfloat16)
            small = (values - large.astype(jnp.float32)).astype(jnp.bfloat16)
            values = jnp.dot(
                interleave[...], large, preferred_element_type=jnp.float32
            ) + jnp.dot(interleave[...], small, preferred_element_type=jnp.float32)
            out_ref[c, :, :, lanes] = values.reshape(block, times, 2 * LANES)


def on_device(
    devices,
    log_amplitude,
    phase,
    redundant_group_index,
    antenna_couples,
    tile_flag_mask,
    inverse,
    integration_kernel,
    channel_kernel,
):
    own, _, channels = log_amplitude.shape
    total = own * devices
    real_antennas = inverse.shape[1]
    antennas = round_up(real_antennas, LANES)
    sent_antennas = round_up(real_antennas, 16)
    times = integration_kernel.shape[0]
    block = tile_flag_mask.shape[0]
    reach = (channel_kernel.shape[0] - 1) // 2
    tiles = channels // LANES
    parts = parts_of(channels, devices)
    gap = antennas - real_antennas
    wide_inverse = jnp.pad(inverse, ((0, 0), (0, gap), (0, gap)))
    lanes = sum(part.lanes for part in parts)
    extra = digit_rows(own, lanes)
    shape = (devices, own + extra, lanes)
    blocks = 4
    packed = call(
        functools.partial(pack_kernel, parts),
        jax.ShapeDtypeStruct(shape, jnp.bfloat16),
        60,
        (0, 8 * own * channels),
        in_specs=[
            pl.BlockSpec(memory_space=pltpu.VMEM),
            pl.BlockSpec(memory_space=pltpu.VMEM),
            pl.BlockSpec(memory_space=pl.ANY),
            pl.BlockSpec(memory_space=pl.ANY),
        ],
        out_specs=pl.BlockSpec(memory_space=pl.ANY),
        scratch_shapes=[pltpu.VMEM(shape, jnp.bfloat16)]
        + [pltpu.VMEM((own, channels), jnp.bfloat16)] * 2
        + [pltpu.SemaphoreType.DMA((2, blocks)), pltpu.SemaphoreType.DMA((blocks + 1,))],
        name="pack",
    )(
        redundant_group_index.reshape(1, own),
        jnp.transpose(antenna_couples),
        log_amplitude.reshape(own, channels),
        phase.reshape(own, channels),
    )
    terms = lax.all_to_all(packed, "bl", split_axis=0, concat_axis=0, tiled=True)

    large = total // 2048
    wide = sum(use.stop - use.start for use in lanes_of(parts, 0))
    gain, sent, indices = call(
        functools.partial(solve_kernel, parts, own),
        [
            jax.ShapeDtypeStruct((antennas, lanes), jnp.float32),
            jax.ShapeDtypeStruct((1, sent_antennas, lanes), jnp.bfloat16),
            jax.ShapeDtypeStruct((devices, 8, own), jnp.float32),
        ],
        min(56, 20 * large),
        (8 * total * (GROUP_ROWS + antennas) * lanes, 8 * total * lanes),
        scratch_shapes=[
            pltpu.VMEM((2, GROUP_ROWS + antennas, wide), jnp.float32),
            pltpu.VMEM((2, antennas, GROUP_ROWS), jnp.float32),
        ],
        name="solve",
    )(terms, wide_inverse)

    held, held_apart = sent, [0]
    hop = devices // 2
    while hop > 4:
        held = jnp.concatenate([held, pass_on(held, devices, hop)], axis=0)
        held_apart = held_apart + [distance ^ hop for distance in held_apart]
        hop //= 2
    far, near, side = [pass_on(held, devices, hop) for hop in (4, 2, 1)]
    gathered = [held, far, near, side]
    gathered += [pass_on(far, devices, hop) for hop in (1, 2, 3)] + [pass_on(near, devices, 1)]
    apart = [[distance ^ more for distance in held_apart] for more in (0, 4, 2, 1, 5, 6, 7, 3)]

    calibrated = call(
        functools.partial(calibrate_kernel, parts, own),
        jax.ShapeDtypeStruct((total, lanes), jnp.bfloat16),
        16,
        (16 * total * antennas * lanes, 8 * total * lanes),
        grid=(devices // 2,),
        in_specs=[
            pl.BlockSpec((2, own + extra, lanes), lambda i: (i, 0, 0)),
            pl.BlockSpec((2, 8, own), lambda i: (i, 0, 0)),
            pl.BlockSpec((antennas, lanes), lambda i: (0, 0)),
        ],
        out_specs=pl.BlockSpec((2 * own, lanes), lambda i: (i, 0)),
        scratch_shapes=[pltpu.VMEM((2, 3, antennas, wide), jnp.bfloat16)],
        name="calibrate",
    )(terms, indices, gain)
    spread = lax.all_to_all(
        after(calibrated, far, near, side), ("bl", "ta"), split_axis=0, concat_axis=0, tiled=True
    ).reshape(devices, times, block, lanes)

    filled, mark = call(
        functools.partial(fill_kernel, parts, times, reach),
        (
            jax.ShapeDtypeStruct((2, block, times, channels), jnp.float32),
            jax.ShapeDtypeStruct((8, LANES), jnp.float32),
        ),
        32,
        (32 * reach * block * times * channels * LANES, 16 * block * times * channels),
        grid=(tiles // 2,),
        in_specs=[
            pl.BlockSpec((block, tiles), lambda i: (0, 0)),
            pl.BlockSpec(memory_space=pltpu.SMEM),
            pl.BlockSpec(channel_kernel.shape, lambda i: (0, 0, 0)),
            pl.BlockSpec(spread.shape, lambda i: (0, 0, 0, 0)),
        ],
        out_specs=(
            pl.BlockSpec((2, block, times, 2 * LANES), lambda i: (0, 0, 0, i)),
            pl.BlockSpec((8, LANES), lambda i: (0, 0)),
        ),
        scratch_shapes=[
            pltpu.VMEM(((2 * times + 1) * block, (tiles + 2 * reach) * LANES), jnp.bfloat16),
            pltpu.VMEM(((2 * reach + 2) * LANES, 2 * LANES), jnp.bfloat16),
            pltpu.VMEM((times * block, times * block), jnp.bfloat16),
        ],
        name="fill",
    )(tile_flag_mask, integration_kernel, channel_kernel, spread)

    gains = call(
        functools.partial(spread_kernel, parts, real_antennas, tiles, apart),
        jax.ShapeDtypeStruct((2 * real_antennas * tiles, LANES), jnp.float32),
        32,
        (0, 12 * real_antennas * channels),
        grid=(2,),
        in_specs=[pl.BlockSpec(memory_space=pltpu.SMEM)]
        + [pl.BlockSpec(values.shape, lambda i: (0, 0, 0)) for values in gathered]
        + [pl.BlockSpec(memory_space=pl.ANY)],
        out_specs=pl.BlockSpec((real_antennas * tiles, LANES), lambda i: (i, 0)),
        scratch_shapes=[pltpu.VMEM((devices, sent_antennas, lanes), jnp.bfloat16)],
        name="gains",
    )(lax.axis_index("bl").astype(jnp.int32).reshape(1), *gathered, mark)

    return gains.reshape(2, real_antennas, 1, channels), filled


def solution(mesh):
    in_specs = (
        P("bl", "ta", None),
        P("bl", "ta", None),
        P("bl"),
        P("bl", None),
        P(("bl", "ta"), None),
        P(),
        P(),
        P(),
    )
    out_specs = (P(None, None, "ta", None), P(None, ("bl", "ta"), None, None))
    return jax.shard_map(
        functools.partial(on_device, mesh.shape["bl"]),
        mesh=mesh,
        in_specs=in_specs,
        out_specs=out_specs,
        check_vma=False,
    )
```

```python
import functools

import jax
import jax.numpy as jnp
from jax import lax
from jax.experimental import pallas as pl
from jax.experimental.pallas import tpu as pltpu
from jax.sharding import PartitionSpec as P

NGRP = 224
GROUP_ROWS = 256
LANES = 128
HIGHEST = lax.Precision.HIGHEST


def round_up(value, unit):
    return -(-value // unit) * unit


class Part:
    def __init__(self, first, half, at):
        self.first = first
        self.half = half
        self.at = at
        self.lanes = 2 * half


def parts_of(channels, devices):
    width = channels // devices
    whole = width // LANES * LANES
    parts = []
    if whole:
        parts.append(Part(0, whole, 0))
    if width - whole:
        parts.append(Part(devices * whole, width - whole, 2 * whole))
    return parts


def tile_pieces(parts, tile, which):
    at = tile * LANES
    index = max(k for k, part in enumerate(parts) if part.first <= at)
    part = parts[index]
    at -= part.first
    end = at + LANES
    pieces = []
    while at < end:
        device, inside = divmod(at, part.half)
        width = min(part.half - inside, end - at)
        pieces.append((index, device, which * part.half + inside, width))
        at += width
    return pieces


def lanes_of(parts, which):
    slices = []
    for part in parts:
        if part.half % LANES == 0:
            slices.append(slice(part.at + which * part.half, part.at + (which + 1) * part.half))
        else:
            slices.append(slice(part.at, part.at + part.lanes))
    return slices


def join(pieces):
    return pieces[0] if len(pieces) == 1 else jnp.concatenate(pieces, axis=-1)


def call(body, out_shape, vmem, work, **kwargs):
    flops, moved = work
    return pl.pallas_call(
        body,
        out_shape=out_shape,
        cost_estimate=pl.CostEstimate(flops=flops, bytes_accessed=moved, transcendentals=0),
        compiler_params=pltpu.CompilerParams(vmem_limit_bytes=vmem * 1024 * 1024),
        **kwargs,
    )


def digit_groups(own, lanes):
    return [(at, min(lanes, own - at)) for at in range(0, own, lanes)]


def digit_rows(own, lanes):
    return round_up(6 * len(digit_groups(own, lanes)), 16)


def pack_kernel(parts, group_ref, couple_ref, amp_hbm, phase_hbm, out_hbm, *refs):
    out, amp, phase, in_sems, out_sems = refs
    own = amp.shape[0]
    devices, _, lanes = out.shape
    blocks = in_sems.shape[1]
    rows = own // blocks
    copies = []
    for k in range(blocks):
        at = pl.ds(k * rows, rows)
        pair = [
            pltpu.make_async_copy(
                source.at[at], target.at[at], in_sems.at[which, k]
            )
            for which, (source, target) in enumerate(((amp_hbm, amp), (phase_hbm, phase)))
        ]
        for copy in pair:
            copy.start()
        copies.append(pair)
    sent = []
    numbers = [group_ref[...], couple_ref[0:1, :], couple_ref[1:2, :]]
    digits = []
    for number in numbers:
        wide = number.astype(jnp.float32)
        high = jnp.floor(wide * (1.0 / LANES))
        digits += [high, wide - high * LANES]
    lines = []
    for first, width in digit_groups(own, lanes):
        for digit in digits:
            line = digit[:, first : first + width]
            if width < lanes:
                line = jnp.concatenate(
                    [line, jnp.zeros((1, lanes - width), line.dtype)], axis=1
                )
            lines.append(line)
    extra = digit_rows(own, lanes)
    lines.append(jnp.zeros((extra - len(lines), lanes), jnp.float32))
    lines = jnp.concatenate(lines, axis=0).astype(jnp.bfloat16)
    for device in range(devices):
        out[device, own:, :] = lines
    block = pl.ds(own, extra)
    copy = pltpu.make_async_copy(out.at[:, block], out_hbm.at[:, block], out_sems.at[blocks])
    copy.start()
    sent.append(copy)
    for k in range(blocks):
        for copy in copies[k]:
            copy.wait()
        at = slice(k * rows, (k + 1) * rows)
        for part in parts:
            half = part.half
            for device in range(devices):
                first = part.first + device * half
                for which, ref in enumerate((amp, phase)):
                    lane = part.at + which * half
                    out[device, at, lane : lane + half] = ref[at, first : first + half]
        block = pl.ds(k * rows, rows)
        copy = pltpu.make_async_copy(out.at[:, block], out_hbm.at[:, block], out_sems.at[k])
        copy.start()
        sent.append(copy)
    for copy in sent:
        copy.wait()


def hot_rows(labels, number):
    rows = lax.broadcasted_iota(jnp.int32, (labels, number.shape[1]), 0).astype(jnp.float32)
    return (rows == number).astype(jnp.float32)


def solve_kernel(parts, own, x_ref, inverse_ref, gain_ref, sent_ref, index_ref, sums, link):
    devices, _, lanes = x_ref.shape
    antennas = gain_ref.shape[0]
    sums[...] = jnp.zeros_like(sums)
    link[...] = jnp.zeros_like(link)

    def gather(device, carry):
        digits = x_ref[device, own:, :].astype(jnp.float32)
        numbers = []
        for k in range(3):
            pieces = []
            for piece, (_, width) in enumerate(digit_groups(own, lanes)):
                at = 6 * piece + 2 * k
                pieces.append(
                    digits[at : at + 1, :width] * LANES + digits[at + 1 : at + 2, :width]
                )
            numbers.append(join(pieces))
        index_ref[device] = jnp.concatenate(numbers + [jnp.zeros((5, own), jnp.float32)], axis=0)
        group_hot = hot_rows(GROUP_ROWS, numbers[0]).astype(jnp.bfloat16)
        first, second = [hot_rows(antennas, number) for number in numbers[1:]]
        for s, couple in enumerate((first + second, first - second)):
            hot = jnp.concatenate([group_hot, couple.astype(jnp.bfloat16)], axis=0)
            values = join([x_ref[device, 0:own, use] for use in lanes_of(parts, s)])
            sums[s] += jnp.dot(hot, values, preferred_element_type=jnp.float32)
            link[s] += lax.dot_general(
                hot[GROUP_ROWS:],
                group_hot,
                (((1,), (1,)), ((), ())),
                preferred_element_type=jnp.float32,
            )
        return carry

    lax.fori_loop(0, devices, gather, 0, unroll=4)
    counts = 0.5 * jnp.sum(link[0], axis=0, keepdims=True)
    share = 1.0 / jnp.maximum(counts, 1.0)
    for s in range(2):
        rhs = sums[s, GROUP_ROWS:, :] - jnp.dot(
            link[s] * share,
            sums[s, :GROUP_ROWS, :],
            precision=HIGHEST,
            preferred_element_type=jnp.float32,
        )
        gain = jnp.dot(
            inverse_ref[s], rhs, precision=HIGHEST, preferred_element_type=jnp.float32
        )
        at = 0
        for part, use in zip(parts, lanes_of(parts, s)):
            width = use.stop - use.start
            values = gain[:, at : at + width]
            if s and width == part.lanes:
                low = lax.broadcasted_iota(jnp.int32, values.shape, 1) < part.half
                values = jnp.where(low, gain_ref[:, use], values)
            gain_ref[:, use] = values
            at += width
    sent_ref[0] = gain_ref[: sent_ref.shape[1], :].astype(jnp.bfloat16)


def reduced(angle):
    turns = jnp.floor(angle * 0.6366197723675814 + 0.5)
    left = angle - turns * 1.5703125
    left = left - turns * 4.83751296997070312e-4
    left = left - turns * 7.54978995489188216e-8
    square = left * left
    sine = ((-1.9515295891e-4 * square + 8.3321608736e-3) * square - 1.6666654611e-1) * square
    sine = sine * left + left
    cosine = (2.443315711809948e-5 * square - 1.388731625493765e-3) * square
    cosine = (cosine + 4.166664568298827e-2) * square * square - 0.5 * square + 1.0
    return turns.astype(jnp.int32), sine, cosine


def quarter(turns, sine, cosine):
    value = jnp.where((turns & 1) == 1, cosine, sine)
    return jnp.where((turns & 2) == 2, -value, value)


def swap(values, half):
    if 2 * half == LANES:
        return pltpu.roll(values, half, 1)
    return jnp.concatenate([values[:, half:], values[:, :half]], axis=1)


def calibrate_kernel(parts, own, x_ref, index_ref, gain_ref, out_ref, split):
    antennas = gain_ref.shape[0]

    @pl.when(pl.program_id(0) == 0)
    def _():
        for s in range(2):
            left = join([gain_ref[:, use] for use in lanes_of(parts, s)])
            for k in range(3):
                part = left.astype(jnp.bfloat16)
                split[s, k] = part
                left = left - part.astype(jnp.float32)

    labels = lax.broadcasted_iota(jnp.int32, (own, antennas), 1).astype(jnp.float32)
    for device in range(x_ref.shape[0]):
        columns = jnp.transpose(index_ref[device])
        first, second = [
            (labels == columns[:, k : k + 1]).astype(jnp.float32) for k in (1, 2)
        ]
        moves = []
        for s, couple in enumerate((first + second, first - second)):
            hot = couple.astype(jnp.bfloat16)
            move = jnp.dot(hot, split[s, 0], preferred_element_type=jnp.float32)
            for k in range(1, 3):
                move = move + jnp.dot(hot, split[s, k], preferred_element_type=jnp.float32)
            moves.append(move)
        rows = slice(device * own, (device + 1) * own)
        at = 0
        for part in parts:
            half, lanes = part.half, part.lanes
            first_lanes = slice(part.at, part.at + half)
            second_lanes = slice(part.at + half, part.at + lanes)
            if half % LANES == 0:
                here = slice(at, at + half)
                left = x_ref[device, 0:own, first_lanes].astype(jnp.float32) - moves[0][:, here]
                magnitude = jnp.exp(left)
                left = x_ref[device, 0:own, second_lanes].astype(jnp.float32) - moves[1][:, here]
                turns, sine, cosine = reduced(left)
                real = magnitude * quarter(turns + 1, sine, cosine)
                imaginary = magnitude * quarter(turns, sine, cosine)
                out_ref[rows, first_lanes] = real.astype(jnp.bfloat16)
                out_ref[rows, second_lanes] = imaginary.astype(jnp.bfloat16)
                at += half
            else:
                here = slice(at, at + lanes)
                both = slice(part.at, part.at + lanes)
                left = x_ref[device, 0:own, both].astype(jnp.float32)
                lower = lax.broadcasted_iota(jnp.int32, left.shape, 1) < half
                left = left - jnp.where(lower, moves[0][:, here], moves[1][:, here])
                turned = swap(left, half)
                magnitude = jnp.exp(jnp.where(lower, left, turned))
                turns, sine, cosine = reduced(jnp.where(lower, turned, left))
                turns = jnp.where(lower, turns + 1, turns)
                value = magnitude * quarter(turns, sine, cosine)
                out_ref[rows, both] = value.astype(jnp.bfloat16)
                at += lanes


def pass_on(held, devices, reach):
    return lax.ppermute(held, "bl", [(i, i ^ reach) for i in range(devices)])


def spread_kernel(parts, antennas, tiles, apart, me_ref, *refs):
    gain_refs, (out_ref, chunks) = refs[: len(apart)], refs[-2:]
    which = pl.program_id(0)

    @pl.when(which == 0)
    def _():
        for gain_ref, distances in zip(gain_refs, apart):
            for entry, distance in enumerate(distances):
                chunks[me_ref[0] ^ distance] = gain_ref[entry]

    for s in range(2):

        @pl.when(which == s)
        def _():
            for tile in range(tiles):
                pieces = []
                for part, device, lane, width in tile_pieces(parts, tile, s):
                    lane += parts[part].at
                    pieces.append(chunks[device, :, lane : lane + width].astype(jnp.float32))
                out_ref[pl.ds(tile, antennas, tiles), :] = join(pieces)[:antennas]


def fill_kernel(parts, times, reach, mask_ref, times_ref, kernel_ref, *refs):
    cal_ref, (out_ref, mark_ref, rows, band, interleave, tile_kernel, sem) = refs[0], refs[1:]
    step = pl.program_id(0)
    block, tiles = mask_ref.shape
    count = 2 * times * block
    span = (2 * reach + 2) * LANES

    @pl.when(step == 0)
    def _():
        copy = pltpu.make_async_copy(kernel_ref, tile_kernel, sem)
        copy.start()
        mark_ref[...] = jnp.zeros_like(mark_ref)
        keep = (1 - mask_ref[...]).astype(jnp.float32)
        edge = reach * LANES
        inner = (reach + tiles) * LANES
        rows[:, :edge] = jnp.zeros((rows.shape[0], edge), rows.dtype)
        rows[:, inner:] = jnp.zeros((rows.shape[0], rows.shape[1] - inner), rows.dtype)
        for tile in range(tiles):
            lanes = slice((reach + tile) * LANES, (reach + tile + 1) * LANES)
            weight = jnp.broadcast_to(keep[:, tile : tile + 1], (block, LANES))
            weight = weight.astype(rows.dtype)
            rows[count:, lanes] = weight
            for c in range(2):
                for t in range(times):
                    values = join(
                        [
                            cal_ref[device, t, :, parts[part].at + lane : parts[part].at + lane + width]
                            for part, device, lane, width in tile_pieces(parts, tile, c)
                        ]
                    )
                    at = (c * times + t) * block
                    rows[at : at + block, lanes] = values * weight
        order = times * block
        place = lax.broadcasted_iota(jnp.int32, (order, order), 0)
        origin = lax.broadcasted_iota(jnp.int32, (order, order), 1)
        moved = (place % times) * block + place // times == origin
        interleave[...] = moved.astype(jnp.float32).astype(jnp.bfloat16)
        band[...] = jnp.zeros(band.shape, band.dtype)
        copy.wait()
        for offset in range(2 * reach + 1):
            turned = jnp.transpose(tile_kernel[offset].astype(jnp.float32)).astype(band.dtype)
            for target in range(2):
                first = (offset + target) * LANES
                band[first : first + LANES, target * LANES : (target + 1) * LANES] = turned

    mixes = []
    for t in range(times):
        scale = times_ref[t, 0]
        for u in range(1, times):
            scale = scale + times_ref[t, u]
        share = 1.0 / scale
        mixes.append([times_ref[t, u] * share for u in range(times)])
    width = out_ref.shape[3]
    for pair in range(width // (2 * LANES)):
        lanes = slice(pair * 2 * LANES, (pair + 1) * 2 * LANES)
        at = pl.multiple_of(step * width + pair * 2 * LANES, 2 * LANES)
        mixed = jnp.dot(
            rows[:, pl.ds(at, span)], band[...], preferred_element_type=jnp.float32
        )
        total = 1.0 / mixed[count:]
        kept = rows[:, pl.ds(pl.multiple_of(at + reach * LANES, LANES), 2 * LANES)]
        kept = kept.astype(jnp.float32)
        keep = kept[count:] > 0.5
        for c in range(2):
            values = []
            for t in range(times):
                value = None
                for u in range(times):
                    first = (c * times + u) * block
                    part = mixes[t][u] * mixed[first : first + block]
                    value = part if value is None else value + part
                first = (c * times + t) * block
                values.append(jnp.where(keep, kept[first : first + block], value * total))
            values = jnp.concatenate(values, axis=0)
            large = values.astype(jnp.bfloat16)
            small = (values - large.astype(jnp.float32)).astype(jnp.bfloat16)
            values = jnp.dot(
                interleave[...], large, preferred_element_type=jnp.float32
            ) + jnp.dot(interleave[...], small, preferred_element_type=jnp.float32)
            out_ref[c, :, :, lanes] = values.reshape(block, times, 2 * LANES)


def on_device(
    devices,
    log_amplitude,
    phase,
    redundant_group_index,
    antenna_couples,
    tile_flag_mask,
    inverse,
    integration_kernel,
    channel_kernel,
):
    own, _, channels = log_amplitude.shape
    total = own * devices
    real_antennas = inverse.shape[1]
    antennas = round_up(real_antennas, LANES)
    sent_antennas = round_up(real_antennas, 16)
    times = integration_kernel.shape[0]
    block = tile_flag_mask.shape[0]
    reach = (channel_kernel.shape[0] - 1) // 2
    tiles = channels // LANES
    parts = parts_of(channels, devices)
    gap = antennas - real_antennas
    wide_inverse = jnp.pad(inverse, ((0, 0), (0, gap), (0, gap)))
    lanes = sum(part.lanes for part in parts)
    extra = digit_rows(own, lanes)
    shape = (devices, own + extra, lanes)
    blocks = 4
    packed = call(
        functools.partial(pack_kernel, parts),
        jax.ShapeDtypeStruct(shape, jnp.bfloat16),
        60,
        (0, 8 * own * channels),
        in_specs=[
            pl.BlockSpec(memory_space=pltpu.VMEM),
            pl.BlockSpec(memory_space=pltpu.VMEM),
            pl.BlockSpec(memory_space=pl.ANY),
            pl.BlockSpec(memory_space=pl.ANY),
        ],
        out_specs=pl.BlockSpec(memory_space=pl.ANY),
        scratch_shapes=[pltpu.VMEM(shape, jnp.bfloat16)]
        + [pltpu.VMEM((own, channels), jnp.bfloat16)] * 2
        + [pltpu.SemaphoreType.DMA((2, blocks)), pltpu.SemaphoreType.DMA((blocks + 1,))],
        name="pack",
    )(
        redundant_group_index.reshape(1, own),
        jnp.transpose(antenna_couples),
        log_amplitude.reshape(own, channels),
        phase.reshape(own, channels),
    )
    terms = lax.all_to_all(packed, "bl", split_axis=0, concat_axis=0, tiled=True)

    large = total // 2048
    wide = sum(use.stop - use.start for use in lanes_of(parts, 0))
    gain, sent, indices = call(
        functools.partial(solve_kernel, parts, own),
        [
            jax.ShapeDtypeStruct((antennas, lanes), jnp.float32),
            jax.ShapeDtypeStruct((1, sent_antennas, lanes), jnp.bfloat16),
            jax.ShapeDtypeStruct((devices, 8, own), jnp.float32),
        ],
        min(56, 20 * large),
        (8 * total * (GROUP_ROWS + antennas) * lanes, 8 * total * lanes),
        scratch_shapes=[
            pltpu.VMEM((2, GROUP_ROWS + antennas, wide), jnp.float32),
            pltpu.VMEM((2, antennas, GROUP_ROWS), jnp.float32),
        ],
        name="solve",
    )(terms, wide_inverse)

    held, held_apart = sent, [0]
    hop = devices // 2
    while hop > 4:
        held = jnp.concatenate([held, pass_on(held, devices, hop)], axis=0)
        held_apart = held_apart + [distance ^ hop for distance in held_apart]
        hop //= 2
    far, near, side = [pass_on(held, devices, hop) for hop in (4, 2, 1)]
    gathered = [held, far, near, side]
    gathered += [pass_on(far, devices, hop) for hop in (1, 2, 3)] + [pass_on(near, devices, 1)]
    apart = [[distance ^ more for distance in held_apart] for more in (0, 4, 2, 1, 5, 6, 7, 3)]

    calibrated = call(
        functools.partial(calibrate_kernel, parts, own),
        jax.ShapeDtypeStruct((total, lanes), jnp.bfloat16),
        16,
        (16 * total * antennas * lanes, 8 * total * lanes),
        grid=(devices // 2,),
        in_specs=[
            pl.BlockSpec((2, own + extra, lanes), lambda i: (i, 0, 0)),
            pl.BlockSpec((2, 8, own), lambda i: (i, 0, 0)),
            pl.BlockSpec((antennas, lanes), lambda i: (0, 0)),
        ],
        out_specs=pl.BlockSpec((2 * own, lanes), lambda i: (i, 0)),
        scratch_shapes=[pltpu.VMEM((2, 3, antennas, wide), jnp.bfloat16)],
        name="calibrate",
    )(terms, indices, gain)
    spread = lax.all_to_all(
        calibrated, ("bl", "ta"), split_axis=0, concat_axis=0, tiled=True
    ).reshape(devices, times, block, lanes)

    filled, mark = call(
        functools.partial(fill_kernel, parts, times, reach),
        (
            jax.ShapeDtypeStruct((2, block, times, channels), jnp.float32),
            jax.ShapeDtypeStruct((8, LANES), jnp.float32),
        ),
        32,
        (32 * reach * block * times * channels * LANES, 16 * block * times * channels),
        grid=(tiles // 2,),
        in_specs=[
            pl.BlockSpec((block, tiles), lambda i: (0, 0)),
            pl.BlockSpec(memory_space=pltpu.SMEM),
            pl.BlockSpec(memory_space=pl.ANY),
            pl.BlockSpec(spread.shape, lambda i: (0, 0, 0, 0)),
        ],
        out_specs=(
            pl.BlockSpec((2, block, times, 2 * LANES), lambda i: (0, 0, 0, i)),
            pl.BlockSpec((8, LANES), lambda i: (0, 0)),
        ),
        scratch_shapes=[
            pltpu.VMEM(((2 * times + 1) * block, (tiles + 2 * reach) * LANES), jnp.bfloat16),
            pltpu.VMEM(((2 * reach + 2) * LANES, 2 * LANES), jnp.bfloat16),
            pltpu.VMEM((times * block, times * block), jnp.bfloat16),
            pltpu.VMEM(channel_kernel.shape, jnp.bfloat16),
            pltpu.SemaphoreType.DMA(()),
        ],
        name="fill",
    )(tile_flag_mask, integration_kernel, channel_kernel, spread)

    gains = call(
        functools.partial(spread_kernel, parts, real_antennas, tiles, apart),
        jax.ShapeDtypeStruct((2 * real_antennas * tiles, LANES), jnp.float32),
        32,
        (0, 12 * real_antennas * channels),
        grid=(2,),
        in_specs=[pl.BlockSpec(memory_space=pltpu.SMEM)]
        + [pl.BlockSpec(values.shape, lambda i: (0, 0, 0)) for values in gathered]
        + [pl.BlockSpec(memory_space=pl.ANY)],
        out_specs=pl.BlockSpec((real_antennas * tiles, LANES), lambda i: (i, 0)),
        scratch_shapes=[pltpu.VMEM((devices, sent_antennas, lanes), jnp.bfloat16)],
        name="gains",
    )(lax.axis_index("bl").astype(jnp.int32).reshape(1), *gathered, mark)

    return gains.reshape(2, real_antennas, 1, channels), filled


def solution(mesh):
    in_specs = (
        P("bl", "ta", None),
        P("bl", "ta", None),
        P("bl"),
        P("bl", None),
        P(("bl", "ta"), None),
        P(),
        P(),
        P(),
    )
    out_specs = (P(None, None, "ta", None), P(None, ("bl", "ta"), None, None))
    return jax.shard_map(
        functools.partial(on_device, mesh.shape["bl"]),
        mesh=mesh,
        in_specs=in_specs,
        out_specs=out_specs,
        check_vma=False,
    )
```

```python
import functools

import jax
import jax.numpy as jnp
from jax import lax
from jax.experimental import pallas as pl
from jax.experimental.pallas import tpu as pltpu
from jax.sharding import PartitionSpec as P

NGRP = 224
GROUP_ROWS = 256
LANES = 128
HIGHEST = lax.Precision.HIGHEST


def round_up(value, unit):
    return -(-value // unit) * unit


class Part:
    def __init__(self, first, half, at):
        self.first = first
        self.half = half
        self.at = at
        self.lanes = 2 * half


def parts_of(channels, devices):
    width = channels // devices
    whole = width // LANES * LANES
    parts = []
    if whole:
        parts.append(Part(0, whole, 0))
    if width - whole:
        parts.append(Part(devices * whole, width - whole, 2 * whole))
    return parts


def tile_pieces(parts, tile, which):
    at = tile * LANES
    index = max(k for k, part in enumerate(parts) if part.first <= at)
    part = parts[index]
    at -= part.first
    end = at + LANES
    pieces = []
    while at < end:
        device, inside = divmod(at, part.half)
        width = min(part.half - inside, end - at)
        pieces.append((index, device, which * part.half + inside, width))
        at += width
    return pieces


def lanes_of(parts, which):
    slices = []
    for part in parts:
        if part.half % LANES == 0:
            slices.append(slice(part.at + which * part.half, part.at + (which + 1) * part.half))
        else:
            slices.append(slice(part.at, part.at + part.lanes))
    return slices


def join(pieces):
    return pieces[0] if len(pieces) == 1 else jnp.concatenate(pieces, axis=-1)


def call(body, out_shape, vmem, work, **kwargs):
    flops, moved = work
    return pl.pallas_call(
        body,
        out_shape=out_shape,
        cost_estimate=pl.CostEstimate(flops=flops, bytes_accessed=moved, transcendentals=0),
        compiler_params=pltpu.CompilerParams(vmem_limit_bytes=vmem * 1024 * 1024),
        **kwargs,
    )


def digit_groups(own, lanes):
    return [(at, min(lanes, own - at)) for at in range(0, own, lanes)]


def digit_rows(own, lanes):
    return round_up(6 * len(digit_groups(own, lanes)), 16)


def pack_kernel(parts, group_ref, couple_ref, amp_hbm, phase_hbm, out_hbm, *refs):
    out, amp, phase, in_sems, out_sems = refs
    own = amp.shape[0]
    devices, _, lanes = out.shape
    blocks = in_sems.shape[1]
    rows = own // blocks
    copies = []
    for k in range(blocks):
        at = pl.ds(k * rows, rows)
        pair = [
            pltpu.make_async_copy(
                source.at[at], target.at[at], in_sems.at[which, k]
            )
            for which, (source, target) in enumerate(((amp_hbm, amp), (phase_hbm, phase)))
        ]
        for copy in pair:
            copy.start()
        copies.append(pair)
    sent = []
    numbers = [group_ref[...], couple_ref[0:1, :], couple_ref[1:2, :]]
    digits = []
    for number in numbers:
        wide = number.astype(jnp.float32)
        high = jnp.floor(wide * (1.0 / LANES))
        digits += [high, wide - high * LANES]
    lines = []
    for first, width in digit_groups(own, lanes):
        for digit in digits:
            line = digit[:, first : first + width]
            if width < lanes:
                line = jnp.concatenate(
                    [line, jnp.zeros((1, lanes - width), line.dtype)], axis=1
                )
            lines.append(line)
    extra = digit_rows(own, lanes)
    lines.append(jnp.zeros((extra - len(lines), lanes), jnp.float32))
    lines = jnp.concatenate(lines, axis=0).astype(jnp.bfloat16)
    for device in range(devices):
        out[device, own:, :] = lines
    block = pl.ds(own, extra)
    copy = pltpu.make_async_copy(out.at[:, block], out_hbm.at[:, block], out_sems.at[blocks])
    copy.start()
    sent.append(copy)
    for k in range(blocks):
        for copy in copies[k]:
            copy.wait()
        at = slice(k * rows, (k + 1) * rows)
        for part in parts:
            half = part.half
            for device in range(devices):
                first = part.first + device * half
                for which, ref in enumerate((amp, phase)):
                    lane = part.at + which * half
                    out[device, at, lane : lane + half] = ref[at, first : first + half]
        block = pl.ds(k * rows, rows)
        copy = pltpu.make_async_copy(out.at[:, block], out_hbm.at[:, block], out_sems.at[k])
        copy.start()
        sent.append(copy)
    for copy in sent:
        copy.wait()


def hot_rows(labels, number):
    rows = lax.broadcasted_iota(jnp.int32, (labels, number.shape[1]), 0).astype(jnp.float32)
    return (rows == number).astype(jnp.float32)


def solve_kernel(parts, own, x_ref, inverse_ref, gain_ref, sent_ref, index_ref, sums, link):
    devices, _, lanes = x_ref.shape
    antennas = gain_ref.shape[0]
    sums[...] = jnp.zeros_like(sums)
    link[...] = jnp.zeros_like(link)

    def gather(device, carry):
        digits = x_ref[device, own:, :].astype(jnp.float32)
        numbers = []
        for k in range(3):
            pieces = []
            for piece, (_, width) in enumerate(digit_groups(own, lanes)):
                at = 6 * piece + 2 * k
                pieces.append(
                    digits[at : at + 1, :width] * LANES + digits[at + 1 : at + 2, :width]
                )
            numbers.append(join(pieces))
        index_ref[device] = jnp.concatenate(numbers + [jnp.zeros((5, own), jnp.float32)], axis=0)
        group_hot = hot_rows(GROUP_ROWS, numbers[0]).astype(jnp.bfloat16)
        first, second = [hot_rows(antennas, number) for number in numbers[1:]]
        for s, couple in enumerate((first + second, first - second)):
            hot = jnp.concatenate([group_hot, couple.astype(jnp.bfloat16)], axis=0)
            values = join([x_ref[device, 0:own, use] for use in lanes_of(parts, s)])
            sums[s] += jnp.dot(hot, values, preferred_element_type=jnp.float32)
            link[s] += lax.dot_general(
                hot[GROUP_ROWS:],
                group_hot,
                (((1,), (1,)), ((), ())),
                preferred_element_type=jnp.float32,
            )
        return carry

    lax.fori_loop(0, devices, gather, 0, unroll=4)
    counts = 0.5 * jnp.sum(link[0], axis=0, keepdims=True)
    share = 1.0 / jnp.maximum(counts, 1.0)
    for s in range(2):
        rhs = sums[s, GROUP_ROWS:, :] - jnp.dot(
            link[s] * share,
            sums[s, :GROUP_ROWS, :],
            precision=HIGHEST,
            preferred_element_type=jnp.float32,
        )
        gain = jnp.dot(
            inverse_ref[s], rhs, precision=HIGHEST, preferred_element_type=jnp.float32
        )
        at = 0
        for part, use in zip(parts, lanes_of(parts, s)):
            width = use.stop - use.start
            values = gain[:, at : at + width]
            if s and width == part.lanes:
                low = lax.broadcasted_iota(jnp.int32, values.shape, 1) < part.half
                values = jnp.where(low, gain_ref[:, use], values)
            gain_ref[:, use] = values
            at += width
    sent_ref[0] = gain_ref[: sent_ref.shape[1], :].astype(jnp.bfloat16)


def reduced(angle):
    turns = jnp.floor(angle * 0.6366197723675814 + 0.5)
    left = angle - turns * 1.5703125
    left = left - turns * 4.83751296997070312e-4
    left = left - turns * 7.54978995489188216e-8
    square = left * left
    sine = ((-1.9515295891e-4 * square + 8.3321608736e-3) * square - 1.6666654611e-1) * square
    sine = sine * left + left
    cosine = (2.443315711809948e-5 * square - 1.388731625493765e-3) * square
    cosine = (cosine + 4.166664568298827e-2) * square * square - 0.5 * square + 1.0
    return turns.astype(jnp.int32), sine, cosine


def quarter(turns, sine, cosine):
    value = jnp.where((turns & 1) == 1, cosine, sine)
    return jnp.where((turns & 2) == 2, -value, value)


def swap(values, half):
    if 2 * half == LANES:
        return pltpu.roll(values, half, 1)
    return jnp.concatenate([values[:, half:], values[:, :half]], axis=1)


def calibrate_kernel(parts, own, x_ref, index_ref, gain_ref, out_ref, split):
    antennas = gain_ref.shape[0]

    @pl.when(pl.program_id(0) == 0)
    def _():
        for s in range(2):
            left = join([gain_ref[:, use] for use in lanes_of(parts, s)])
            for k in range(3):
                part = left.astype(jnp.bfloat16)
                split[s, k] = part
                left = left - part.astype(jnp.float32)

    labels = lax.broadcasted_iota(jnp.int32, (own, antennas), 1).astype(jnp.float32)
    for device in range(x_ref.shape[0]):
        columns = jnp.transpose(index_ref[device])
        first, second = [
            (labels == columns[:, k : k + 1]).astype(jnp.float32) for k in (1, 2)
        ]
        moves = []
        for s, couple in enumerate((first + second, first - second)):
            hot = couple.astype(jnp.bfloat16)
            move = jnp.dot(hot, split[s, 0], preferred_element_type=jnp.float32)
            for k in range(1, 3):
                move = move + jnp.dot(hot, split[s, k], preferred_element_type=jnp.float32)
            moves.append(move)
        rows = slice(device * own, (device + 1) * own)
        at = 0
        for part in parts:
            half, lanes = part.half, part.lanes
            first_lanes = slice(part.at, part.at + half)
            second_lanes = slice(part.at + half, part.at + lanes)
            if half % LANES == 0:
                here = slice(at, at + half)
                left = x_ref[device, 0:own, first_lanes].astype(jnp.float32) - moves[0][:, here]
                magnitude = jnp.exp(left)
                left = x_ref[device, 0:own, second_lanes].astype(jnp.float32) - moves[1][:, here]
                turns, sine, cosine = reduced(left)
                real = magnitude * quarter(turns + 1, sine, cosine)
                imaginary = magnitude * quarter(turns, sine, cosine)
                out_ref[rows, first_lanes] = real.astype(jnp.bfloat16)
                out_ref[rows, second_lanes] = imaginary.astype(jnp.bfloat16)
                at += half
            else:
                here = slice(at, at + lanes)
                both = slice(part.at, part.at + lanes)
                left = x_ref[device, 0:own, both].astype(jnp.float32)
                lower = lax.broadcasted_iota(jnp.int32, left.shape, 1) < half
                left = left - jnp.where(lower, moves[0][:, here], moves[1][:, here])
                turned = swap(left, half)
                magnitude = jnp.exp(jnp.where(lower, left, turned))
                turns, sine, cosine = reduced(jnp.where(lower, turned, left))
                turns = jnp.where(lower, turns + 1, turns)
                value = magnitude * quarter(turns, sine, cosine)
                out_ref[rows, both] = value.astype(jnp.bfloat16)
                at += lanes


def nothing(*refs):
    pass


def after(values, *others):
    return call(
        nothing,
        jax.ShapeDtypeStruct(values.shape, values.dtype),
        4,
        (0, 8 * values.size),
        in_specs=[pl.BlockSpec(memory_space=pl.ANY)] * (1 + len(others)),
        out_specs=pl.BlockSpec(memory_space=pl.ANY),
        input_output_aliases={0: 0},
        name="after",
    )(values, *others)


def pass_on(held, devices, reach):
    return lax.ppermute(held, "bl", [(i, i ^ reach) for i in range(devices)])


def spread_kernel(parts, antennas, tiles, apart, me_ref, *refs):
    gain_refs, (out_ref, chunks) = refs[: len(apart)], refs[-2:]
    which = pl.program_id(0)

    @pl.when(which == 0)
    def _():
        for gain_ref, distances in zip(gain_refs, apart):
            for entry, distance in enumerate(distances):
                chunks[me_ref[0] ^ distance] = gain_ref[entry]

    for s in range(2):

        @pl.when(which == s)
        def _():
            for tile in range(tiles):
                pieces = []
                for part, device, lane, width in tile_pieces(parts, tile, s):
                    lane += parts[part].at
                    pieces.append(chunks[device, :, lane : lane + width].astype(jnp.float32))
                out_ref[pl.ds(tile, antennas, tiles), :] = join(pieces)[:antennas]


def fill_kernel(parts, times, reach, mask_ref, times_ref, kernel_ref, *refs):
    cal_ref, (out_ref, mark_ref, rows, band, interleave) = refs[0], refs[1:]
    step = pl.program_id(0)
    block, tiles = mask_ref.shape
    count = 2 * times * block
    span = (2 * reach + 2) * LANES

    @pl.when(step == 0)
    def _():
        mark_ref[...] = jnp.zeros_like(mark_ref)
        keep = (1 - mask_ref[...]).astype(jnp.float32)
        edge = reach * LANES
        inner = (reach + tiles) * LANES
        rows[:, :edge] = jnp.zeros((rows.shape[0], edge), rows.dtype)
        rows[:, inner:] = jnp.zeros((rows.shape[0], rows.shape[1] - inner), rows.dtype)
        for tile in range(tiles):
            lanes = slice((reach + tile) * LANES, (reach + tile + 1) * LANES)
            weight = jnp.broadcast_to(keep[:, tile : tile + 1], (block, LANES))
            weight = weight.astype(rows.dtype)
            rows[count:, lanes] = weight
            for c in range(2):
                for t in range(times):
                    values = join(
                        [
                            cal_ref[device, t, :, parts[part].at + lane : parts[part].at + lane + width]
                            for part, device, lane, width in tile_pieces(parts, tile, c)
                        ]
                    )
                    at = (c * times + t) * block
                    rows[at : at + block, lanes] = values * weight
        order = times * block
        place = lax.broadcasted_iota(jnp.int32, (order, order), 0)
        origin = lax.broadcasted_iota(jnp.int32, (order, order), 1)
        moved = (place % times) * block + place // times == origin
        interleave[...] = moved.astype(jnp.float32).astype(jnp.bfloat16)
        band[...] = jnp.zeros(band.shape, band.dtype)
        for offset in range(2 * reach + 1):
            turned = jnp.transpose(kernel_ref[offset].astype(jnp.float32)).astype(band.dtype)
            for target in range(2):
                first = (offset + target) * LANES
                band[first : first + LANES, target * LANES : (target + 1) * LANES] = turned

    mixes = []
    for t in range(times):
        scale = times_ref[t, 0]
        for u in range(1, times):
            scale = scale + times_ref[t, u]
        share = 1.0 / scale
        mixes.append([times_ref[t, u] * share for u in range(times)])
    width = out_ref.shape[3]
    for pair in range(width // (2 * LANES)):
        lanes = slice(pair * 2 * LANES, (pair + 1) * 2 * LANES)
        at = pl.multiple_of(step * width + pair * 2 * LANES, 2 * LANES)
        mixed = jnp.dot(
            rows[:, pl.ds(at, span)], band[...], preferred_element_type=jnp.float32
        )
        total = 1.0 / mixed[count:]
        kept = rows[:, pl.ds(pl.multiple_of(at + reach * LANES, LANES), 2 * LANES)]
        kept = kept.astype(jnp.float32)
        keep = kept[count:] > 0.5
        for c in range(2):
            values = []
            for t in range(times):
                value = None
                for u in range(times):
                    first = (c * times + u) * block
                    part = mixes[t][u] * mixed[first : first + block]
                    value = part if value is None else value + part
                first = (c * times + t) * block
                values.append(jnp.where(keep, kept[first : first + block], value * total))
            values = jnp.concatenate(values, axis=0)
            large = values.astype(jnp.bfloat16)
            small = (values - large.astype(jnp.float32)).astype(jnp.bfloat16)
            values = jnp.dot(
                interleave[...], large, preferred_element_type=jnp.float32
            ) + jnp.dot(interleave[...], small, preferred_element_type=jnp.float32)
            out_ref[c, :, :, lanes] = values.reshape(block, times, 2 * LANES)


def on_device(
    devices,
    log_amplitude,
    phase,
    redundant_group_index,
    antenna_couples,
    tile_flag_mask,
    inverse,
    integration_kernel,
    channel_kernel,
):
    own, _, channels = log_amplitude.shape
    total = own * devices
    real_antennas = inverse.shape[1]
    antennas = round_up(real_antennas, LANES)
    sent_antennas = round_up(real_antennas, 16)
    times = integration_kernel.shape[0]
    block = tile_flag_mask.shape[0]
    reach = (channel_kernel.shape[0] - 1) // 2
    tiles = channels // LANES
    parts = parts_of(channels, devices)
    gap = antennas - real_antennas
    wide_inverse = jnp.pad(inverse, ((0, 0), (0, gap), (0, gap)))
    lanes = sum(part.lanes for part in parts)
    extra = digit_rows(own, lanes)
    shape = (devices, own + extra, lanes)
    blocks = 4
    packed = call(
        functools.partial(pack_kernel, parts),
        jax.ShapeDtypeStruct(shape, jnp.bfloat16),
        60,
        (0, 8 * own * channels),
        in_specs=[
            pl.BlockSpec(memory_space=pltpu.VMEM),
            pl.BlockSpec(memory_space=pltpu.VMEM),
            pl.BlockSpec(memory_space=pl.ANY),
            pl.BlockSpec(memory_space=pl.ANY),
        ],
        out_specs=pl.BlockSpec(memory_space=pl.ANY),
        scratch_shapes=[pltpu.VMEM(shape, jnp.bfloat16)]
        + [pltpu.VMEM((own, channels), jnp.bfloat16)] * 2
        + [pltpu.SemaphoreType.DMA((2, blocks)), pltpu.SemaphoreType.DMA((blocks + 1,))],
        name="pack",
    )(
        redundant_group_index.reshape(1, own),
        jnp.transpose(antenna_couples),
        log_amplitude.reshape(own, channels),
        phase.reshape(own, channels),
    )
    terms = lax.all_to_all(packed, "bl", split_axis=0, concat_axis=0, tiled=True)

    large = total // 2048
    wide = sum(use.stop - use.start for use in lanes_of(parts, 0))
    gain, sent, indices = call(
        functools.partial(solve_kernel, parts, own),
        [
            jax.ShapeDtypeStruct((antennas, lanes), jnp.float32),
            jax.ShapeDtypeStruct((1, sent_antennas, lanes), jnp.bfloat16),
            jax.ShapeDtypeStruct((devices, 8, own), jnp.float32),
        ],
        min(56, 20 * large),
        (8 * total * (GROUP_ROWS + antennas) * lanes, 8 * total * lanes),
        scratch_shapes=[
            pltpu.VMEM((2, GROUP_ROWS + antennas, wide), jnp.float32),
            pltpu.VMEM((2, antennas, GROUP_ROWS), jnp.float32),
        ],
        name="solve",
    )(terms, wide_inverse)

    held, held_apart = sent, [0]
    hop = devices // 2
    while hop > 4:
        held = jnp.concatenate([held, pass_on(held, devices, hop)], axis=0)
        held_apart = held_apart + [distance ^ hop for distance in held_apart]
        hop //= 2
    far, near, side = [pass_on(held, devices, hop) for hop in (4, 2, 1)]
    gathered = [held, far, near, side]
    gathered += [pass_on(far, devices, hop) for hop in (1, 2, 3)] + [pass_on(near, devices, 1)]
    apart = [[distance ^ more for distance in held_apart] for more in (0, 4, 2, 1, 5, 6, 7, 3)]

    calibrated = call(
        functools.partial(calibrate_kernel, parts, own),
        jax.ShapeDtypeStruct((total, lanes), jnp.bfloat16),
        16,
        (16 * total * antennas * lanes, 8 * total * lanes),
        grid=(devices // 2,),
        in_specs=[
            pl.BlockSpec((2, own + extra, lanes), lambda i: (i, 0, 0)),
            pl.BlockSpec((2, 8, own), lambda i: (i, 0, 0)),
            pl.BlockSpec((antennas, lanes), lambda i: (0, 0)),
        ],
        out_specs=pl.BlockSpec((2 * own, lanes), lambda i: (i, 0)),
        scratch_shapes=[pltpu.VMEM((2, 3, antennas, wide), jnp.bfloat16)],
        name="calibrate",
    )(terms, indices, gain)
    spread = lax.all_to_all(
        after(calibrated, far, near), ("bl", "ta"), split_axis=0, concat_axis=0, tiled=True
    ).reshape(devices, times, block, lanes)

    filled, mark = call(
        functools.partial(fill_kernel, parts, times, reach),
        (
            jax.ShapeDtypeStruct((2, block, times, channels), jnp.float32),
            jax.ShapeDtypeStruct((8, LANES), jnp.float32),
        ),
        32,
        (32 * reach * block * times * channels * LANES, 16 * block * times * channels),
        grid=(tiles // 2,),
        in_specs=[
            pl.BlockSpec((block, tiles), lambda i: (0, 0)),
            pl.BlockSpec(memory_space=pltpu.SMEM),
            pl.BlockSpec(channel_kernel.shape, lambda i: (0, 0, 0)),
            pl.BlockSpec(spread.shape, lambda i: (0, 0, 0, 0)),
        ],
        out_specs=(
            pl.BlockSpec((2, block, times, 2 * LANES), lambda i: (0, 0, 0, i)),
            pl.BlockSpec((8, LANES), lambda i: (0, 0)),
        ),
        scratch_shapes=[
            pltpu.VMEM(((2 * times + 1) * block, (tiles + 2 * reach) * LANES), jnp.bfloat16),
            pltpu.VMEM(((2 * reach + 2) * LANES, 2 * LANES), jnp.bfloat16),
            pltpu.VMEM((times * block, times * block), jnp.bfloat16),
        ],
        name="fill",
    )(tile_flag_mask, integration_kernel, channel_kernel, spread)

    gains = call(
        functools.partial(spread_kernel, parts, real_antennas, tiles, apart),
        jax.ShapeDtypeStruct((2 * real_antennas * tiles, LANES), jnp.float32),
        32,
        (0, 12 * real_antennas * channels),
        grid=(2,),
        in_specs=[pl.BlockSpec(memory_space=pltpu.SMEM)]
        + [pl.BlockSpec(values.shape, lambda i: (0, 0, 0)) for values in gathered]
        + [pl.BlockSpec(memory_space=pl.ANY)],
        out_specs=pl.BlockSpec((real_antennas * tiles, LANES), lambda i: (i, 0)),
        scratch_shapes=[pltpu.VMEM((devices, sent_antennas, lanes), jnp.bfloat16)],
        name="gains",
    )(lax.axis_index("bl").astype(jnp.int32).reshape(1), *gathered, mark)

    return gains.reshape(2, real_antennas, 1, channels), filled


def solution(mesh):
    in_specs = (
        P("bl", "ta", None),
        P("bl", "ta", None),
        P("bl"),
        P("bl", None),
        P(("bl", "ta"), None),
        P(),
        P(),
        P(),
    )
    out_specs = (P(None, None, "ta", None), P(None, ("bl", "ta"), None, None))
    return jax.shard_map(
        functools.partial(on_device, mesh.shape["bl"]),
        mesh=mesh,
        in_specs=in_specs,
        out_specs=out_specs,
        check_vma=False,
    )
```

```python
import functools

import jax
import jax.numpy as jnp
from jax import lax
from jax.experimental import pallas as pl
from jax.experimental.pallas import tpu as pltpu
from jax.sharding import PartitionSpec as P

NGRP = 224
GROUP_ROWS = 256
LANES = 128
HIGHEST = lax.Precision.HIGHEST


def round_up(value, unit):
    return -(-value // unit) * unit


class Part:
    def __init__(self, first, half, at):
        self.first = first
        self.half = half
        self.at = at
        self.lanes = 2 * half


def parts_of(channels, devices):
    width = channels // devices
    whole = width // LANES * LANES
    parts = []
    if whole:
        parts.append(Part(0, whole, 0))
    if width - whole:
        parts.append(Part(devices * whole, width - whole, 2 * whole))
    return parts


def tile_pieces(parts, tile, which):
    at = tile * LANES
    index = max(k for k, part in enumerate(parts) if part.first <= at)
    part = parts[index]
    at -= part.first
    end = at + LANES
    pieces = []
    while at < end:
        device, inside = divmod(at, part.half)
        width = min(part.half - inside, end - at)
        pieces.append((index, device, which * part.half + inside, width))
        at += width
    return pieces


def lanes_of(parts, which):
    slices = []
    for part in parts:
        if part.half % LANES == 0:
            slices.append(slice(part.at + which * part.half, part.at + (which + 1) * part.half))
        else:
            slices.append(slice(part.at, part.at + part.lanes))
    return slices


def join(pieces):
    return pieces[0] if len(pieces) == 1 else jnp.concatenate(pieces, axis=-1)


def call(body, out_shape, vmem, work, **kwargs):
    flops, moved = work
    return pl.pallas_call(
        body,
        out_shape=out_shape,
        cost_estimate=pl.CostEstimate(flops=flops, bytes_accessed=moved, transcendentals=0),
        compiler_params=pltpu.CompilerParams(vmem_limit_bytes=vmem * 1024 * 1024),
        **kwargs,
    )


def digit_groups(own, lanes):
    return [(at, min(lanes, own - at)) for at in range(0, own, lanes)]


def digit_rows(own, lanes):
    return round_up(6 * len(digit_groups(own, lanes)), 16)


def pack_kernel(parts, group_ref, couple_ref, amp_hbm, phase_hbm, out_hbm, *refs):
    out, amp, phase, in_sems, out_sems = refs
    own = amp.shape[0]
    devices, _, lanes = out.shape
    blocks = in_sems.shape[1]
    rows = own // blocks
    copies = []
    for k in range(blocks):
        at = pl.ds(k * rows, rows)
        pair = [
            pltpu.make_async_copy(
                source.at[at], target.at[at], in_sems.at[which, k]
            )
            for which, (source, target) in enumerate(((amp_hbm, amp), (phase_hbm, phase)))
        ]
        for copy in pair:
            copy.start()
        copies.append(pair)
    sent = []
    numbers = [group_ref[...], couple_ref[0:1, :], couple_ref[1:2, :]]
    digits = []
    for number in numbers:
        wide = number.astype(jnp.float32)
        high = jnp.floor(wide * (1.0 / LANES))
        digits += [high, wide - high * LANES]
    lines = []
    for first, width in digit_groups(own, lanes):
        for digit in digits:
            line = digit[:, first : first + width]
            if width < lanes:
                line = jnp.concatenate(
                    [line, jnp.zeros((1, lanes - width), line.dtype)], axis=1
                )
            lines.append(line)
    extra = digit_rows(own, lanes)
    lines.append(jnp.zeros((extra - len(lines), lanes), jnp.float32))
    lines = jnp.concatenate(lines, axis=0).astype(jnp.bfloat16)
    for device in range(devices):
        out[device, own:, :] = lines
    block = pl.ds(own, extra)
    copy = pltpu.make_async_copy(out.at[:, block], out_hbm.at[:, block], out_sems.at[blocks])
    copy.start()
    sent.append(copy)
    for k in range(blocks):
        for copy in copies[k]:
            copy.wait()
        at = slice(k * rows, (k + 1) * rows)
        for part in parts:
            half = part.half
            for device in range(devices):
                first = part.first + device * half
                for which, ref in enumerate((amp, phase)):
                    lane = part.at + which * half
                    out[device, at, lane : lane + half] = ref[at, first : first + half]
        block = pl.ds(k * rows, rows)
        copy = pltpu.make_async_copy(out.at[:, block], out_hbm.at[:, block], out_sems.at[k])
        copy.start()
        sent.append(copy)
    for copy in sent:
        copy.wait()


def hot_rows(labels, number):
    rows = lax.broadcasted_iota(jnp.int32, (labels, number.shape[1]), 0).astype(jnp.float32)
    return (rows == number).astype(jnp.float32)


def solve_kernel(parts, own, x_ref, inverse_ref, gain_ref, sent_ref, index_ref, sums, link):
    devices, _, lanes = x_ref.shape
    antennas = gain_ref.shape[0]
    sums[...] = jnp.zeros_like(sums)
    link[...] = jnp.zeros_like(link)

    def gather(device, carry):
        digits = x_ref[device, own:, :].astype(jnp.float32)
        numbers = []
        for k in range(3):
            pieces = []
            for piece, (_, width) in enumerate(digit_groups(own, lanes)):
                at = 6 * piece + 2 * k
                pieces.append(
                    digits[at : at + 1, :width] * LANES + digits[at + 1 : at + 2, :width]
                )
            numbers.append(join(pieces))
        index_ref[device] = jnp.concatenate(numbers + [jnp.zeros((5, own), jnp.float32)], axis=0)
        group_hot = hot_rows(GROUP_ROWS, numbers[0]).astype(jnp.bfloat16)
        first, second = [hot_rows(antennas, number) for number in numbers[1:]]
        for s, couple in enumerate((first + second, first - second)):
            hot = jnp.concatenate([group_hot, couple.astype(jnp.bfloat16)], axis=0)
            values = join([x_ref[device, 0:own, use] for use in lanes_of(parts, s)])
            sums[s] += jnp.dot(hot, values, preferred_element_type=jnp.float32)
            link[s] += lax.dot_general(
                hot[GROUP_ROWS:],
                group_hot,
                (((1,), (1,)), ((), ())),
                preferred_element_type=jnp.float32,
            )
        return carry

    lax.fori_loop(0, devices, gather, 0, unroll=4)
    counts = 0.5 * jnp.sum(link[0], axis=0, keepdims=True)
    share = 1.0 / jnp.maximum(counts, 1.0)
    for s in range(2):
        rhs = sums[s, GROUP_ROWS:, :] - jnp.dot(
            link[s] * share,
            sums[s, :GROUP_ROWS, :],
            precision=HIGHEST,
            preferred_element_type=jnp.float32,
        )
        gain = jnp.dot(
            inverse_ref[s], rhs, precision=HIGHEST, preferred_element_type=jnp.float32
        )
        at = 0
        for part, use in zip(parts, lanes_of(parts, s)):
            width = use.stop - use.start
            values = gain[:, at : at + width]
            if s and width == part.lanes:
                low = lax.broadcasted_iota(jnp.int32, values.shape, 1) < part.half
                values = jnp.where(low, gain_ref[:, use], values)
            gain_ref[:, use] = values
            at += width
    sent_ref[0] = gain_ref[: sent_ref.shape[1], :].astype(jnp.bfloat16)


def reduced(angle):
    turns = jnp.floor(angle * 0.6366197723675814 + 0.5)
    left = angle - turns * 1.5703125
    left = left - turns * 4.83751296997070312e-4
    left = left - turns * 7.54978995489188216e-8
    square = left * left
    sine = ((-1.9515295891e-4 * square + 8.3321608736e-3) * square - 1.6666654611e-1) * square
    sine = sine * left + left
    cosine = (2.443315711809948e-5 * square - 1.388731625493765e-3) * square
    cosine = (cosine + 4.166664568298827e-2) * square * square - 0.5 * square + 1.0
    return turns.astype(jnp.int32), sine, cosine


def quarter(turns, sine, cosine):
    value = jnp.where((turns & 1) == 1, cosine, sine)
    return jnp.where((turns & 2) == 2, -value, value)


def swap(values, half):
    if 2 * half == LANES:
        return pltpu.roll(values, half, 1)
    return jnp.concatenate([values[:, half:], values[:, :half]], axis=1)


def calibrate_kernel(parts, own, x_ref, index_ref, gain_ref, out_ref, split):
    antennas = gain_ref.shape[0]

    @pl.when(pl.program_id(0) == 0)
    def _():
        for s in range(2):
            left = join([gain_ref[:, use] for use in lanes_of(parts, s)])
            for k in range(3):
                part = left.astype(jnp.bfloat16)
                split[s, k] = part
                left = left - part.astype(jnp.float32)

    labels = lax.broadcasted_iota(jnp.int32, (own, antennas), 1).astype(jnp.float32)
    for device in range(x_ref.shape[0]):
        columns = jnp.transpose(index_ref[device])
        first, second = [
            (labels == columns[:, k : k + 1]).astype(jnp.float32) for k in (1, 2)
        ]
        moves = []
        for s, couple in enumerate((first + second, first - second)):
            hot = couple.astype(jnp.bfloat16)
            move = jnp.dot(hot, split[s, 0], preferred_element_type=jnp.float32)
            for k in range(1, 3):
                move = move + jnp.dot(hot, split[s, k], preferred_element_type=jnp.float32)
            moves.append(move)
        rows = slice(device * own, (device + 1) * own)
        at = 0
        for part in parts:
            half, lanes = part.half, part.lanes
            first_lanes = slice(part.at, part.at + half)
            second_lanes = slice(part.at + half, part.at + lanes)
            if half % LANES == 0:
                here = slice(at, at + half)
                left = x_ref[device, 0:own, first_lanes].astype(jnp.float32) - moves[0][:, here]
                magnitude = jnp.exp(left)
                left = x_ref[device, 0:own, second_lanes].astype(jnp.float32) - moves[1][:, here]
                turns, sine, cosine = reduced(left)
                real = magnitude * quarter(turns + 1, sine, cosine)
                imaginary = magnitude * quarter(turns, sine, cosine)
                out_ref[rows, first_lanes] = real.astype(jnp.bfloat16)
                out_ref[rows, second_lanes] = imaginary.astype(jnp.bfloat16)
                at += half
            else:
                here = slice(at, at + lanes)
                both = slice(part.at, part.at + lanes)
                left = x_ref[device, 0:own, both].astype(jnp.float32)
                lower = lax.broadcasted_iota(jnp.int32, left.shape, 1) < half
                left = left - jnp.where(lower, moves[0][:, here], moves[1][:, here])
                turned = swap(left, half)
                magnitude = jnp.exp(jnp.where(lower, left, turned))
                turns, sine, cosine = reduced(jnp.where(lower, turned, left))
                turns = jnp.where(lower, turns + 1, turns)
                value = magnitude * quarter(turns, sine, cosine)
                out_ref[rows, both] = value.astype(jnp.bfloat16)
                at += lanes


def nothing(*refs):
    pass


def after(values, *others):
    return call(
        nothing,
        jax.ShapeDtypeStruct(values.shape, values.dtype),
        4,
        (0, 8 * values.size),
        in_specs=[pl.BlockSpec(memory_space=pl.ANY)] * (1 + len(others)),
        out_specs=pl.BlockSpec(memory_space=pl.ANY),
        input_output_aliases={0: 0},
        name="after",
    )(values, *others)


def pass_on(held, devices, reach):
    return lax.ppermute(held, "bl", [(i, i ^ reach) for i in range(devices)])


def spread_kernel(parts, antennas, tiles, apart, me_ref, *refs):
    gain_refs, (out_ref, chunks) = refs[: len(apart)], refs[-2:]
    which = pl.program_id(0)

    @pl.when(which == 0)
    def _():
        for gain_ref, distances in zip(gain_refs, apart):
            for entry, distance in enumerate(distances):
                chunks[me_ref[0] ^ distance] = gain_ref[entry]

    for s in range(2):

        @pl.when(which == s)
        def _():
            for tile in range(tiles):
                pieces = []
                for part, device, lane, width in tile_pieces(parts, tile, s):
                    lane += parts[part].at
                    pieces.append(chunks[device, :, lane : lane + width].astype(jnp.float32))
                out_ref[pl.ds(tile, antennas, tiles), :] = join(pieces)[:antennas]


def fill_kernel(parts, times, reach, mask_ref, times_ref, kernel_ref, *refs):
    cal_ref, (out_ref, mark_ref, rows, band, interleave) = refs[0], refs[1:]
    step = pl.program_id(0)
    block, tiles = mask_ref.shape
    count = 2 * times * block
    span = (2 * reach + 2) * LANES

    @pl.when(step == 0)
    def _():
        mark_ref[...] = jnp.zeros_like(mark_ref)
        keep = (1 - mask_ref[...]).astype(jnp.float32)
        edge = reach * LANES
        inner = (reach + tiles) * LANES
        rows[:, :edge] = jnp.zeros((rows.shape[0], edge), rows.dtype)
        rows[:, inner:] = jnp.zeros((rows.shape[0], rows.shape[1] - inner), rows.dtype)
        for tile in range(tiles):
            lanes = slice((reach + tile) * LANES, (reach + tile + 1) * LANES)
            weight = jnp.broadcast_to(keep[:, tile : tile + 1], (block, LANES))
            weight = weight.astype(rows.dtype)
            rows[count:, lanes] = weight
            for c in range(2):
                for t in range(times):
                    values = join(
                        [
                            cal_ref[device, t, :, parts[part].at + lane : parts[part].at + lane + width]
                            for part, device, lane, width in tile_pieces(parts, tile, c)
                        ]
                    )
                    at = (c * times + t) * block
                    rows[at : at + block, lanes] = values * weight
        order = times * block
        place = lax.broadcasted_iota(jnp.int32, (order, order), 0)
        origin = lax.broadcasted_iota(jnp.int32, (order, order), 1)
        moved = (place % times) * block + place // times == origin
        interleave[...] = moved.astype(jnp.float32).astype(jnp.bfloat16)
        band[...] = jnp.zeros(band.shape, band.dtype)
        for offset in range(2 * reach + 1):
            turned = jnp.transpose(kernel_ref[offset].astype(jnp.float32)).astype(band.dtype)
            for target in range(2):
                first = (offset + target) * LANES
                band[first : first + LANES, target * LANES : (target + 1) * LANES] = turned

    mixes = []
    for t in range(times):
        scale = times_ref[t, 0]
        for u in range(1, times):
            scale = scale + times_ref[t, u]
        share = 1.0 / scale
        mixes.append([times_ref[t, u] * share for u in range(times)])
    width = out_ref.shape[3]
    for pair in range(width // (2 * LANES)):
        lanes = slice(pair * 2 * LANES, (pair + 1) * 2 * LANES)
        at = pl.multiple_of(step * width + pair * 2 * LANES, 2 * LANES)
        mixed = jnp.dot(
            rows[:, pl.ds(at, span)], band[...], preferred_element_type=jnp.float32
        )
        total = 1.0 / mixed[count:]
        kept = rows[:, pl.ds(pl.multiple_of(at + reach * LANES, LANES), 2 * LANES)]
        kept = kept.astype(jnp.float32)
        keep = kept[count:] > 0.5
        for c in range(2):
            values = []
            for t in range(times):
                value = None
                for u in range(times):
                    first = (c * times + u) * block
                    part = mixes[t][u] * mixed[first : first + block]
                    value = part if value is None else value + part
                first = (c * times + t) * block
                values.append(jnp.where(keep, kept[first : first + block], value * total))
            values = jnp.concatenate(values, axis=0)
            large = values.astype(jnp.bfloat16)
            small = (values - large.astype(jnp.float32)).astype(jnp.bfloat16)
            values = jnp.dot(
                interleave[...], large, preferred_element_type=jnp.float32
            ) + jnp.dot(interleave[...], small, preferred_element_type=jnp.float32)
            out_ref[c, :, :, lanes] = values.reshape(block, times, 2 * LANES)


def on_device(
    devices,
    log_amplitude,
    phase,
    redundant_group_index,
    antenna_couples,
    tile_flag_mask,
    inverse,
    integration_kernel,
    channel_kernel,
):
    own, _, channels = log_amplitude.shape
    total = own * devices
    real_antennas = inverse.shape[1]
    antennas = round_up(real_antennas, LANES)
    sent_antennas = round_up(real_antennas, 16)
    times = integration_kernel.shape[0]
    block = tile_flag_mask.shape[0]
    reach = (channel_kernel.shape[0] - 1) // 2
    tiles = channels // LANES
    parts = parts_of(channels, devices)
    gap = antennas - real_antennas
    wide_inverse = jnp.pad(inverse, ((0, 0), (0, gap), (0, gap)))
    lanes = sum(part.lanes for part in parts)
    extra = digit_rows(own, lanes)
    shape = (devices, own + extra, lanes)
    blocks = 4
    packed = call(
        functools.partial(pack_kernel, parts),
        jax.ShapeDtypeStruct(shape, jnp.bfloat16),
        60,
        (0, 8 * own * channels),
        in_specs=[
            pl.BlockSpec(memory_space=pltpu.VMEM),
            pl.BlockSpec(memory_space=pltpu.VMEM),
            pl.BlockSpec(memory_space=pl.ANY),
            pl.BlockSpec(memory_space=pl.ANY),
        ],
        out_specs=pl.BlockSpec(memory_space=pl.ANY),
        scratch_shapes=[pltpu.VMEM(shape, jnp.bfloat16)]
        + [pltpu.VMEM((own, channels), jnp.bfloat16)] * 2
        + [pltpu.SemaphoreType.DMA((2, blocks)), pltpu.SemaphoreType.DMA((blocks + 1,))],
        name="pack",
    )(
        redundant_group_index.reshape(1, own),
        jnp.transpose(antenna_couples),
        log_amplitude.reshape(own, channels),
        phase.reshape(own, channels),
    )
    terms = lax.all_to_all(packed, "bl", split_axis=0, concat_axis=0, tiled=True)

    large = total // 2048
    wide = sum(use.stop - use.start for use in lanes_of(parts, 0))
    gain, sent, indices = call(
        functools.partial(solve_kernel, parts, own),
        [
            jax.ShapeDtypeStruct((antennas, lanes), jnp.float32),
            jax.ShapeDtypeStruct((1, sent_antennas, lanes), jnp.bfloat16),
            jax.ShapeDtypeStruct((devices, 8, own), jnp.float32),
        ],
        min(56, 20 * large),
        (8 * total * (GROUP_ROWS + antennas) * lanes, 8 * total * lanes),
        scratch_shapes=[
            pltpu.VMEM((2, GROUP_ROWS + antennas, wide), jnp.float32),
            pltpu.VMEM((2, antennas, GROUP_ROWS), jnp.float32),
        ],
        name="solve",
    )(terms, wide_inverse)

    held, held_apart = sent, [0]
    hop = devices // 2
    while hop > 4:
        held = jnp.concatenate([held, pass_on(held, devices, hop)], axis=0)
        held_apart = held_apart + [distance ^ hop for distance in held_apart]
        hop //= 2
    far, near, side = [pass_on(held, devices, hop) for hop in (4, 2, 1)]
    gathered = [held, far, near, side]
    gathered += [pass_on(far, devices, hop) for hop in (1, 2, 3)] + [pass_on(near, devices, 1)]
    apart = [[distance ^ more for distance in held_apart] for more in (0, 4, 2, 1, 5, 6, 7, 3)]

    calibrated = call(
        functools.partial(calibrate_kernel, parts, own),
        jax.ShapeDtypeStruct((total, lanes), jnp.bfloat16),
        16,
        (16 * total * antennas * lanes, 8 * total * lanes),
        grid=(devices // 2,),
        in_specs=[
            pl.BlockSpec((2, own + extra, lanes), lambda i: (i, 0, 0)),
            pl.BlockSpec((2, 8, own), lambda i: (i, 0, 0)),
            pl.BlockSpec((antennas, lanes), lambda i: (0, 0)),
        ],
        out_specs=pl.BlockSpec((2 * own, lanes), lambda i: (i, 0)),
        scratch_shapes=[pltpu.VMEM((2, 3, antennas, wide), jnp.bfloat16)],
        name="calibrate",
    )(terms, indices, gain)
    spread = lax.all_to_all(
        after(calibrated, far), ("bl", "ta"), split_axis=0, concat_axis=0, tiled=True
    ).reshape(devices, times, block, lanes)

    filled, mark = call(
        functools.partial(fill_kernel, parts, times, reach),
        (
            jax.ShapeDtypeStruct((2, block, times, channels), jnp.float32),
            jax.ShapeDtypeStruct((8, LANES), jnp.float32),
        ),
        32,
        (32 * reach * block * times * channels * LANES, 16 * block * times * channels),
        grid=(tiles // 2,),
        in_specs=[
            pl.BlockSpec((block, tiles), lambda i: (0, 0)),
            pl.BlockSpec(memory_space=pltpu.SMEM),
            pl.BlockSpec(channel_kernel.shape, lambda i: (0, 0, 0)),
            pl.BlockSpec(spread.shape, lambda i: (0, 0, 0, 0)),
        ],
        out_specs=(
            pl.BlockSpec((2, block, times, 2 * LANES), lambda i: (0, 0, 0, i)),
            pl.BlockSpec((8, LANES), lambda i: (0, 0)),
        ),
        scratch_shapes=[
            pltpu.VMEM(((2 * times + 1) * block, (tiles + 2 * reach) * LANES), jnp.bfloat16),
            pltpu.VMEM(((2 * reach + 2) * LANES, 2 * LANES), jnp.bfloat16),
            pltpu.VMEM((times * block, times * block), jnp.bfloat16),
        ],
        name="fill",
    )(tile_flag_mask, integration_kernel, channel_kernel, spread)

    gains = call(
        functools.partial(spread_kernel, parts, real_antennas, tiles, apart),
        jax.ShapeDtypeStruct((2 * real_antennas * tiles, LANES), jnp.float32),
        32,
        (0, 12 * real_antennas * channels),
        grid=(2,),
        in_specs=[pl.BlockSpec(memory_space=pltpu.SMEM)]
        + [pl.BlockSpec(values.shape, lambda i: (0, 0, 0)) for values in gathered]
        + [pl.BlockSpec(memory_space=pl.ANY)],
        out_specs=pl.BlockSpec((real_antennas * tiles, LANES), lambda i: (i, 0)),
        scratch_shapes=[pltpu.VMEM((devices, sent_antennas, lanes), jnp.bfloat16)],
        name="gains",
    )(lax.axis_index("bl").astype(jnp.int32).reshape(1), *gathered, mark)

    return gains.reshape(2, real_antennas, 1, channels), filled


def solution(mesh):
    in_specs = (
        P("bl", "ta", None),
        P("bl", "ta", None),
        P("bl"),
        P("bl", None),
        P(("bl", "ta"), None),
        P(),
        P(),
        P(),
    )
    out_specs = (P(None, None, "ta", None), P(None, ("bl", "ta"), None, None))
    return jax.shard_map(
        functools.partial(on_device, mesh.shape["bl"]),
        mesh=mesh,
        in_specs=in_specs,
        out_specs=out_specs,
        check_vma=False,
    )
```
